32 devices in a mesh: seq: 8 (over z, x), head: 4 (over y, core).
Axes of the slice: x: 2, y: 2, z: 4, core: 2. Of those that a mesh axis runs over, the one named last changes fastest.
Arguments:
- hidden: bfloat16 [2048, 2560], P(('seq', 'head')), may hold values from -6 to 6
- w_values: bfloat16 [2560, 2560], P('seq', 'head'), may hold values from -0.125 to 0.125
- w_gates: bfloat16 [2560, 2560], P('seq', 'head'), may hold values from -0.125 to 0.125
- w_steps: bfloat16 [2560, 40], P('seq', 'head'), may hold values from -0.0625 to 0.0625
- w_states: bfloat16 [2560, 256], P('seq'), may hold values from -0.125 to 0.125
- conv_weight: float32 [4, 2816], replicated, may hold values from -3 to 3
- conv_bias: float32 [2816], replicated, may hold values from -3 to 3
- step_bias: float32 [40], P('head'), may hold values from -1 to 0.5
- decay_rate: float32 [40], P('head'), may hold values from 0 to 1, as said below
- skip_gain: float32 [40], P('head'), may hold values from 1 to 8
- norm_gain: float32 [2560], replicated, may hold values from 0.5 to 1.5
- lengths: int32 [4], replicated, may hold values from 256 to 768, as said below
Outputs:
- gated_out: bfloat16 [2048, 2560], P(('seq', 'head'))
- final_states: float32 [8, 40, 64, 128], P('seq', 'head')
The draws below stay inside these ranges and needn't reach their ends.
Inputs may be any that keep to these rules, and one draw needn't show every extreme that they name: Prompts are packed in order, each holding 256 to 768 tokens; the lengths sum to 2048. `decay_rate`: positive rates.
All inputs are finite; a program needn't handle non-finite values.
Results may differ from the reference program's by a relative error of at most 0.01.
Values may be sent and summed in bfloat16 or wider, within the bound.
A program may use at most 128 MiB of HBM per device.

```python
import math
import jax
import jax.numpy as jnp
from jax import lax

D = 2560
HEADS = 40
HEAD_DIM = 64
STATE = 128
CONV = 4
STRETCH = 256
TOK_DEV = 256
INNER = 2560
CONV_CH = 2816
TOKENS = 2048
BLOCKS = 8
PROMPTS = 4


def draw_lengths(key, part):
    order_key = jax.random.fold_in(key, 11)
    offset_key = jax.random.fold_in(key, 12)
    cycle_order = jax.random.permutation(order_key, PROMPTS)
    offsets = jax.random.randint(offset_key, (PROMPTS,), 0, TOK_DEV + 1)
    cycle_slots = jnp.arange(PROMPTS, dtype=jnp.int32)
    offsets = jnp.where(cycle_slots == 0, TOK_DEV, offsets)
    offsets = jnp.where(cycle_slots == 1, 0, offsets)
    offsets = jnp.where(cycle_slots == 2, TOK_DEV, offsets)
    along_cycle = 2 * TOK_DEV + offsets - jnp.roll(offsets, -1)
    placing = jnp.argsort(cycle_order, stable=True)
    return along_cycle[placing].astype(jnp.int32)


def draw_decay_rate(key, part):
    pick_key = jax.random.fold_in(key, 21)
    slow_key = jax.random.fold_in(key, 22)
    fast_key = jax.random.fold_in(key, 23)
    chooser = jax.random.uniform(pick_key, (HEADS,), jnp.float32)
    fast_share = 0.5
    slow_rate = jnp.exp(jax.random.uniform(slow_key, (HEADS,), jnp.float32, math.log(0.1), math.log(0.8))) / (3.0 * TOK_DEV)
    fast_rate = jnp.exp(jax.random.uniform(fast_key, (HEADS,), jnp.float32, math.log(0.04), math.log(0.12)))
    return jnp.where(chooser < fast_share, fast_rate, slow_rate).astype(jnp.float32)


def block_scale(rng, shape, split, low, largest):
    gain = 1.0
    for dim, parts in split:
        heights = jax.random.uniform(jax.random.fold_in(jax.random.fold_in(rng, 6), dim), (parts,), jnp.float32, low / len(split), largest / len(split))
        gain = gain * jnp.repeat(jnp.exp(heights), shape[dim] // parts).reshape((-1,) + (1,) * (len(shape) - 1 - dim))
    return gain


def centred(own_key, extent, width, most, split=(), kind=jnp.bfloat16):
    entries = jax.random.normal(own_key, extent, jnp.float32) * width
    if len(split) > 0:
        entries = block_scale(own_key, extent, split, -0.22, 0.18) * entries
    return jnp.clip(entries, min=-most, max=most).astype(kind)


def setup_inputs(seed: int = 0) -> dict:
    key_of = jax.random.split(jax.random.key(seed), 13)
    hidden = centred(key_of[0], (TOKENS, D), 1.0, 6.0, ((0, 32),))
    w_values = centred(key_of[1], (D, INNER), D ** -0.5, 0.125, ((0, 8), (1, 4)))
    w_gates = centred(key_of[2], (D, INNER), D ** -0.5, 0.125, ((0, 8), (1, 4)))
    w_steps = centred(key_of[3], (D, HEADS), (4 * D) ** -0.5, 0.0625, ((0, 8), (1, 4)))
    w_states = centred(key_of[4], (D, 2 * STATE), D ** -0.5, 0.125, ((0, 8),))
    conv_weight = centred(key_of[5], (CONV, CONV_CH), CONV ** -0.5, 3.0, (), jnp.float32)
    conv_bias = centred(key_of[6], (CONV_CH,), 0.5, 3.0, (), jnp.float32)
    step_bias = jnp.clip(-1.0 + 1.5 * jax.random.uniform(key_of[7], (HEADS,), jnp.float32) ** block_scale(key_of[7], (HEADS,), ((0, 4),), -0.2, 0.2), -1.0, 0.5)
    decay_rate = draw_decay_rate(jax.random.fold_in(key_of[12], 71), 0)
    skip_gain = jnp.clip(1.0 + 7.0 * jax.random.uniform(key_of[9], (HEADS,), jnp.float32) ** block_scale(key_of[9], (HEADS,), ((0, 4),), -0.2, 0.2), 1.0, 8.0)
    norm_gain = jnp.clip(1.0 + 0.1 * jax.random.normal(key_of[10], (INNER,), jnp.float32), 0.5, 1.5)
    lengths = draw_lengths(jax.random.fold_in(key_of[12], 71), 0)
    return {"hidden": hidden, "w_values": w_values, "w_gates": w_gates, "w_steps": w_steps, "w_states": w_states, "conv_weight": conv_weight, "conv_bias": conv_bias, "step_bias": step_bias, "decay_rate": decay_rate, "skip_gain": skip_gain, "norm_gain": norm_gain, "lengths": lengths}


epsilon = 1e-05
highest = lax.Precision.HIGHEST

def segments_at(positions, prompt_ends):
    counted = lax.optimization_barrier(jnp.sum((prompt_ends[None, :] <= positions[:, None]).astype(jnp.int32), axis=1)).astype(jnp.int32)
    return jnp.where(positions < 0, -1, counted).astype(jnp.int32)

def rounded(values):
    return lax.optimization_barrier(values.astype(jnp.bfloat16)).astype(jnp.float32)

def stretch_pass(skip_gain, running, pieces):
    values, write_state, read_state, step_sizes, decay_steps, stretch_ids, prior_id, ends_mask = pieces
    log_decay = -jnp.cumsum(decay_steps, axis=0)
    decay_heads = log_decay.T
    step_heads = step_sizes.T
    intersection = jnp.dot(read_state, write_state.T, preferred_element_type=jnp.float32)
    positions = jnp.arange(STRETCH, dtype=jnp.int32)
    causal = positions[:, None] >= positions[None, :]
    allowed = causal & (stretch_ids[:, None] == stretch_ids[None, :])
    spread = decay_heads[:, :, None] - decay_heads[:, None, :]
    weights = jnp.where(allowed[None], jnp.exp(jnp.minimum(spread, 0.0)), 0.0) * step_heads[:, None, :]
    scores = rounded(intersection[None] * weights)
    values_wide = values.astype(jnp.float32)
    within_stretch = jnp.einsum('hts,shp->thp', scores, values_wide, precision=highest)
    last_id = stretch_ids[-1]
    tail_coef = jnp.where((stretch_ids == last_id)[None, :], jnp.exp(jnp.minimum(decay_heads[:, -1:] - decay_heads, 0.0)), 0.0) * step_heads
    tail_rows = rounded(values_wide * tail_coef.T[:, :, None])
    write_wide = write_state.astype(jnp.float32)
    stretch_state = jnp.einsum('lhp,ln->hpn', tail_rows, write_wide, precision=highest)
    stretch_gate = jnp.exp(decay_heads[:, -1]) * (last_id == prior_id).astype(jnp.float32)
    carry_decay = jnp.exp(log_decay) * (stretch_ids == prior_id).astype(jnp.float32)[:, None]
    from_before = jnp.einsum('ln,hpn->lhp', read_state.astype(jnp.float32), rounded(running), precision=highest) * carry_decay[:, :, None]
    result = within_stretch + from_before + skip_gain[None, :, None] * values_wide
    ssm_rows = result.reshape(STRETCH, INNER).astype(jnp.bfloat16)
    end_weight = ends_mask.astype(jnp.float32)
    has_end = jnp.sum(end_weight)
    end_decay = lax.optimization_barrier(jnp.sum(decay_heads * end_weight[None, :], axis=1))
    end_id = jnp.sum(jnp.where(ends_mask, stretch_ids, 0)).astype(jnp.int32)
    keep_end = (stretch_ids == end_id) & (has_end > 0)
    end_coef = jnp.where(keep_end[None, :], jnp.exp(jnp.minimum(end_decay[:, None] - decay_heads, 0.0)), 0.0) * step_heads
    end_rows = rounded(values_wide * end_coef.T[:, :, None])
    end_state = jnp.einsum('lhp,ln->hpn', end_rows, write_wide, precision=highest)
    end_carry = jnp.exp(end_decay) * ((end_id == prior_id) & (has_end > 0)).astype(jnp.float32)
    end_state = end_state + end_carry[:, None, None] * running
    new_running = stretch_gate[:, None, None] * running + stretch_state
    return (new_running, (ssm_rows, end_state))

def partial_pass(skip_gain):

    def stepper(running, pieces):
        return stretch_pass(skip_gain, running, pieces)
    return stepper

def reference(hidden, w_values, w_gates, w_steps, w_states, conv_weight, conv_bias, step_bias, decay_rate, skip_gain, norm_gain, lengths):
    conv_input = jnp.dot(hidden, jnp.concatenate([w_values, w_states], axis=1), preferred_element_type=jnp.float32).astype(jnp.bfloat16)
    gate_input = jnp.dot(hidden, w_gates, preferred_element_type=jnp.float32).astype(jnp.bfloat16)
    step_input = jnp.dot(hidden, w_steps, preferred_element_type=jnp.float32)
    prompt_ends = jnp.cumsum(lengths).astype(jnp.int32)
    positions = jnp.arange(TOKENS, dtype=jnp.int32)
    segment_ids = segments_at(positions, prompt_ends)
    extended = jnp.concatenate([jnp.zeros((CONV - 1, CONV_CH), jnp.bfloat16), conv_input], axis=0)
    ext_ids = jnp.concatenate([jnp.full((CONV - 1,), -1, jnp.int32), segment_ids], axis=0)
    filtered = jnp.zeros((TOKENS, CONV_CH), jnp.float32) + conv_bias[None, :]
    for offset in range(CONV):
        matches = (ext_ids[offset:offset + TOKENS] == segment_ids).astype(jnp.float32)
        filtered = filtered + conv_weight[offset][None, :] * extended[offset:offset + TOKENS].astype(jnp.float32) * matches[:, None]
    conv_out = jax.nn.silu(filtered).astype(jnp.bfloat16)
    stretch_count = TOKENS // STRETCH
    values = conv_out[:, :INNER].reshape(stretch_count, STRETCH, HEADS, HEAD_DIM)
    write_state = conv_out[:, INNER:INNER + STATE].reshape(stretch_count, STRETCH, STATE)
    read_state = conv_out[:, INNER + STATE:].reshape(stretch_count, STRETCH, STATE)
    step_sizes = jax.nn.softplus(step_input + step_bias[None, :])
    decay_steps = step_sizes * decay_rate[None, :]
    before_ids = segments_at(positions - 1, prompt_ends)
    next_ids = segments_at(positions + 1, prompt_ends)
    ends_mask = segment_ids != next_ids
    pieces = (values, write_state, read_state, step_sizes.reshape(stretch_count, STRETCH, HEADS), decay_steps.reshape(stretch_count, STRETCH, HEADS), segment_ids.reshape(stretch_count, STRETCH), before_ids.reshape(stretch_count, STRETCH)[:, 0], ends_mask.reshape(stretch_count, STRETCH))
    start_state = jnp.zeros((HEADS, HEAD_DIM, STATE), jnp.float32)
    final_running, stacked = lax.scan(partial_pass(skip_gain), start_state, pieces)
    ssm_rows = stacked[0].reshape(TOKENS, INNER)
    final_states = lax.optimization_barrier(jnp.sum(stacked[1].reshape(BLOCKS, TOK_DEV // STRETCH, HEADS, HEAD_DIM, STATE), axis=1))
    gated = ssm_rows.astype(jnp.float32) * jax.nn.silu(gate_input.astype(jnp.float32))
    mean_square = lax.optimization_barrier(jnp.mean(gated * gated, axis=1))
    gated_out = (gated * lax.rsqrt(mean_square + epsilon)[:, None] * norm_gain[None, :]).astype(jnp.bfloat16)
    return (gated_out, final_states)
```

```python
import jax
import jax.numpy as jnp
from jax import lax
from jax.experimental import pallas as pl
from jax.experimental.pallas import tpu as pltpu
from jax.sharding import PartitionSpec as P

STRETCH = 256


epsilon = 1e-05


def from_behind(block, axis, distance):
    devices = range(lax.axis_size(axis))
    route = [(i - distance, i) for i in devices if i - distance in devices]
    return lax.ppermute(block, axis, route)


def prefix(value, axis, join, neutral):
    place = lax.axis_index(axis)
    gathered = jax.tree.map(
        lambda a, kind: lax.all_gather(a.astype(kind), axis), value, (jnp.bfloat16, jnp.bfloat16)
    )
    state = jax.tree.map(lambda a, e: jnp.zeros_like(a) + jnp.asarray(e, a.dtype), value, neutral)

    def one(turn, state):
        return join(
            state,
            jax.tree.map(
                lambda a, own: lax.dynamic_index_in_dim(a, turn, 0, False).astype(own.dtype),
                gathered,
                value,
            ),
        )

    return lax.fori_loop(0, place, one, state)


def segments_at(positions, prompt_ends):
    counted = jnp.sum((prompt_ends[None, :] <= positions[:, None]).astype(jnp.int32), axis=1)
    return jnp.where(positions < 0, -1, counted)


MESH = pl.DeviceIdType.MESH
BF16 = jnp.bfloat16
F32 = jnp.float32


def rdma(src, dst, send_sem, recv_sem, seq, head):
    return pltpu.make_async_remote_copy(
        src_ref=src,
        dst_ref=dst,
        send_sem=send_sem,
        recv_sem=recv_sem,
        device_id=(seq, head),
        device_id_type=MESH,
    )


def project_kernel(
    hidden_ref,
    values_ref,
    small_ref,
    gates_ref,
    pre_ref,
    states_ref,
    steps_ref,
    gate_ref,
    hid,
    wbuf,
    out_v,
    out_s,
    out_g,
    in_v,
    in_s,
    in_g,
    own,
    tile,
    tiles,
    local_sem,
    hid_send,
    hid_recv,
    w_send,
    w_recv,
    part_send,
    part_recv,
    tile_send,
    tile_recv,
):
    s = lax.axis_index("seq")
    h = lax.axis_index("head")
    z = lax.div(s, 2)
    x = lax.rem(s, 2)
    z_lo = lax.rem(z, 2)
    z_hi = lax.div(z, 2)
    beside = s + 1 - 2 * x
    partner = s + 2 - 4 * z_lo
    far = s + 4 - 8 * z_hi
    heads = [lax.rem(h + d, 4) for d in (1, 2, 3)]
    rows_w = values_ref.shape[0]
    rows_h = hidden_ref.shape[0]
    depth = 2 * rows_w
    width = values_ref.shape[1]
    narrow = small_ref.shape[1]

    barrier = pltpu.get_barrier_semaphore()
    for to in (beside, partner, far):
        pl.semaphore_signal(barrier, inc=1, device_id=(to, h), device_id_type=MESH)
    for to in heads:
        pl.semaphore_signal(barrier, inc=1, device_id=(s, to), device_id_type=MESH)

    my_rows = pl.ds(pl.multiple_of(x * rows_w, 64), rows_w)
    my_tokens = pl.ds(pl.multiple_of(h * rows_h, 64), rows_h)
    windows = (pl.ds(0, width), pl.ds(width, narrow), pl.ds(width + narrow, width))
    sources = (values_ref, small_ref, gates_ref)

    def columns(low, zh):
        return pl.ds(pl.multiple_of((low + 2 * zh) * depth, 128), depth)

    local = []
    for p in range(3):
        local.append(
            pltpu.make_async_copy(
                sources[p], wbuf.at[z_hi, my_rows, windows[p]], local_sem.at[p]
            )
        )
    for zh in range(2):
        local.append(
            pltpu.make_async_copy(
                hidden_ref.at[:, columns(z_lo, zh)],
                hid.at[0, zh, my_tokens],
                local_sem.at[3 + zh],
            )
        )
    for c in local:
        c.start()
    pl.semaphore_wait(barrier, 6)

    to_far = [
        rdma(sources[p], wbuf.at[z_hi, my_rows, windows[p]], w_send.at[0, p], w_recv.at[0, p], far, h)
        for p in range(3)
    ]
    to_beside = [
        rdma(sources[p], wbuf.at[z_hi, my_rows, windows[p]], w_send.at[1, p], w_recv.at[1, p], beside, h)
        for p in range(3)
    ]
    passed = [
        rdma(
            wbuf.at[1 - z_hi, my_rows, windows[p]],
            wbuf.at[1 - z_hi, my_rows, windows[p]],
            w_send.at[2, p],
            w_recv.at[2, p],
            beside,
            h,
        )
        for p in range(3)
    ]
    hid_over = [
        rdma(
            hidden_ref.at[:, columns(1 - z_lo, zh)],
            hid.at[1, zh, my_tokens],
            hid_send.at[0, zh],
            hid_recv.at[0, zh],
            partner,
            h,
        )
        for zh in range(2)
    ]
    hid_own = [
        rdma(
            hidden_ref.at[:, columns(z_lo, zh)],
            hid.at[0, zh, my_tokens],
            hid_send.at[1 + d, zh],
            hid_recv.at[1 + d, zh],
            s,
            heads[d],
        )
        for zh in range(2)
        for d in range(3)
    ]
    hid_pass = [
        rdma(
            hid.at[1, zh, my_tokens],
            hid.at[1, zh, my_tokens],
            hid_send.at[4 + d, zh],
            hid_recv.at[4 + d, zh],
            s,
            heads[d],
        )
        for zh in range(2)
        for d in range(3)
    ]
    for c in hid_over:
        c.start()
    for p in (0, 1):
        to_far[p].start()
    for p in (0, 1):
        to_beside[p].start()
    for c in hid_own:
        c.start()
    for zh in range(2):
        hid_over[zh].wait_recv()
        for d in range(3):
            hid_pass[3 * zh + d].start()
    for p in (0, 1):
        to_far[p].wait_recv()
        passed[p].start()
    to_far[2].start()
    to_beside[2].start()
    for c in local:
        c.wait()
    for c in hid_own:
        c.wait_recv()
    for c in hid_pass:
        c.wait_recv()
    for p in (0, 1):
        to_beside[p].wait_recv()
        passed[p].wait_recv()

    def product(which, window):
        return jnp.dot(
            hid[which, 0], wbuf[0, :, window], preferred_element_type=F32
        ) + jnp.dot(hid[which, 1], wbuf[1, :, window], preferred_element_type=F32)

    out_s[...] = product(1, windows[1])
    part_s = rdma(out_s, in_s, part_send.at[0], part_recv.at[0], partner, h)
    part_s.start()
    out_v[...] = product(1, windows[0]).astype(BF16)
    part_v = rdma(out_v, in_v, part_send.at[1], part_recv.at[1], partner, h)
    part_v.start()
    small = product(0, windows[1])
    part_s.wait_recv()
    small = small + in_s[...]
    steps_ref[...] = small
    tile[...] = small.astype(BF16)
    tiles_out = [
        rdma(tile, tiles.at[h], tile_send.at[d], tile_recv.at[d], s, heads[d]) for d in range(3)
    ]
    for c in tiles_out:
        c.start()
    tiles[h] = tile[...]
    own[...] = product(0, windows[0])
    part_v.wait_recv()
    pre_ref[...] = (own[...] + in_v[...].astype(F32)).astype(BF16)
    for c in tiles_out:
        c.wait_recv()
    lane = lax.broadcasted_iota(jnp.int32, tile.shape, 1)
    for half in range(2):
        first = tiles[2 * half].astype(F32)
        second = pltpu.roll(tiles[2 * half + 1].astype(F32), narrow // 2, 1)
        states_ref[:, half * narrow : (half + 1) * narrow] = jnp.where(
            lane < narrow // 2, first, second
        ).astype(BF16)

    to_far[2].wait_recv()
    passed[2].start()
    to_beside[2].wait_recv()
    passed[2].wait_recv()
    out_g[...] = product(1, windows[2]).astype(BF16)
    part_g = rdma(out_g, in_g, part_send.at[2], part_recv.at[2], partner, h)
    part_g.start()
    own[...] = product(0, windows[2])
    part_g.wait_recv()
    gate_ref[...] = (own[...] + in_g[...].astype(F32)).astype(BF16)
    for c in [*to_far, *to_beside, *passed, *hid_over, *hid_own, *hid_pass, *tiles_out]:
        c.wait_send()
    for c in (part_s, part_v, part_g):
        c.wait_send()


def project(hidden, w_values, w_gates, w_steps, w_states):
    group = lax.axis_index("head")
    rows = hidden.shape[0] * 4
    width = w_values.shape[1]
    share = w_states.shape[1] // 4
    narrow = 2 * share
    part = lax.dynamic_slice_in_dim(w_states, group * share, share, 1)
    small = jnp.concatenate(
        [part, w_steps, jnp.zeros((w_steps.shape[0], narrow - share - w_steps.shape[1]), BF16)],
        axis=1,
    )
    depth = 2 * w_values.shape[0]
    vmem = pl.BlockSpec(memory_space=pltpu.VMEM)
    anywhere = pl.BlockSpec(memory_space=pl.ANY)
    dma = pltpu.SemaphoreType.DMA
    pre, states, steps, gates = pl.pallas_call(
        project_kernel,
        out_shape=(
            jax.ShapeDtypeStruct((rows, width), BF16),
            jax.ShapeDtypeStruct((rows, 2 * narrow), BF16),
            jax.ShapeDtypeStruct((rows, narrow), F32),
            jax.ShapeDtypeStruct((rows, width), BF16),
        ),
        in_specs=[anywhere] * 4,
        out_specs=[vmem] * 4,
        scratch_shapes=[
            pltpu.VMEM((2, 2, rows, depth), BF16),
            pltpu.VMEM((2, depth, 2 * width + narrow), BF16),
            pltpu.VMEM((rows, width), BF16),
            pltpu.VMEM((rows, narrow), F32),
            pltpu.VMEM((rows, width), BF16),
            pltpu.VMEM((rows, width), BF16),
            pltpu.VMEM((rows, narrow), F32),
            pltpu.VMEM((rows, width), BF16),
            pltpu.VMEM((rows, width), F32),
            pltpu.VMEM((rows, narrow), BF16),
            pltpu.VMEM((4, rows, narrow), BF16),
            dma((5,)),
            dma((7, 2)),
            dma((7, 2)),
            dma((3, 3)),
            dma((3, 3)),
            dma((3,)),
            dma((3,)),
            dma((3,)),
            dma((3,)),
        ],
        compiler_params=pltpu.CompilerParams(
            collective_id=0, has_side_effects=True, vmem_limit_bytes=48 * 1024 * 1024
        ),
    )(hidden, w_values, small, w_gates)
    return pre, states, steps[:, share : share + w_steps.shape[1]], gates


def on_device(
    hidden,
    w_values,
    w_gates,
    w_steps,
    w_states,
    conv_weight,
    conv_bias,
    step_bias,
    decay_rate,
    skip_gain,
    norm_gain,
    lengths,
):
    groups = lax.axis_size("head")
    group_index = lax.axis_index("head")
    block_index = lax.axis_index("seq")
    local_width = w_values.shape[1]
    inner_width = local_width * groups
    local_heads = decay_rate.shape[0]
    head_width = local_width // local_heads
    state_width = w_states.shape[1] // 2
    conv_taps = conv_weight.shape[0]
    prompt_ends = jnp.cumsum(lengths)
    block_rows = hidden.shape[0] * groups
    sub_rows = hidden.shape[0]
    if lax.axis_size("seq") == 8 and groups == 4:
        values_in, states_in, steps_sum, head_gates = project(
            hidden, w_values, w_gates, w_steps, w_states
        )
    else:
        block_hidden = lax.all_gather(hidden, "head", axis=0, tiled=True)

        def contract(piece):
            return jnp.dot(
                block_hidden,
                lax.all_gather(piece, "seq", axis=0, tiled=True),
                preferred_element_type=jnp.float32,
            )

        values_in = contract(w_values).astype(jnp.bfloat16)
        states_in = contract(w_states).astype(jnp.bfloat16)
        steps_sum = contract(w_steps)
        head_gates = contract(w_gates).astype(jnp.bfloat16)
    pre_rows = jnp.concatenate([values_in, states_in], axis=1)
    local_taps = jnp.concatenate(
        [
            lax.dynamic_slice_in_dim(conv_weight, group_index * local_width, local_width, 1),
            conv_weight[:, inner_width:],
        ],
        axis=1,
    )
    local_bias = jnp.concatenate(
        [
            lax.dynamic_slice_in_dim(conv_bias, group_index * local_width, local_width, 0),
            conv_bias[inner_width:],
        ],
        axis=0,
    )
    block_start = block_index * block_rows
    rim_rows = pre_rows[block_rows - (conv_taps - 1) :]
    prior_rim = from_behind(rim_rows, "seq", 1)
    extended = jnp.concatenate([prior_rim, pre_rows], axis=0)
    ext_positions = (
        block_start - (conv_taps - 1) + jnp.arange(block_rows + conv_taps - 1, dtype=jnp.int32)
    )
    ext_ids = segments_at(ext_positions, prompt_ends)
    own_ids = ext_ids[conv_taps - 1 :]
    filtered = jnp.zeros(pre_rows.shape, jnp.float32) + local_bias[None, :]
    for offset in range(conv_taps):
        matches = (ext_ids[offset : offset + block_rows] == own_ids).astype(jnp.float32)
        filtered = (
            filtered
            + local_taps[offset][None, :]
            * extended[offset : offset + block_rows].astype(jnp.float32)
            * matches[:, None]
        )
    conv_out = jax.nn.silu(filtered).astype(jnp.bfloat16)
    head_values = conv_out[:, :local_width]
    both_states = conv_out[:, local_width:]
    stretch_rows = STRETCH
    stretches = block_rows // stretch_rows
    positions = block_start + jnp.arange(block_rows, dtype=jnp.int32)
    segment_ids = segments_at(positions, prompt_ends)
    next_ids = segments_at(positions + 1, prompt_ends)
    before_ids = segments_at(positions - 1, prompt_ends)
    stretch_ids = segment_ids.reshape(stretches, stretch_rows)
    prior_ids = before_ids.reshape(stretches, stretch_rows)[:, 0]
    ends_mask = (segment_ids != next_ids).reshape(stretches, stretch_rows)
    step_sizes = jax.nn.softplus(steps_sum + step_bias[None, :])
    decay_steps = step_sizes * decay_rate[None, :]
    log_decay = -jnp.cumsum(decay_steps.reshape(stretches, stretch_rows, local_heads), axis=1)
    decay_heads = jnp.swapaxes(log_decay, 1, 2)
    step_heads = jnp.swapaxes(step_sizes.reshape(stretches, stretch_rows, local_heads), 1, 2)
    values = head_values.reshape(stretches, stretch_rows, local_heads, head_width)
    write_state = both_states[:, :state_width].reshape(stretches, stretch_rows, state_width)
    read_state = both_states[:, state_width:].reshape(stretches, stretch_rows, state_width)
    intersection = jnp.einsum(
        "ctn,csn->cts", read_state, write_state, preferred_element_type=jnp.float32
    )
    token_order = jnp.arange(stretch_rows, dtype=jnp.int32)
    causal = token_order[:, None] >= token_order[None, :]
    allowed = causal[None] & (stretch_ids[:, :, None] == stretch_ids[:, None, :])
    spread = decay_heads[:, :, :, None] - decay_heads[:, :, None, :]
    weights = (
        jnp.where(allowed[:, None], jnp.exp(jnp.minimum(spread, 0.0)), 0.0)
        * step_heads[:, :, None, :]
    )
    scores = (intersection[:, None] * weights).astype(jnp.bfloat16)
    within_stretch = jnp.einsum(
        "chts,cshp->cthp", scores, values, preferred_element_type=jnp.float32
    )
    last_ids = stretch_ids[:, -1]
    tail_decay = decay_heads[:, :, -1:]
    keep_tail = (stretch_ids == last_ids[:, None])[:, None, :]
    tail_coef = (
        jnp.where(keep_tail, jnp.exp(jnp.minimum(tail_decay - decay_heads, 0.0)), 0.0) * step_heads
    )
    tail_rows = (values.astype(jnp.float32) * jnp.swapaxes(tail_coef, 1, 2)[:, :, :, None]).astype(
        jnp.bfloat16
    )
    stretch_states = jnp.einsum(
        "clhp,cln->chpn", tail_rows, write_state, preferred_element_type=jnp.float32
    )
    stretch_gates = (
        jnp.exp(decay_heads[:, :, -1]) * (last_ids == prior_ids).astype(jnp.float32)[:, None]
    )
    block_gate = jnp.ones((local_heads,), jnp.float32)
    block_state = jnp.zeros((local_heads, head_width, state_width), jnp.float32)
    block_state = stretch_gates[0][:, None, None] * block_state + stretch_states[0]
    block_gate = block_gate * stretch_gates[0]

    def compose(earlier, later):
        return (earlier[0] * later[0], later[0][:, None, None] * earlier[1] + later[1])

    identity_pair = (jnp.ones_like(block_gate), jnp.zeros_like(block_state))
    carried = prefix((block_gate, block_state), "seq", compose, identity_pair)
    incoming = carried[1]
    arriving = []
    arriving.append(incoming)
    arriving = jnp.stack(arriving)
    carry_mask = (stretch_ids == prior_ids[:, None]).astype(jnp.float32)
    carry_decay = jnp.exp(log_decay) * carry_mask[:, :, None]
    from_before = (
        jnp.einsum(
            "cln,chpn->clhp",
            read_state,
            arriving.astype(jnp.bfloat16),
            preferred_element_type=jnp.float32,
        )
        * carry_decay[:, :, :, None]
    )
    result = (
        within_stretch + from_before + skip_gain[None, None, :, None] * values.astype(jnp.float32)
    )
    ssm_rows = result.reshape(block_rows, local_width).astype(jnp.bfloat16)
    end_weight = ends_mask.astype(jnp.float32)
    has_end = jnp.sum(end_weight, axis=1)
    end_decay = jnp.sum(decay_heads * end_weight[:, None, :], axis=2)
    end_ids = jnp.sum(jnp.where(ends_mask, stretch_ids, 0), axis=1)
    keep_end = ((stretch_ids == end_ids[:, None]) & (has_end[:, None] > 0))[:, None, :]
    end_coef = (
        jnp.where(keep_end, jnp.exp(jnp.minimum(end_decay[:, :, None] - decay_heads, 0.0)), 0.0)
        * step_heads
    )
    end_rows = (values.astype(jnp.float32) * jnp.swapaxes(end_coef, 1, 2)[:, :, :, None]).astype(
        jnp.bfloat16
    )
    end_states = jnp.einsum(
        "clhp,cln->chpn", end_rows, write_state, preferred_element_type=jnp.float32
    )
    end_carry = (
        jnp.exp(end_decay) * ((end_ids == prior_ids) & (has_end > 0)).astype(jnp.float32)[:, None]
    )
    end_states = end_states + end_carry[:, :, None, None] * arriving
    final_block = jnp.sum(end_states, axis=0)[None]
    norm_slice = lax.dynamic_slice_in_dim(norm_gain, group_index * local_width, local_width)
    gated = ssm_rows.astype(jnp.float32) * jax.nn.silu(head_gates.astype(jnp.float32))
    squares = lax.psum(jnp.sum(gated * gated, axis=1), "head")
    scaled = gated * lax.rsqrt(squares / inner_width + epsilon)[:, None] * norm_slice[None, :]
    outgoing = scaled.astype(jnp.bfloat16)
    returned = lax.all_to_all(
        outgoing.reshape(groups, sub_rows, local_width),
        "head",
        split_axis=0,
        concat_axis=2,
        tiled=True,
    )
    gated_out = returned.reshape(sub_rows, inner_width)
    return (gated_out, final_block)


def solution(mesh):
    in_specs = (
        P(("seq", "head"), None),
        P("seq", "head"),
        P("seq", "head"),
        P("seq", "head"),
        P("seq", None),
        P(),
        P(),
        P("head"),
        P("head"),
        P("head"),
        P(),
        P(),
    )
    out_specs = (P(("seq", "head"), None), P("seq", "head", None, None))
    return jax.shard_map(
        on_device, mesh=mesh, in_specs=in_specs, out_specs=out_specs, check_vma=False
    )
```

```python
import jax
import jax.numpy as jnp
from jax import lax
from jax.experimental import pallas as pl
from jax.experimental.pallas import tpu as pltpu
from jax.sharding import PartitionSpec as P

STRETCH = 256


epsilon = 1e-05


def from_behind(block, axis, distance):
    devices = range(lax.axis_size(axis))
    route = [(i - distance, i) for i in devices if i - distance in devices]
    return lax.ppermute(block, axis, route)


def prefix(value, axis, join, neutral):
    place = lax.axis_index(axis)
    gathered = jax.tree.map(
        lambda a, kind: lax.all_gather(a.astype(kind), axis), value, (jnp.bfloat16, jnp.bfloat16)
    )
    state = jax.tree.map(lambda a, e: jnp.zeros_like(a) + jnp.asarray(e, a.dtype), value, neutral)

    def one(turn, state):
        return join(
            state,
            jax.tree.map(
                lambda a, own: lax.dynamic_index_in_dim(a, turn, 0, False).astype(own.dtype),
                gathered,
                value,
            ),
        )

    return lax.fori_loop(0, place, one, state)


def segments_at(positions, prompt_ends):
    counted = jnp.sum((prompt_ends[None, :] <= positions[:, None]).astype(jnp.int32), axis=1)
    return jnp.where(positions < 0, -1, counted)


MESH = pl.DeviceIdType.MESH
BF16 = jnp.bfloat16
F32 = jnp.float32


def rdma(src, dst, send_sem, recv_sem, seq, head):
    return pltpu.make_async_remote_copy(
        src_ref=src,
        dst_ref=dst,
        send_sem=send_sem,
        recv_sem=recv_sem,
        device_id=(seq, head),
        device_id_type=MESH,
    )


def layer_kernel(
    hidden_ref,
    values_ref,
    small_ref,
    gates_ref,
    taps_ref,
    bias_ref,
    heads_ref,
    norm_ref,
    lengths_ref,
    out_ref,
    final_ref,
    hid,
    wbuf,
    out_v,
    out_s,
    out_g,
    in_v,
    in_s,
    in_g,
    own,
    tile,
    tiles,
    local_sem,
    hid_send,
    hid_recv,
    w_send,
    w_recv,
    part_send,
    part_recv,
    tile_send,
    tile_recv,
    halo_out,
    halo_in,
    ext,
    conv,
    cum_ref,
    cum_rows,
    dt_rows,
    carry_ref,
    end_ref,
    y_ref,
    inc,
    local_out,
    gate_out,
    local_in,
    gate_in,
    gated,
    whole,
    halo_send,
    halo_recv,
    state_send,
    state_recv,
    turn_send,
    turn_recv,
):
    s = lax.axis_index("seq")
    h = lax.axis_index("head")
    z = lax.div(s, 2)
    x = lax.rem(s, 2)
    z_lo = lax.rem(z, 2)
    z_hi = lax.div(z, 2)
    beside = s + 1 - 2 * x
    partner = s + 2 - 4 * z_lo
    far = s + 4 - 8 * z_hi
    heads = [lax.rem(h + d, 4) for d in (1, 2, 3)]
    rows_w = values_ref.shape[0]
    rows_h = hidden_ref.shape[0]
    depth = 2 * rows_w
    width = values_ref.shape[1]
    narrow = small_ref.shape[1]

    barrier = pltpu.get_barrier_semaphore()
    for d in range(1, 8):
        pl.semaphore_signal(
            barrier, inc=1, device_id=(lax.rem(s + d, 8), h), device_id_type=MESH
        )
    for to in heads:
        pl.semaphore_signal(barrier, inc=1, device_id=(s, to), device_id_type=MESH)

    my_rows = pl.ds(pl.multiple_of(x * rows_w, 64), rows_w)
    my_tokens = pl.ds(pl.multiple_of(h * rows_h, 64), rows_h)
    windows = (pl.ds(0, width), pl.ds(width, narrow), pl.ds(width + narrow, width))
    sources = (values_ref, small_ref, gates_ref)

    def columns(low, zh):
        return pl.ds(pl.multiple_of((low + 2 * zh) * depth, 128), depth)

    local = []
    for p in range(3):
        local.append(
            pltpu.make_async_copy(
                sources[p], wbuf.at[z_hi, my_rows, windows[p]], local_sem.at[p]
            )
        )
    for zh in range(2):
        local.append(
            pltpu.make_async_copy(
                hidden_ref.at[:, columns(z_lo, zh)],
                hid.at[0, zh, my_tokens],
                local_sem.at[3 + zh],
            )
        )
    for c in local:
        c.start()
    pl.semaphore_wait(barrier, 10)

    to_far = [
        rdma(sources[p], wbuf.at[z_hi, my_rows, windows[p]], w_send.at[0, p], w_recv.at[0, p], far, h)
        for p in range(3)
    ]
    to_beside = [
        rdma(sources[p], wbuf.at[z_hi, my_rows, windows[p]], w_send.at[1, p], w_recv.at[1, p], beside, h)
        for p in range(3)
    ]
    passed = [
        rdma(
            wbuf.at[1 - z_hi, my_rows, windows[p]],
            wbuf.at[1 - z_hi, my_rows, windows[p]],
            w_send.at[2, p],
            w_recv.at[2, p],
            beside,
            h,
        )
        for p in range(3)
    ]
    hid_over = [
        rdma(
            hidden_ref.at[:, columns(1 - z_lo, zh)],
            hid.at[1, zh, my_tokens],
            hid_send.at[0, zh],
            hid_recv.at[0, zh],
            partner,
            h,
        )
        for zh in range(2)
    ]
    hid_own = [
        rdma(
            hidden_ref.at[:, columns(z_lo, zh)],
            hid.at[0, zh, my_tokens],
            hid_send.at[1 + d, zh],
            hid_recv.at[1 + d, zh],
            s,
            heads[d],
        )
        for zh in range(2)
        for d in range(3)
    ]
    hid_pass = [
        rdma(
            hid.at[1, zh, my_tokens],
            hid.at[1, zh, my_tokens],
            hid_send.at[4 + d, zh],
            hid_recv.at[4 + d, zh],
            s,
            heads[d],
        )
        for zh in range(2)
        for d in range(3)
    ]
    for c in hid_over:
        c.start()
    for p in (0, 1):
        to_far[p].start()
    for p in (0, 1):
        to_beside[p].start()
    for c in hid_own:
        c.start()
    for zh in range(2):
        hid_over[zh].wait_recv()
        for d in range(3):
            hid_pass[3 * zh + d].start()
    for p in (0, 1):
        to_far[p].wait_recv()
        passed[p].start()
    to_far[2].start()
    to_beside[2].start()
    for c in local:
        c.wait()
    for c in hid_own:
        c.wait_recv()
    for c in hid_pass:
        c.wait_recv()
    for p in (0, 1):
        to_beside[p].wait_recv()
        passed[p].wait_recv()

    def product(which, window):
        return jnp.dot(
            hid[which, 0], wbuf[0, :, window], preferred_element_type=F32
        ) + jnp.dot(hid[which, 1], wbuf[1, :, window], preferred_element_type=F32)

    out_s[...] = product(1, windows[1])
    part_s = rdma(out_s, in_s, part_send.at[0], part_recv.at[0], partner, h)
    part_s.start()
    out_v[...] = product(1, windows[0]).astype(BF16)
    part_v = rdma(out_v, in_v, part_send.at[1], part_recv.at[1], partner, h)
    part_v.start()
    small = product(0, windows[1])
    part_s.wait_recv()
    small = small + in_s[...]
    tile[...] = small.astype(BF16)
    tiles_out = [
        rdma(tile, tiles.at[h], tile_send.at[d], tile_recv.at[d], s, heads[d]) for d in range(3)
    ]
    for c in tiles_out:
        c.start()
    tiles[h] = tile[...]
    own[...] = product(0, windows[0])
    to_far[2].wait_recv()
    passed[2].start()

    rows = own.shape[0]
    start = s * rows
    count = lengths_ref.shape[0]
    ends = []
    for i in range(count):
        ends.append(lengths_ref[i] + (ends[i - 1] if i else 0))

    def segment(position):
        found = jnp.where(position < 0, -1, 0)
        for end in ends:
            found = found + jnp.where(end <= position, 1, 0)
        return found

    last_id = segment(start + rows - 1)
    prior_id = segment(start - 1)
    end_id = jnp.int32(-2)
    end_row = jnp.int32(-1)
    for i, end in enumerate(ends):
        inside = (end - 1 >= start) & (end - 1 < start + rows)
        end_id = jnp.where(inside, i, end_id)
        end_row = jnp.where(inside, end - 1 - start, end_row)

    order = lax.broadcasted_iota(jnp.int32, (rows, rows), 0)
    across = lax.broadcasted_iota(jnp.int32, (rows, rows), 1)
    lower = order >= across
    lower_ones = lower.astype(F32).astype(BF16)
    lane = lax.broadcasted_iota(jnp.int32, (rows, narrow), 1)
    token = lax.broadcasted_iota(jnp.int32, (rows, narrow), 0)
    ids = segment(start + token)

    def parts(value, number):
        taken = []
        for _ in range(number):
            piece = value.astype(BF16)
            taken.append(piece)
            value = value - piece.astype(F32)
        return taken

    share = narrow // 2
    step = jax.nn.softplus(small + heads_ref[0:1, :])
    rate = step * heads_ref[1:2, :]
    cum = jnp.zeros((rows, narrow), F32)
    for piece in parts(rate, 3):
        cum = cum - jnp.dot(lower_ones, piece, preferred_element_type=F32)
    cum_ref[...] = cum
    cum_rows[...] = cum.T
    dt_rows[...] = step.T
    head_row = lax.broadcasted_iota(jnp.int32, (narrow, width), 0) - share
    channel = lax.broadcasted_iota(jnp.int32, (narrow, width), 1)
    spread = (
        ((channel >= head_row * share) & (channel < head_row * share + share))
        .astype(F32)
        .astype(BF16)
    )

    def expand(value, number):
        total = None
        for piece in parts(value, number):
            term = jnp.dot(piece, spread, preferred_element_type=F32)
            total = term if total is None else total + term
        return total

    cum_last = cum[rows - 1 : rows, :]
    cum_end = jnp.sum(jnp.where(token == end_row, cum, 0.0), axis=0, keepdims=True)
    gate_row = jnp.where(last_id == prior_id, jnp.exp(cum_last), 0.0)
    end_gate = jnp.where(end_id == prior_id, jnp.exp(cum_end), 0.0)
    eight = lax.broadcasted_iota(jnp.int32, (8, narrow), 0)
    rows8 = jnp.where(
        eight == 0,
        gate_row,
        jnp.where(eight == 1, end_gate, jnp.where(eight == 2, heads_ref[2:3, :], 0.0)),
    )
    wide8 = expand(rows8, 3)
    gate_out[...] = wide8
    tail = jnp.where(ids == last_id, jnp.exp(jnp.minimum(cum_last - cum, 0.0)), 0.0) * step
    tail_wide = expand(tail, 2)
    end_ref[...] = expand(
        jnp.where(ids == end_id, jnp.exp(jnp.minimum(cum_end - cum, 0.0)), 0.0) * step, 2
    )
    carry_ref[...] = expand(jnp.where(ids == prior_id, jnp.exp(cum), 0.0), 2)

    part_v.wait_recv()
    pre = (own[...] + in_v[...].astype(F32)).astype(BF16)
    ext[8:, 0:width] = pre.astype(F32)
    halo_out[:, 0:width] = pre[rows - 16 :, :]
    for c in tiles_out:
        c.wait_recv()
    for half in range(2):
        first = tiles[2 * half].astype(F32)
        second = pltpu.roll(tiles[2 * half + 1].astype(F32), share, 1)
        both = jnp.where(lane < share, first, second)
        low = width + half * narrow
        ext[8:, low : low + narrow] = both
        halo_out[:, low : low + narrow] = both[rows - 16 :, :].astype(BF16)
    halo = rdma(
        halo_out, halo_in, halo_send.at[0], halo_recv.at[0], lax.rem(s + 1, 8), h
    )
    halo.start()

    to_beside[2].wait_recv()
    passed[2].wait_recv()
    out_g[...] = product(1, windows[2]).astype(BF16)
    part_g = rdma(out_g, in_g, part_send.at[2], part_recv.at[2], partner, h)
    part_g.start()
    own[...] = product(0, windows[2])

    halo.wait_recv()
    ext[0:8, :] = halo_in[8:16, :].astype(F32)
    inner = 4 * width
    same = [
        (segment(start + token - d) == ids).astype(F32) for d in range(3, 0, -1)
    ]
    chunks = (width + 2 * narrow) // narrow
    for j in range(chunks):
        low = j * narrow
        if low < width:
            from_lane = pl.ds(pl.multiple_of(h * width + low, 128), narrow)
        else:
            from_lane = pl.ds(inner + low - width, narrow)
        taps = taps_ref[:, from_lane]
        total = jnp.zeros((rows, narrow), F32) + bias_ref[:, from_lane]
        for tap in range(4):
            piece = ext[5 + tap : 5 + tap + rows, low : low + narrow] * taps[tap : tap + 1, :]
            total = total + (piece * same[tap] if tap < 3 else piece)
        conv[:, low : low + narrow] = jax.nn.silu(total).astype(BF16)

    values = conv[:, 0:width]
    write_turned = conv[:, width : width + narrow].astype(F32).T.astype(BF16)
    read_state = conv[:, width + narrow :]
    local_out[...] = jnp.dot(
        write_turned,
        (values.astype(F32) * tail_wide).astype(BF16),
        preferred_element_type=F32,
    ).astype(BF16)
    onward = []
    for d in range(3):
        to = lax.rem(s + d + 1, 8)
        onward.append(
            (
                rdma(local_out, local_in.at[d], state_send.at[0, d], state_recv.at[0, d], to, h),
                rdma(gate_out, gate_in.at[d], state_send.at[1, d], state_recv.at[1, d], to, h),
            )
        )
    for d in range(3):

        @pl.when(s + d + 1 < 8)
        def _(d=d):
            onward[d][0].start()
            onward[d][1].start()

    met = jnp.where(
        lower & (segment(start + order) == segment(start + across)),
        jnp.dot(read_state, write_turned, preferred_element_type=F32),
        0.0,
    )
    pairs = width // narrow
    for j in range(pairs):
        pair = conv[:, j * narrow : (j + 1) * narrow]
        halves = []
        for a in range(2):
            at = share + 2 * j + a
            decay = cum_ref[:, at : at + 1] - cum_rows[at : at + 1, :]
            scores = met * jnp.exp(jnp.minimum(decay, 0.0)) * dt_rows[at : at + 1, :]
            halves.append(jnp.dot(scores.astype(BF16), pair, preferred_element_type=F32))
        y_ref[:, j * narrow : (j + 1) * narrow] = jnp.where(lane < share, halves[0], halves[1])
    end_local = jnp.dot(
        write_turned,
        (values.astype(F32) * end_ref[...]).astype(BF16),
        preferred_element_type=F32,
    )

    inc[...] = jnp.zeros(inc.shape, F32)
    for d in range(3):

        @pl.when(s >= d + 1)
        def _(d=d):
            onward[d][0].wait_recv()
            onward[d][1].wait_recv()
            arrived = local_in[d].astype(F32)
            for e in range(d):
                arrived = arrived * gate_in[e, 0:1, :]
            inc[...] += arrived

    part_g.wait_recv()
    for j in range(pairs):
        span = slice(j * narrow, (j + 1) * narrow)
        state = inc[:, span]
        final_ref[span, :] = (end_local[:, span] + wide8[1:2, span] * state).T
        before = jnp.dot(read_state, state.astype(BF16), preferred_element_type=F32)
        y = (
            y_ref[:, span]
            + before * carry_ref[:, span]
            + wide8[2:3, span] * conv[:, span].astype(F32)
        ).astype(BF16)
        gate = (own[:, span] + in_g[:, span].astype(F32)).astype(BF16).astype(F32)
        gated[:, span] = (y.astype(F32) * jax.nn.silu(gate)).astype(BF16)

    my_columns = pl.ds(pl.multiple_of(h * width, 128), width)
    turned = [
        rdma(
            gated.at[pl.ds(pl.multiple_of(heads[d] * rows_h, 64), rows_h)],
            whole.at[:, my_columns],
            turn_send.at[d],
            turn_recv.at[d],
            s,
            heads[d],
        )
        for d in range(3)
    ]
    for c in turned:
        c.start()
    keep = pltpu.make_async_copy(gated.at[my_tokens], whole.at[:, my_columns], local_sem.at[5])
    keep.start()
    keep.wait()
    for c in turned:
        c.wait_recv()
    full = whole[...].astype(F32)
    mean = jnp.sum(full * full, axis=1, keepdims=True) / inner
    out_ref[...] = (full * lax.rsqrt(mean + epsilon) * norm_ref[...]).astype(BF16)

    for c in [*to_far, *to_beside, *passed, *hid_over, *hid_own, *hid_pass, *tiles_out, *turned]:
        c.wait_send()
    for c in (part_s, part_v, part_g, halo):
        c.wait_send()
    for d in range(3):

        @pl.when(s + d + 1 < 8)
        def _(d=d):
            onward[d][0].wait_send()
            onward[d][1].wait_send()


def layer(
    hidden,
    w_values,
    w_gates,
    w_steps,
    w_states,
    conv_weight,
    conv_bias,
    step_bias,
    decay_rate,
    skip_gain,
    norm_gain,
    lengths,
):
    group = lax.axis_index("head")
    rows = hidden.shape[0] * 4
    width = w_values.shape[1]
    count = step_bias.shape[0]
    share = w_states.shape[1] // 4
    narrow = 2 * share
    part = lax.dynamic_slice_in_dim(w_states, group * share, share, 1)
    small = jnp.concatenate(
        [part, w_steps, jnp.zeros((w_steps.shape[0], narrow - share - count), BF16)],
        axis=1,
    )
    per_head = jnp.pad(
        jnp.stack([step_bias, decay_rate, skip_gain]), ((0, 5), (share, narrow - share - count))
    )
    depth = 2 * w_values.shape[0]
    channels = width + 2 * narrow
    vmem = pl.BlockSpec(memory_space=pltpu.VMEM)
    smem = pl.BlockSpec(memory_space=pltpu.SMEM)
    anywhere = pl.BlockSpec(memory_space=pl.ANY)
    dma = pltpu.SemaphoreType.DMA
    gated_out, final = pl.pallas_call(
        layer_kernel,
        out_shape=(
            jax.ShapeDtypeStruct(hidden.shape, BF16),
            jax.ShapeDtypeStruct((width, narrow), F32),
        ),
        in_specs=[anywhere] * 4 + [vmem] * 4 + [smem],
        out_specs=[vmem] * 2,
        scratch_shapes=[
            pltpu.VMEM((2, 2, rows, depth), BF16),
            pltpu.VMEM((2, depth, 2 * width + narrow), BF16),
            pltpu.VMEM((rows, width), BF16),
            pltpu.VMEM((rows, narrow), F32),
            pltpu.VMEM((rows, width), BF16),
            pltpu.VMEM((rows, width), BF16),
            pltpu.VMEM((rows, narrow), F32),
            pltpu.VMEM((rows, width), BF16),
            pltpu.VMEM((rows, width), F32),
            pltpu.VMEM((rows, narrow), BF16),
            pltpu.VMEM((4, rows, narrow), BF16),
            dma((6,)),
            dma((7, 2)),
            dma((7, 2)),
            dma((3, 3)),
            dma((3, 3)),
            dma((3,)),
            dma((3,)),
            dma((3,)),
            dma((3,)),
            pltpu.VMEM((16, channels), BF16),
            pltpu.VMEM((16, channels), BF16),
            pltpu.VMEM((8 + rows, channels), F32),
            pltpu.VMEM((rows, channels), BF16),
            pltpu.VMEM((rows, narrow), F32),
            pltpu.VMEM((narrow, rows), F32),
            pltpu.VMEM((narrow, rows), F32),
            pltpu.VMEM((rows, width), F32),
            pltpu.VMEM((rows, width), F32),
            pltpu.VMEM((rows, width), F32),
            pltpu.VMEM((narrow, width), F32),
            pltpu.VMEM((narrow, width), BF16),
            pltpu.VMEM((8, width), F32),
            pltpu.VMEM((3, narrow, width), BF16),
            pltpu.VMEM((3, 8, width), F32),
            pltpu.VMEM((rows, width), BF16),
            pltpu.VMEM(hidden.shape, BF16),
            dma((1,)),
            dma((1,)),
            dma((2, 3)),
            dma((2, 3)),
            dma((3,)),
            dma((3,)),
        ],
        compiler_params=pltpu.CompilerParams(
            collective_id=0, has_side_effects=True, vmem_limit_bytes=48 * 1024 * 1024
        ),
    )(
        hidden,
        w_values,
        small,
        w_gates,
        conv_weight,
        conv_bias[None, :],
        per_head,
        norm_gain[None, :],
        lengths,
    )
    return gated_out, final.reshape(1, count, width // count, narrow)


def on_device(
    hidden,
    w_values,
    w_gates,
    w_steps,
    w_states,
    conv_weight,
    conv_bias,
    step_bias,
    decay_rate,
    skip_gain,
    norm_gain,
    lengths,
):
    groups = lax.axis_size("head")
    if lax.axis_size("seq") == 8 and groups == 4:
        return layer(
            hidden,
            w_values,
            w_gates,
            w_steps,
            w_states,
            conv_weight,
            conv_bias,
            step_bias,
            decay_rate,
            skip_gain,
            norm_gain,
            lengths,
        )
    group_index = lax.axis_index("head")
    block_index = lax.axis_index("seq")
    local_width = w_values.shape[1]
    inner_width = local_width * groups
    local_heads = decay_rate.shape[0]
    head_width = local_width // local_heads
    state_width = w_states.shape[1] // 2
    conv_taps = conv_weight.shape[0]
    prompt_ends = jnp.cumsum(lengths)
    block_hidden = lax.all_gather(hidden, "head", axis=0, tiled=True)
    block_rows = block_hidden.shape[0]
    sub_rows = block_rows // groups

    def contract(piece):
        return jnp.dot(block_hidden, piece, preferred_element_type=jnp.float32)

    pieces = (
        lax.all_gather(w_values, "seq", axis=0, tiled=True),
        lax.all_gather(w_states, "seq", axis=0, tiled=True),
        lax.all_gather(w_steps, "seq", axis=0, tiled=True),
        lax.all_gather(w_gates, "seq", axis=0, tiled=True),
    )
    values_sum, states_sum, steps_sum, gates_sum = tuple((contract(piece) for piece in pieces))
    pre_rows = jnp.concatenate(
        [values_sum.astype(jnp.bfloat16), states_sum.astype(jnp.bfloat16)], axis=1
    )
    local_taps = jnp.concatenate(
        [
            lax.dynamic_slice_in_dim(conv_weight, group_index * local_width, local_width, 1),
            conv_weight[:, inner_width:],
        ],
        axis=1,
    )
    local_bias = jnp.concatenate(
        [
            lax.dynamic_slice_in_dim(conv_bias, group_index * local_width, local_width, 0),
            conv_bias[inner_width:],
        ],
        axis=0,
    )
    block_start = block_index * block_rows
    rim_rows = pre_rows[block_rows - (conv_taps - 1) :]
    prior_rim = from_behind(rim_rows, "seq", 1)
    extended = jnp.concatenate([prior_rim, pre_rows], axis=0)
    ext_positions = (
        block_start - (conv_taps - 1) + jnp.arange(block_rows + conv_taps - 1, dtype=jnp.int32)
    )
    ext_ids = segments_at(ext_positions, prompt_ends)
    own_ids = ext_ids[conv_taps - 1 :]
    filtered = jnp.zeros(pre_rows.shape, jnp.float32) + local_bias[None, :]
    for offset in range(conv_taps):
        matches = (ext_ids[offset : offset + block_rows] == own_ids).astype(jnp.float32)
        filtered = (
            filtered
            + local_taps[offset][None, :]
            * extended[offset : offset + block_rows].astype(jnp.float32)
            * matches[:, None]
        )
    conv_out = jax.nn.silu(filtered).astype(jnp.bfloat16)
    head_values = conv_out[:, :local_width]
    both_states = conv_out[:, local_width:]
    stretch_rows = STRETCH
    stretches = block_rows // stretch_rows
    positions = block_start + jnp.arange(block_rows, dtype=jnp.int32)
    segment_ids = segments_at(positions, prompt_ends)
    next_ids = segments_at(positions + 1, prompt_ends)
    before_ids = segments_at(positions - 1, prompt_ends)
    stretch_ids = segment_ids.reshape(stretches, stretch_rows)
    prior_ids = before_ids.reshape(stretches, stretch_rows)[:, 0]
    ends_mask = (segment_ids != next_ids).reshape(stretches, stretch_rows)
    step_sizes = jax.nn.softplus(steps_sum + step_bias[None, :])
    decay_steps = step_sizes * decay_rate[None, :]
    log_decay = -jnp.cumsum(decay_steps.reshape(stretches, stretch_rows, local_heads), axis=1)
    decay_heads = jnp.swapaxes(log_decay, 1, 2)
    step_heads = jnp.swapaxes(step_sizes.reshape(stretches, stretch_rows, local_heads), 1, 2)
    values = head_values.reshape(stretches, stretch_rows, local_heads, head_width)
    write_state = both_states[:, :state_width].reshape(stretches, stretch_rows, state_width)
    read_state = both_states[:, state_width:].reshape(stretches, stretch_rows, state_width)
    intersection = jnp.einsum(
        "ctn,csn->cts", read_state, write_state, preferred_element_type=jnp.float32
    )
    token_order = jnp.arange(stretch_rows, dtype=jnp.int32)
    causal = token_order[:, None] >= token_order[None, :]
    allowed = causal[None] & (stretch_ids[:, :, None] == stretch_ids[:, None, :])
    spread = decay_heads[:, :, :, None] - decay_heads[:, :, None, :]
    weights = (
        jnp.where(allowed[:, None], jnp.exp(jnp.minimum(spread, 0.0)), 0.0)
        * step_heads[:, :, None, :]
    )
    scores = (intersection[:, None] * weights).astype(jnp.bfloat16)
    within_stretch = jnp.einsum(
        "chts,cshp->cthp", scores, values, preferred_element_type=jnp.float32
    )
    last_ids = stretch_ids[:, -1]
    tail_decay = decay_heads[:, :, -1:]
    keep_tail = (stretch_ids == last_ids[:, None])[:, None, :]
    tail_coef = (
        jnp.where(keep_tail, jnp.exp(jnp.minimum(tail_decay - decay_heads, 0.0)), 0.0) * step_heads
    )
    tail_rows = (values.astype(jnp.float32) * jnp.swapaxes(tail_coef, 1, 2)[:, :, :, None]).astype(
        jnp.bfloat16
    )
    stretch_states = jnp.einsum(
        "clhp,cln->chpn", tail_rows, write_state, preferred_element_type=jnp.float32
    )
    stretch_gates = (
        jnp.exp(decay_heads[:, :, -1]) * (last_ids == prior_ids).astype(jnp.float32)[:, None]
    )
    block_gate = jnp.ones((local_heads,), jnp.float32)
    block_state = jnp.zeros((local_heads, head_width, state_width), jnp.float32)
    block_state = stretch_gates[0][:, None, None] * block_state + stretch_states[0]
    block_gate = block_gate * stretch_gates[0]

    def compose(earlier, later):
        return (earlier[0] * later[0], later[0][:, None, None] * earlier[1] + later[1])

    identity_pair = (jnp.ones_like(block_gate), jnp.zeros_like(block_state))
    carried = prefix((block_gate, block_state), "seq", compose, identity_pair)
    incoming = carried[1]
    arriving = []
    arriving.append(incoming)
    arriving = jnp.stack(arriving)
    carry_mask = (stretch_ids == prior_ids[:, None]).astype(jnp.float32)
    carry_decay = jnp.exp(log_decay) * carry_mask[:, :, None]
    from_before = (
        jnp.einsum(
            "cln,chpn->clhp",
            read_state,
            arriving.astype(jnp.bfloat16),
            preferred_element_type=jnp.float32,
        )
        * carry_decay[:, :, :, None]
    )
    result = (
        within_stretch + from_before + skip_gain[None, None, :, None] * values.astype(jnp.float32)
    )
    ssm_rows = result.reshape(block_rows, local_width).astype(jnp.bfloat16)
    end_weight = ends_mask.astype(jnp.float32)
    has_end = jnp.sum(end_weight, axis=1)
    end_decay = jnp.sum(decay_heads * end_weight[:, None, :], axis=2)
    end_ids = jnp.sum(jnp.where(ends_mask, stretch_ids, 0), axis=1)
    keep_end = ((stretch_ids == end_ids[:, None]) & (has_end[:, None] > 0))[:, None, :]
    end_coef = (
        jnp.where(keep_end, jnp.exp(jnp.minimum(end_decay[:, :, None] - decay_heads, 0.0)), 0.0)
        * step_heads
    )
    end_rows = (values.astype(jnp.float32) * jnp.swapaxes(end_coef, 1, 2)[:, :, :, None]).astype(
        jnp.bfloat16
    )
    end_states = jnp.einsum(
        "clhp,cln->chpn", end_rows, write_state, preferred_element_type=jnp.float32
    )
    end_carry = (
        jnp.exp(end_decay) * ((end_ids == prior_ids) & (has_end > 0)).astype(jnp.float32)[:, None]
    )
    end_states = end_states + end_carry[:, :, None, None] * arriving
    final_block = jnp.sum(end_states, axis=0)[None]
    head_gates = gates_sum.astype(jnp.bfloat16)
    norm_slice = lax.dynamic_slice_in_dim(norm_gain, group_index * local_width, local_width)
    gated = ssm_rows.astype(jnp.float32) * jax.nn.silu(head_gates.astype(jnp.float32))
    squares = lax.psum(jnp.sum(gated * gated, axis=1), "head")
    scaled = gated * lax.rsqrt(squares / inner_width + epsilon)[:, None] * norm_slice[None, :]
    outgoing = scaled.astype(jnp.bfloat16)
    returned = lax.all_to_all(
        outgoing.reshape(groups, sub_rows, local_width),
        "head",
        split_axis=0,
        concat_axis=2,
        tiled=True,
    )
    gated_out = returned.reshape(sub_rows, inner_width)
    return (gated_out, final_block)


def solution(mesh):
    in_specs = (
        P(("seq", "head"), None),
        P("seq", "head"),
        P("seq", "head"),
        P("seq", "head"),
        P("seq", None),
        P(),
        P(),
        P("head"),
        P("head"),
        P("head"),
        P(),
        P(),
    )
    out_specs = (P(("seq", "head"), None), P("seq", "head", None, None))
    return jax.shard_map(
        on_device, mesh=mesh, in_specs=in_specs, out_specs=out_specs, check_vma=False
    )
```

```python
import jax
import jax.numpy as jnp
from jax import lax
from jax.experimental import pallas as pl
from jax.experimental.pallas import tpu as pltpu
from jax.sharding import PartitionSpec as P

STRETCH = 256


epsilon = 1e-05


def from_behind(block, axis, distance):
    devices = range(lax.axis_size(axis))
    route = [(i - distance, i) for i in devices if i - distance in devices]
    return lax.ppermute(block, axis, route)


def prefix(value, axis, join, neutral):
    place = lax.axis_index(axis)
    gathered = jax.tree.map(
        lambda a, kind: lax.all_gather(a.astype(kind), axis), value, (jnp.bfloat16, jnp.bfloat16)
    )
    state = jax.tree.map(lambda a, e: jnp.zeros_like(a) + jnp.asarray(e, a.dtype), value, neutral)

    def one(turn, state):
        return join(
            state,
            jax.tree.map(
                lambda a, own: lax.dynamic_index_in_dim(a, turn, 0, False).astype(own.dtype),
                gathered,
                value,
            ),
        )

    return lax.fori_loop(0, place, one, state)


def segments_at(positions, prompt_ends):
    counted = jnp.sum((prompt_ends[None, :] <= positions[:, None]).astype(jnp.int32), axis=1)
    return jnp.where(positions < 0, -1, counted)


MESH = pl.DeviceIdType.MESH
BF16 = jnp.bfloat16
F32 = jnp.float32


def rdma(src, dst, send_sem, recv_sem, seq, head):
    return pltpu.make_async_remote_copy(
        src_ref=src,
        dst_ref=dst,
        send_sem=send_sem,
        recv_sem=recv_sem,
        device_id=(seq, head),
        device_id_type=MESH,
    )


def layer_kernel(
    hidden_ref,
    values_ref,
    small_ref,
    gates_ref,
    taps_ref,
    bias_ref,
    heads_ref,
    norm_ref,
    lengths_ref,
    out_ref,
    final_ref,
    hid,
    wbuf,
    out_v,
    out_s,
    out_g,
    in_v,
    in_s,
    in_g,
    own,
    tile,
    tiles,
    local_sem,
    hid_send,
    hid_recv,
    w_send,
    w_recv,
    part_send,
    part_recv,
    tile_send,
    tile_recv,
    halo_out,
    halo_in,
    ext,
    conv,
    cum_ref,
    cum_rows,
    dt_rows,
    carry_ref,
    end_ref,
    y_ref,
    inc,
    local_out,
    gate_out,
    local_in,
    gate_in,
    gated,
    whole,
    halo_send,
    halo_recv,
    state_send,
    state_recv,
    turn_send,
    turn_recv,
):
    s = lax.axis_index("seq")
    h = lax.axis_index("head")
    z = lax.div(s, 2)
    x = lax.rem(s, 2)
    z_lo = lax.rem(z, 2)
    z_hi = lax.div(z, 2)
    beside = s + 1 - 2 * x
    partner = s + 2 - 4 * z_lo
    far = s + 4 - 8 * z_hi
    heads = [lax.rem(h + d, 4) for d in (1, 2, 3)]
    rows_w = values_ref.shape[0]
    rows_h = hidden_ref.shape[0]
    depth = 2 * rows_w
    width = values_ref.shape[1]
    narrow = small_ref.shape[1]

    barrier = pltpu.get_barrier_semaphore()
    for d in range(1, 8):
        pl.semaphore_signal(
            barrier, inc=1, device_id=(lax.rem(s + d, 8), h), device_id_type=MESH
        )
    for to in heads:
        pl.semaphore_signal(barrier, inc=1, device_id=(s, to), device_id_type=MESH)

    my_rows = pl.ds(pl.multiple_of(x * rows_w, 64), rows_w)
    my_tokens = pl.ds(pl.multiple_of(h * rows_h, 64), rows_h)
    cuts = (0, 2 * narrow, width)
    gate_cuts = (0, 2 * narrow, 4 * narrow, width)
    pieces = [(small_ref, 0, width, narrow)]
    pieces += [(values_ref, a, a, b - a) for a, b in zip(cuts, cuts[1:])]
    pieces += [
        (gates_ref, a, width + narrow + a, b - a) for a, b in zip(gate_cuts, gate_cuts[1:])
    ]
    sources = [ref.at[:, pl.ds(a, size)] for ref, a, _, size in pieces]
    windows = [pl.ds(at, size) for _, _, at, size in pieces]
    number = len(pieces)

    def columns(low, zh):
        return pl.ds(pl.multiple_of((low + 2 * zh) * depth, 128), depth)

    local = []
    for p in range(number):
        local.append(
            pltpu.make_async_copy(
                sources[p], wbuf.at[z_hi, my_rows, windows[p]], local_sem.at[p]
            )
        )
    for zh in range(2):
        local.append(
            pltpu.make_async_copy(
                hidden_ref.at[:, columns(z_lo, zh)],
                hid.at[0, zh, my_tokens],
                local_sem.at[number + zh],
            )
        )
    for c in local:
        c.start()
    pl.semaphore_wait(barrier, 10)

    to_far = [
        rdma(sources[p], wbuf.at[z_hi, my_rows, windows[p]], w_send.at[0, p], w_recv.at[0, p], far, h)
        for p in range(number)
    ]
    to_beside = [
        rdma(sources[p], wbuf.at[z_hi, my_rows, windows[p]], w_send.at[1, p], w_recv.at[1, p], beside, h)
        for p in range(number)
    ]
    passed = [
        rdma(
            wbuf.at[1 - z_hi, my_rows, windows[p]],
            wbuf.at[1 - z_hi, my_rows, windows[p]],
            w_send.at[2, p],
            w_recv.at[2, p],
            beside,
            h,
        )
        for p in range(number)
    ]
    hid_over = [
        rdma(
            hidden_ref.at[:, columns(1 - z_lo, zh)],
            hid.at[1, zh, my_tokens],
            hid_send.at[0, zh],
            hid_recv.at[0, zh],
            partner,
            h,
        )
        for zh in range(2)
    ]
    hid_own = [
        rdma(
            hidden_ref.at[:, columns(z_lo, zh)],
            hid.at[0, zh, my_tokens],
            hid_send.at[1 + d, zh],
            hid_recv.at[1 + d, zh],
            s,
            heads[d],
        )
        for zh in range(2)
        for d in range(3)
    ]
    hid_pass = [
        rdma(
            hid.at[1, zh, my_tokens],
            hid.at[1, zh, my_tokens],
            hid_send.at[4 + d, zh],
            hid_recv.at[4 + d, zh],
            s,
            heads[d],
        )
        for zh in range(2)
        for d in range(3)
    ]
    for c in hid_over:
        c.start()
    for p in range(3):
        to_far[p].start()
        to_beside[p].start()
    for c in hid_own:
        c.start()
    for zh in range(2):
        hid_over[zh].wait_recv()
        for d in range(3):
            hid_pass[3 * zh + d].start()

    def forward(p):
        to_far[p].wait_recv()
        passed[p].start()
        if p + 3 < number:
            to_far[p + 3].start()
            to_beside[p + 3].start()

    def landed(p):
        to_beside[p].wait_recv()
        passed[p].wait_recv()

    def product(which, window):
        return jnp.dot(
            hid[which, 0], wbuf[0, :, window], preferred_element_type=F32
        ) + jnp.dot(hid[which, 1], wbuf[1, :, window], preferred_element_type=F32)

    def span_of(p):
        _, a, _, size = pieces[p]
        return slice(a, a + size)

    def to_partner(p, out, arriving):
        landed(p)
        span = span_of(p)
        out[:, span] = product(1, windows[p]).astype(out.dtype)
        part = rdma(
            out.at[:, span], arriving.at[:, span], part_send.at[p], part_recv.at[p], partner, h
        )
        part.start()
        return part

    for p in range(3):
        forward(p)
    for c in local:
        c.wait()
    for c in hid_own:
        c.wait_recv()
    for c in hid_pass:
        c.wait_recv()
    part_s = to_partner(0, out_s, in_s)
    part_v = [to_partner(1, out_v, in_v)]
    forward(3)
    part_v.append(to_partner(2, out_v, in_v))
    small = product(0, windows[0])
    part_s.wait_recv()
    small = small + in_s[...]
    tile[...] = small.astype(BF16)
    tiles_out = [
        rdma(tile, tiles.at[h], tile_send.at[d], tile_recv.at[d], s, heads[d]) for d in range(3)
    ]
    for c in tiles_out:
        c.start()
    tiles[h] = tile[...]
    for p in (1, 2):
        own[:, span_of(p)] = product(0, windows[p])
    forward(4)

    rows = own.shape[0]
    start = s * rows
    count = lengths_ref.shape[0]
    ends = []
    for i in range(count):
        ends.append(lengths_ref[i] + (ends[i - 1] if i else 0))

    def segment(position):
        found = jnp.where(position < 0, -1, 0)
        for end in ends:
            found = found + jnp.where(end <= position, 1, 0)
        return found

    last_id = segment(start + rows - 1)
    prior_id = segment(start - 1)
    end_id = jnp.int32(-2)
    end_row = jnp.int32(-1)
    for i, end in enumerate(ends):
        inside = (end - 1 >= start) & (end - 1 < start + rows)
        end_id = jnp.where(inside, i, end_id)
        end_row = jnp.where(inside, end - 1 - start, end_row)

    order = lax.broadcasted_iota(jnp.int32, (rows, rows), 0)
    across = lax.broadcasted_iota(jnp.int32, (rows, rows), 1)
    lower = order >= across
    lower_ones = lower.astype(F32).astype(BF16)
    lane = lax.broadcasted_iota(jnp.int32, (rows, narrow), 1)
    token = lax.broadcasted_iota(jnp.int32, (rows, narrow), 0)
    ids = segment(start + token)

    def parts(value, number):
        taken = []
        for _ in range(number):
            piece = value.astype(BF16)
            taken.append(piece)
            value = value - piece.astype(F32)
        return taken

    share = narrow // 2
    step = jax.nn.softplus(small + heads_ref[0:1, :])
    rate = step * heads_ref[1:2, :]
    cum = jnp.zeros((rows, narrow), F32)
    for piece in parts(rate, 3):
        cum = cum - jnp.dot(lower_ones, piece, preferred_element_type=F32)
    cum_ref[...] = cum
    cum_rows[...] = cum.T
    dt_rows[...] = step.T
    head_row = lax.broadcasted_iota(jnp.int32, (narrow, width), 0) - share
    channel = lax.broadcasted_iota(jnp.int32, (narrow, width), 1)
    spread = (
        ((channel >= head_row * share) & (channel < head_row * share + share))
        .astype(F32)
        .astype(BF16)
    )

    def expand(value, number):
        total = None
        for piece in parts(value, number):
            term = jnp.dot(piece, spread, preferred_element_type=F32)
            total = term if total is None else total + term
        return total

    cum_last = cum[rows - 1 : rows, :]
    cum_end = jnp.sum(jnp.where(token == end_row, cum, 0.0), axis=0, keepdims=True)
    gate_row = jnp.where(last_id == prior_id, jnp.exp(cum_last), 0.0)
    end_gate = jnp.where(end_id == prior_id, jnp.exp(cum_end), 0.0)
    eight = lax.broadcasted_iota(jnp.int32, (8, narrow), 0)
    rows8 = jnp.where(
        eight == 0,
        gate_row,
        jnp.where(eight == 1, end_gate, jnp.where(eight == 2, heads_ref[2:3, :], 0.0)),
    )
    wide8 = expand(rows8, 3)
    gate_out[...] = wide8
    tail = jnp.where(ids == last_id, jnp.exp(jnp.minimum(cum_last - cum, 0.0)), 0.0) * step
    tail_wide = expand(tail, 2)
    end_ref[...] = expand(
        jnp.where(ids == end_id, jnp.exp(jnp.minimum(cum_end - cum, 0.0)), 0.0) * step, 2
    )
    carry_ref[...] = expand(jnp.where(ids == prior_id, jnp.exp(cum), 0.0), 2)

    forward(5)
    for c in part_v:
        c.wait_recv()
    pre = (own[...] + in_v[...].astype(F32)).astype(BF16)
    ext[8:, 0:width] = pre.astype(F32)
    halo_out[:, 0:width] = pre[rows - 16 :, :]
    for c in tiles_out:
        c.wait_recv()
    for half in range(2):
        first = tiles[2 * half].astype(F32)
        second = pltpu.roll(tiles[2 * half + 1].astype(F32), share, 1)
        both = jnp.where(lane < share, first, second)
        low = width + half * narrow
        ext[8:, low : low + narrow] = both
        halo_out[:, low : low + narrow] = both[rows - 16 :, :].astype(BF16)
    halo = rdma(
        halo_out, halo_in, halo_send.at[0], halo_recv.at[0], lax.rem(s + 1, 8), h
    )
    halo.start()

    part_g = [to_partner(3, out_g, in_g)]
    own[:, span_of(3)] = product(0, windows[3])

    halo.wait_recv()
    ext[0:8, :] = halo_in[8:16, :].astype(F32)
    inner = 4 * width
    same = [
        (segment(start + token - d) == ids).astype(F32) for d in range(3, 0, -1)
    ]
    chunks = (width + 2 * narrow) // narrow
    for j in range(chunks):
        low = j * narrow
        if low < width:
            from_lane = pl.ds(pl.multiple_of(h * width + low, 128), narrow)
        else:
            from_lane = pl.ds(inner + low - width, narrow)
        taps = taps_ref[:, from_lane]
        total = jnp.zeros((rows, narrow), F32) + bias_ref[:, from_lane]
        for tap in range(4):
            piece = ext[5 + tap : 5 + tap + rows, low : low + narrow] * taps[tap : tap + 1, :]
            total = total + (piece * same[tap] if tap < 3 else piece)
        conv[:, low : low + narrow] = jax.nn.silu(total).astype(BF16)

    values = conv[:, 0:width]
    write_turned = conv[:, width : width + narrow].astype(F32).T.astype(BF16)
    read_state = conv[:, width + narrow :]
    local_out[...] = jnp.dot(
        write_turned,
        (values.astype(F32) * tail_wide).astype(BF16),
        preferred_element_type=F32,
    ).astype(BF16)
    onward = []
    for d in range(3):
        to = lax.rem(s + d + 1, 8)
        onward.append(
            (
                rdma(local_out, local_in.at[d], state_send.at[0, d], state_recv.at[0, d], to, h),
                rdma(gate_out, gate_in.at[d], state_send.at[1, d], state_recv.at[1, d], to, h),
            )
        )
    for d in range(3):

        @pl.when(s + d + 1 < 8)
        def _(d=d):
            onward[d][0].start()
            onward[d][1].start()

    part_g.append(to_partner(4, out_g, in_g))
    own[:, span_of(4)] = product(0, windows[4])
    met = jnp.where(
        lower & (segment(start + order) == segment(start + across)),
        jnp.dot(read_state, write_turned, preferred_element_type=F32),
        0.0,
    )
    pairs = width // narrow
    for j in range(pairs):
        pair = conv[:, j * narrow : (j + 1) * narrow]
        halves = []
        for a in range(2):
            at = share + 2 * j + a
            decay = cum_ref[:, at : at + 1] - cum_rows[at : at + 1, :]
            scores = met * jnp.exp(jnp.minimum(decay, 0.0)) * dt_rows[at : at + 1, :]
            halves.append(jnp.dot(scores.astype(BF16), pair, preferred_element_type=F32))
        y_ref[:, j * narrow : (j + 1) * narrow] = jnp.where(lane < share, halves[0], halves[1])
    end_local = jnp.dot(
        write_turned,
        (values.astype(F32) * end_ref[...]).astype(BF16),
        preferred_element_type=F32,
    )

    part_g.append(to_partner(5, out_g, in_g))
    own[:, span_of(5)] = product(0, windows[5])

    inc[...] = jnp.zeros(inc.shape, F32)
    for d in range(3):

        @pl.when(s >= d + 1)
        def _(d=d):
            onward[d][0].wait_recv()
            onward[d][1].wait_recv()
            arrived = local_in[d].astype(F32)
            for e in range(d):
                arrived = arrived * gate_in[e, 0:1, :]
            inc[...] += arrived

    for c in part_g:
        c.wait_recv()
    for j in range(pairs):
        span = slice(j * narrow, (j + 1) * narrow)
        state = inc[:, span]
        final_ref[span, :] = (end_local[:, span] + wide8[1:2, span] * state).T
        before = jnp.dot(read_state, state.astype(BF16), preferred_element_type=F32)
        y = (
            y_ref[:, span]
            + before * carry_ref[:, span]
            + wide8[2:3, span] * conv[:, span].astype(F32)
        ).astype(BF16)
        gate = (own[:, span] + in_g[:, span].astype(F32)).astype(BF16).astype(F32)
        gated[:, span] = (y.astype(F32) * jax.nn.silu(gate)).astype(BF16)

    my_columns = pl.ds(pl.multiple_of(h * width, 128), width)
    turned = [
        rdma(
            gated.at[pl.ds(pl.multiple_of(heads[d] * rows_h, 64), rows_h)],
            whole.at[:, my_columns],
            turn_send.at[d],
            turn_recv.at[d],
            s,
            heads[d],
        )
        for d in range(3)
    ]
    for c in turned:
        c.start()
    keep = pltpu.make_async_copy(gated.at[my_tokens], whole.at[:, my_columns], local_sem.at[number + 2])
    keep.start()
    keep.wait()
    for c in turned:
        c.wait_recv()
    full = whole[...].astype(F32)
    mean = jnp.sum(full * full, axis=1, keepdims=True) / inner
    out_ref[...] = (full * lax.rsqrt(mean + epsilon) * norm_ref[...]).astype(BF16)

    for c in [*to_far, *to_beside, *passed, *hid_over, *hid_own, *hid_pass, *tiles_out, *turned]:
        c.wait_send()
    for c in [part_s, *part_v, *part_g, halo]:
        c.wait_send()
    for d in range(3):

        @pl.when(s + d + 1 < 8)
        def _(d=d):
            onward[d][0].wait_send()
            onward[d][1].wait_send()


def layer(
    hidden,
    w_values,
    w_gates,
    w_steps,
    w_states,
    conv_weight,
    conv_bias,
    step_bias,
    decay_rate,
    skip_gain,
    norm_gain,
    lengths,
):
    group = lax.axis_index("head")
    rows = hidden.shape[0] * 4
    width = w_values.shape[1]
    count = step_bias.shape[0]
    share = w_states.shape[1] // 4
    narrow = 2 * share
    part = lax.dynamic_slice_in_dim(w_states, group * share, share, 1)
    small = jnp.concatenate(
        [part, w_steps, jnp.zeros((w_steps.shape[0], narrow - share - count), BF16)],
        axis=1,
    )
    per_head = jnp.pad(
        jnp.stack([step_bias, decay_rate, skip_gain]), ((0, 5), (share, narrow - share - count))
    )
    depth = 2 * w_values.shape[0]
    channels = width + 2 * narrow
    vmem = pl.BlockSpec(memory_space=pltpu.VMEM)
    smem = pl.BlockSpec(memory_space=pltpu.SMEM)
    anywhere = pl.BlockSpec(memory_space=pl.ANY)
    dma = pltpu.SemaphoreType.DMA
    gated_out, final = pl.pallas_call(
        layer_kernel,
        out_shape=(
            jax.ShapeDtypeStruct(hidden.shape, BF16),
            jax.ShapeDtypeStruct((width, narrow), F32),
        ),
        in_specs=[anywhere] * 4 + [vmem] * 4 + [smem],
        out_specs=[vmem] * 2,
        scratch_shapes=[
            pltpu.VMEM((2, 2, rows, depth), BF16),
            pltpu.VMEM((2, depth, 2 * width + narrow), BF16),
            pltpu.VMEM((rows, width), BF16),
            pltpu.VMEM((rows, narrow), F32),
            pltpu.VMEM((rows, width), BF16),
            pltpu.VMEM((rows, width), BF16),
            pltpu.VMEM((rows, narrow), F32),
            pltpu.VMEM((rows, width), BF16),
            pltpu.VMEM((rows, width), F32),
            pltpu.VMEM((rows, narrow), BF16),
            pltpu.VMEM((4, rows, narrow), BF16),
            dma((9,)),
            dma((7, 2)),
            dma((7, 2)),
            dma((3, 6)),
            dma((3, 6)),
            dma((6,)),
            dma((6,)),
            dma((3,)),
            dma((3,)),
            pltpu.VMEM((16, channels), BF16),
            pltpu.VMEM((16, channels), BF16),
            pltpu.VMEM((8 + rows, channels), F32),
            pltpu.VMEM((rows, channels), BF16),
            pltpu.VMEM((rows, narrow), F32),
            pltpu.VMEM((narrow, rows), F32),
            pltpu.VMEM((narrow, rows), F32),
            pltpu.VMEM((rows, width), F32),
            pltpu.VMEM((rows, width), F32),
            pltpu.VMEM((rows, width), F32),
            pltpu.VMEM((narrow, width), F32),
            pltpu.VMEM((narrow, width), BF16),
            pltpu.VMEM((8, width), F32),
            pltpu.VMEM((3, narrow, width), BF16),
            pltpu.VMEM((3, 8, width), F32),
            pltpu.VMEM((rows, width), BF16),
            pltpu.VMEM(hidden.shape, BF16),
            dma((1,)),
            dma((1,)),
            dma((2, 3)),
            dma((2, 3)),
            dma((3,)),
            dma((3,)),
        ],
        compiler_params=pltpu.CompilerParams(
            collective_id=0, has_side_effects=True, vmem_limit_bytes=60 * 1024 * 1024
        ),
    )(
        hidden,
        w_values,
        small,
        w_gates,
        conv_weight,
        conv_bias[None, :],
        per_head,
        norm_gain[None, :],
        lengths,
    )
    return gated_out, final.reshape(1, count, width // count, narrow)


def on_device(
    hidden,
    w_values,
    w_gates,
    w_steps,
    w_states,
    conv_weight,
    conv_bias,
    step_bias,
    decay_rate,
    skip_gain,
    norm_gain,
    lengths,
):
    groups = lax.axis_size("head")
    if lax.axis_size("seq") == 8 and groups == 4:
        return layer(
            hidden,
            w_values,
            w_gates,
            w_steps,
            w_states,
            conv_weight,
            conv_bias,
            step_bias,
            decay_rate,
            skip_gain,
            norm_gain,
            lengths,
        )
    group_index = lax.axis_index("head")
    block_index = lax.axis_index("seq")
    local_width = w_values.shape[1]
    inner_width = local_width * groups
    local_heads = decay_rate.shape[0]
    head_width = local_width // local_heads
    state_width = w_states.shape[1] // 2
    conv_taps = conv_weight.shape[0]
    prompt_ends = jnp.cumsum(lengths)
    block_hidden = lax.all_gather(hidden, "head", axis=0, tiled=True)
    block_rows = block_hidden.shape[0]
    sub_rows = block_rows // groups

    def contract(piece):
        return jnp.dot(block_hidden, piece, preferred_element_type=jnp.float32)

    pieces = (
        lax.all_gather(w_values, "seq", axis=0, tiled=True),
        lax.all_gather(w_states, "seq", axis=0, tiled=True),
        lax.all_gather(w_steps, "seq", axis=0, tiled=True),
        lax.all_gather(w_gates, "seq", axis=0, tiled=True),
    )
    values_sum, states_sum, steps_sum, gates_sum = tuple((contract(piece) for piece in pieces))
    pre_rows = jnp.concatenate(
        [values_sum.astype(jnp.bfloat16), states_sum.astype(jnp.bfloat16)], axis=1
    )
    local_taps = jnp.concatenate(
        [
            lax.dynamic_slice_in_dim(conv_weight, group_index * local_width, local_width, 1),
            conv_weight[:, inner_width:],
        ],
        axis=1,
    )
    local_bias = jnp.concatenate(
        [
            lax.dynamic_slice_in_dim(conv_bias, group_index * local_width, local_width, 0),
            conv_bias[inner_width:],
        ],
        axis=0,
    )
    block_start = block_index * block_rows
    rim_rows = pre_rows[block_rows - (conv_taps - 1) :]
    prior_rim = from_behind(rim_rows, "seq", 1)
    extended = jnp.concatenate([prior_rim, pre_rows], axis=0)
    ext_positions = (
        block_start - (conv_taps - 1) + jnp.arange(block_rows + conv_taps - 1, dtype=jnp.int32)
    )
    ext_ids = segments_at(ext_positions, prompt_ends)
    own_ids = ext_ids[conv_taps - 1 :]
    filtered = jnp.zeros(pre_rows.shape, jnp.float32) + local_bias[None, :]
    for offset in range(conv_taps):
        matches = (ext_ids[offset : offset + block_rows] == own_ids).astype(jnp.float32)
        filtered = (
            filtered
            + local_taps[offset][None, :]
            * extended[offset : offset + block_rows].astype(jnp.float32)
            * matches[:, None]
        )
    conv_out = jax.nn.silu(filtered).astype(jnp.bfloat16)
    head_values = conv_out[:, :local_width]
    both_states = conv_out[:, local_width:]
    stretch_rows = STRETCH
    stretches = block_rows // stretch_rows
    positions = block_start + jnp.arange(block_rows, dtype=jnp.int32)
    segment_ids = segments_at(positions, prompt_ends)
    next_ids = segments_at(positions + 1, prompt_ends)
    before_ids = segments_at(positions - 1, prompt_ends)
    stretch_ids = segment_ids.reshape(stretches, stretch_rows)
    prior_ids = before_ids.reshape(stretches, stretch_rows)[:, 0]
    ends_mask = (segment_ids != next_ids).reshape(stretches, stretch_rows)
    step_sizes = jax.nn.softplus(steps_sum + step_bias[None, :])
    decay_steps = step_sizes * decay_rate[None, :]
    log_decay = -jnp.cumsum(decay_steps.reshape(stretches, stretch_rows, local_heads), axis=1)
    decay_heads = jnp.swapaxes(log_decay, 1, 2)
    step_heads = jnp.swapaxes(step_sizes.reshape(stretches, stretch_rows, local_heads), 1, 2)
    values = head_values.reshape(stretches, stretch_rows, local_heads, head_width)
    write_state = both_states[:, :state_width].reshape(stretches, stretch_rows, state_width)
    read_state = both_states[:, state_width:].reshape(stretches, stretch_rows, state_width)
    intersection = jnp.einsum(
        "ctn,csn->cts", read_state, write_state, preferred_element_type=jnp.float32
    )
    token_order = jnp.arange(stretch_rows, dtype=jnp.int32)
    causal = token_order[:, None] >= token_order[None, :]
    allowed = causal[None] & (stretch_ids[:, :, None] == stretch_ids[:, None, :])
    spread = decay_heads[:, :, :, None] - decay_heads[:, :, None, :]
    weights = (
        jnp.where(allowed[:, None], jnp.exp(jnp.minimum(spread, 0.0)), 0.0)
        * step_heads[:, :, None, :]
    )
    scores = (intersection[:, None] * weights).astype(jnp.bfloat16)
    within_stretch = jnp.einsum(
        "chts,cshp->cthp", scores, values, preferred_element_type=jnp.float32
    )
    last_ids = stretch_ids[:, -1]
    tail_decay = decay_heads[:, :, -1:]
    keep_tail = (stretch_ids == last_ids[:, None])[:, None, :]
    tail_coef = (
        jnp.where(keep_tail, jnp.exp(jnp.minimum(tail_decay - decay_heads, 0.0)), 0.0) * step_heads
    )
    tail_rows = (values.astype(jnp.float32) * jnp.swapaxes(tail_coef, 1, 2)[:, :, :, None]).astype(
        jnp.bfloat16
    )
    stretch_states = jnp.einsum(
        "clhp,cln->chpn", tail_rows, write_state, preferred_element_type=jnp.float32
    )
    stretch_gates = (
        jnp.exp(decay_heads[:, :, -1]) * (last_ids == prior_ids).astype(jnp.float32)[:, None]
    )
    block_gate = jnp.ones((local_heads,), jnp.float32)
    block_state = jnp.zeros((local_heads, head_width, state_width), jnp.float32)
    block_state = stretch_gates[0][:, None, None] * block_state + stretch_states[0]
    block_gate = block_gate * stretch_gates[0]

    def compose(earlier, later):
        return (earlier[0] * later[0], later[0][:, None, None] * earlier[1] + later[1])

    identity_pair = (jnp.ones_like(block_gate), jnp.zeros_like(block_state))
    carried = prefix((block_gate, block_state), "seq", compose, identity_pair)
    incoming = carried[1]
    arriving = []
    arriving.append(incoming)
    arriving = jnp.stack(arriving)
    carry_mask = (stretch_ids == prior_ids[:, None]).astype(jnp.float32)
    carry_decay = jnp.exp(log_decay) * carry_mask[:, :, None]
    from_before = (
        jnp.einsum(
            "cln,chpn->clhp",
            read_state,
            arriving.astype(jnp.bfloat16),
            preferred_element_type=jnp.float32,
        )
        * carry_decay[:, :, :, None]
    )
    result = (
        within_stretch + from_before + skip_gain[None, None, :, None] * values.astype(jnp.float32)
    )
    ssm_rows = result.reshape(block_rows, local_width).astype(jnp.bfloat16)
    end_weight = ends_mask.astype(jnp.float32)
    has_end = jnp.sum(end_weight, axis=1)
    end_decay = jnp.sum(decay_heads * end_weight[:, None, :], axis=2)
    end_ids = jnp.sum(jnp.where(ends_mask, stretch_ids, 0), axis=1)
    keep_end = ((stretch_ids == end_ids[:, None]) & (has_end[:, None] > 0))[:, None, :]
    end_coef = (
        jnp.where(keep_end, jnp.exp(jnp.minimum(end_decay[:, :, None] - decay_heads, 0.0)), 0.0)
        * step_heads
    )
    end_rows = (values.astype(jnp.float32) * jnp.swapaxes(end_coef, 1, 2)[:, :, :, None]).astype(
        jnp.bfloat16
    )
    end_states = jnp.einsum(
        "clhp,cln->chpn", end_rows, write_state, preferred_element_type=jnp.float32
    )
    end_carry = (
        jnp.exp(end_decay) * ((end_ids == prior_ids) & (has_end > 0)).astype(jnp.float32)[:, None]
    )
    end_states = end_states + end_carry[:, :, None, None] * arriving
    final_block = jnp.sum(end_states, axis=0)[None]
    head_gates = gates_sum.astype(jnp.bfloat16)
    norm_slice = lax.dynamic_slice_in_dim(norm_gain, group_index * local_width, local_width)
    gated = ssm_rows.astype(jnp.float32) * jax.nn.silu(head_gates.astype(jnp.float32))
    squares = lax.psum(jnp.sum(gated * gated, axis=1), "head")
    scaled = gated * lax.rsqrt(squares / inner_width + epsilon)[:, None] * norm_slice[None, :]
    outgoing = scaled.astype(jnp.bfloat16)
    returned = lax.all_to_all(
        outgoing.reshape(groups, sub_rows, local_width),
        "head",
        split_axis=0,
        concat_axis=2,
        tiled=True,
    )
    gated_out = returned.reshape(sub_rows, inner_width)
    return (gated_out, final_block)


def solution(mesh):
    in_specs = (
        P(("seq", "head"), None),
        P("seq", "head"),
        P("seq", "head"),
        P("seq", "head"),
        P("seq", None),
        P(),
        P(),
        P("head"),
        P("head"),
        P("head"),
        P(),
        P(),
    )
    out_specs = (P(("seq", "head"), None), P("seq", "head", None, None))
    return jax.shard_map(
        on_device, mesh=mesh, in_specs=in_specs, out_specs=out_specs, check_vma=False
    )
```

```python
import jax
import jax.numpy as jnp
from jax import lax
from jax.experimental import pallas as pl
from jax.experimental.pallas import tpu as pltpu
from jax.sharding import PartitionSpec as P

STRETCH = 256


epsilon = 1e-05


def from_behind(block, axis, distance):
    devices = range(lax.axis_size(axis))
    route = [(i - distance, i) for i in devices if i - distance in devices]
    return lax.ppermute(block, axis, route)


def prefix(value, axis, join, neutral):
    place = lax.axis_index(axis)
    gathered = jax.tree.map(
        lambda a, kind: lax.all_gather(a.astype(kind), axis), value, (jnp.bfloat16, jnp.bfloat16)
    )
    state = jax.tree.map(lambda a, e: jnp.zeros_like(a) + jnp.asarray(e, a.dtype), value, neutral)

    def one(turn, state):
        return join(
            state,
            jax.tree.map(
                lambda a, own: lax.dynamic_index_in_dim(a, turn, 0, False).astype(own.dtype),
                gathered,
                value,
            ),
        )

    return lax.fori_loop(0, place, one, state)


def segments_at(positions, prompt_ends):
    counted = jnp.sum((prompt_ends[None, :] <= positions[:, None]).astype(jnp.int32), axis=1)
    return jnp.where(positions < 0, -1, counted)


MESH = pl.DeviceIdType.MESH
BF16 = jnp.bfloat16
F32 = jnp.float32


def rdma(src, dst, send_sem, recv_sem, seq, head):
    return pltpu.make_async_remote_copy(
        src_ref=src,
        dst_ref=dst,
        send_sem=send_sem,
        recv_sem=recv_sem,
        device_id=(seq, head),
        device_id_type=MESH,
    )


def layer_kernel(
    hidden_ref,
    values_ref,
    gates_ref,
    states_ref,
    steps_ref,
    channel_ref,
    bias_ref,
    decay_ref,
    skip_ref,
    lengths_ref,
    out_ref,
    final_ref,
    hid,
    wbuf,
    out_v,
    out_s,
    out_g,
    in_v,
    in_s,
    in_g,
    own,
    tile,
    tiles,
    local_sem,
    hid_send,
    hid_recv,
    w_send,
    w_recv,
    part_send,
    part_recv,
    tile_send,
    tile_recv,
    halo_out,
    halo_in,
    ext,
    conv,
    cum_ref,
    cum_rows,
    dt_rows,
    carry_ref,
    end_ref,
    y_ref,
    inc,
    local_out,
    gate_out,
    local_in,
    gate_in,
    gated,
    whole,
    halo_send,
    halo_recv,
    state_send,
    state_recv,
    turn_send,
    turn_recv,
    small_ref,
    local_f32,
):
    s = lax.axis_index("seq")
    h = lax.axis_index("head")
    z = lax.div(s, 2)
    x = lax.rem(s, 2)
    z_lo = lax.rem(z, 2)
    z_hi = lax.div(z, 2)
    beside = s + 1 - 2 * x
    partner = s + 2 - 4 * z_lo
    far = s + 4 - 8 * z_hi
    heads = [lax.rem(h + d, 4) for d in (1, 2, 3)]
    rows_w = values_ref.shape[0]
    rows_h = hidden_ref.shape[0]
    depth = 2 * rows_w
    width = values_ref.shape[1]
    narrow = small_ref.shape[1]
    count_heads = steps_ref.shape[0]

    share = narrow // 2
    barrier = pltpu.get_barrier_semaphore()
    for d in range(1, 8):
        pl.semaphore_signal(
            barrier, inc=1, device_id=(lax.rem(s + d, 8), h), device_id_type=MESH
        )
    for to in heads:
        pl.semaphore_signal(barrier, inc=1, device_id=(s, to), device_id_type=MESH)

    wide_states = states_ref[
        :, pl.ds(pl.multiple_of(lax.div(h, 2) * narrow, 128), narrow)
    ].astype(F32)
    turned_states = pltpu.roll(wide_states, share, 1)
    place = (
        lax.broadcasted_iota(jnp.int32, (count_heads, narrow), 1)
        == lax.broadcasted_iota(jnp.int32, (count_heads, narrow), 0) + share
    )
    step_columns = lax.dot_general(
        steps_ref[...],
        place.astype(F32).astype(BF16),
        (((0,), (0,)), ((), ())),
        preferred_element_type=F32,
    )
    small_ref[...] = jnp.where(
        lax.broadcasted_iota(jnp.int32, small_ref.shape, 1) < share,
        jnp.where(lax.rem(h, 2) == 1, turned_states, wide_states),
        step_columns,
    ).astype(BF16)

    my_rows = pl.ds(pl.multiple_of(x * rows_w, 64), rows_w)
    my_tokens = pl.ds(pl.multiple_of(h * rows_h, 64), rows_h)
    cuts = (0, 2 * narrow, width)
    gate_cuts = (0, 2 * narrow, 4 * narrow, width)
    pieces = [(small_ref, 0, width, narrow)]
    pieces += [(values_ref, a, a, b - a) for a, b in zip(cuts, cuts[1:])]
    pieces += [
        (gates_ref, a, width + narrow + a, b - a) for a, b in zip(gate_cuts, gate_cuts[1:])
    ]
    sources = [ref.at[:, pl.ds(a, size)] for ref, a, _, size in pieces]
    windows = [pl.ds(at, size) for _, _, at, size in pieces]
    number = len(pieces)

    def columns(low, zh):
        return pl.ds(pl.multiple_of((low + 2 * zh) * depth, 128), depth)

    local = []
    for p in range(number):
        local.append(
            pltpu.make_async_copy(
                sources[p], wbuf.at[z_hi, my_rows, windows[p]], local_sem.at[p]
            )
        )
    for zh in range(2):
        local.append(
            pltpu.make_async_copy(
                hidden_ref.at[:, columns(z_lo, zh)],
                hid.at[0, zh, my_tokens],
                local_sem.at[number + zh],
            )
        )
    for c in local:
        c.start()
    pl.semaphore_wait(barrier, 10)

    to_far = [
        rdma(sources[p], wbuf.at[z_hi, my_rows, windows[p]], w_send.at[0, p], w_recv.at[0, p], far, h)
        for p in range(number)
    ]
    to_beside = [
        rdma(sources[p], wbuf.at[z_hi, my_rows, windows[p]], w_send.at[1, p], w_recv.at[1, p], beside, h)
        for p in range(number)
    ]
    passed = [
        rdma(
            wbuf.at[1 - z_hi, my_rows, windows[p]],
            wbuf.at[1 - z_hi, my_rows, windows[p]],
            w_send.at[2, p],
            w_recv.at[2, p],
            beside,
            h,
        )
        for p in range(number)
    ]
    hid_over = [
        rdma(
            hidden_ref.at[:, columns(1 - z_lo, zh)],
            hid.at[1, zh, my_tokens],
            hid_send.at[0, zh],
            hid_recv.at[0, zh],
            partner,
            h,
        )
        for zh in range(2)
    ]
    hid_own = [
        rdma(
            hidden_ref.at[:, columns(z_lo, zh)],
            hid.at[0, zh, my_tokens],
            hid_send.at[1 + d, zh],
            hid_recv.at[1 + d, zh],
            s,
            heads[d],
        )
        for zh in range(2)
        for d in range(3)
    ]
    hid_pass = [
        rdma(
            hid.at[1, zh, my_tokens],
            hid.at[1, zh, my_tokens],
            hid_send.at[4 + d, zh],
            hid_recv.at[4 + d, zh],
            s,
            heads[d],
        )
        for zh in range(2)
        for d in range(3)
    ]
    for c in hid_over:
        c.start()
    for p in range(3):
        to_far[p].start()
        to_beside[p].start()
    for c in hid_own:
        c.start()
    for zh in range(2):
        hid_over[zh].wait_recv()
        for d in range(3):
            hid_pass[3 * zh + d].start()

    def forward(p):
        to_far[p].wait_recv()
        passed[p].start()
        if p + 3 < number:
            to_far[p + 3].start()
            to_beside[p + 3].start()

    def landed(p):
        to_beside[p].wait_recv()
        passed[p].wait_recv()

    def product(which, window):
        return jnp.dot(
            hid[which, 0], wbuf[0, :, window], preferred_element_type=F32
        ) + jnp.dot(hid[which, 1], wbuf[1, :, window], preferred_element_type=F32)

    def span_of(p):
        _, a, _, size = pieces[p]
        return slice(a, a + size)

    def to_partner(p, out, arriving):
        landed(p)
        span = span_of(p)
        out[:, span] = product(1, windows[p]).astype(out.dtype)
        part = rdma(
            out.at[:, span], arriving.at[:, span], part_send.at[p], part_recv.at[p], partner, h
        )
        part.start()
        return part

    for p in range(3):
        forward(p)
    for c in local:
        c.wait()
    for c in hid_own:
        c.wait_recv()
    for c in hid_pass:
        c.wait_recv()
    part_s = to_partner(0, out_s, in_s)
    part_v = [to_partner(1, out_v, in_v)]
    forward(3)
    part_v.append(to_partner(2, out_v, in_v))
    small = product(0, windows[0])
    part_s.wait_recv()
    small = small + in_s[...].astype(F32)
    tile[...] = small.astype(BF16)
    tiles_out = [
        rdma(tile, tiles.at[h], tile_send.at[d], tile_recv.at[d], s, heads[d]) for d in range(3)
    ]
    for c in tiles_out:
        c.start()
    tiles[h] = tile[...]
    for p in (1, 2):
        own[:, span_of(p)] = product(0, windows[p])
    forward(4)

    rows = own.shape[0]
    start = s * rows
    count = lengths_ref.shape[0]
    ends = []
    for i in range(count):
        ends.append(lengths_ref[i] + (ends[i - 1] if i else 0))

    def segment(position):
        found = jnp.where(position < 0, -1, 0)
        for end in ends:
            found = found + jnp.where(end <= position, 1, 0)
        return found

    last_id = segment(start + rows - 1)
    prior_id = segment(start - 1)
    end_id = jnp.int32(-2)
    end_row = jnp.int32(-1)
    for i, end in enumerate(ends):
        inside = (end - 1 >= start) & (end - 1 < start + rows)
        end_id = jnp.where(inside, i, end_id)
        end_row = jnp.where(inside, end - 1 - start, end_row)

    order = lax.broadcasted_iota(jnp.int32, (rows, rows), 0)
    across = lax.broadcasted_iota(jnp.int32, (rows, rows), 1)
    lower = order >= across
    lower_ones = lower.astype(F32).astype(BF16)
    lane = lax.broadcasted_iota(jnp.int32, (rows, narrow), 1)
    token = lax.broadcasted_iota(jnp.int32, (rows, narrow), 0)
    ids = segment(start + token)

    def parts(value, number):
        taken = []
        for _ in range(number):
            piece = value.astype(BF16)
            taken.append(piece)
            value = value - piece.astype(F32)
        return taken

    head_lane = lax.broadcasted_iota(jnp.int32, (8, narrow), 1) - share

    def over_lanes(ref):
        row = jnp.zeros((8, narrow), F32)
        for i in range(count_heads):
            row = jnp.where(head_lane == i, ref[i], row)
        return row

    step = jax.nn.softplus(small + over_lanes(bias_ref)[0:1, :])
    rate = step * over_lanes(decay_ref)[0:1, :]
    cum = jnp.zeros((rows, narrow), F32)
    for piece in parts(rate, 3):
        cum = cum - jnp.dot(lower_ones, piece, preferred_element_type=F32)
    cum_ref[...] = cum
    cum_rows[...] = cum.T
    dt_rows[...] = step.T
    head_row = lax.broadcasted_iota(jnp.int32, (narrow, width), 0) - share
    channel = lax.broadcasted_iota(jnp.int32, (narrow, width), 1)
    spread = (
        ((channel >= head_row * share) & (channel < head_row * share + share))
        .astype(F32)
        .astype(BF16)
    )

    def expand(value, number):
        total = None
        for piece in parts(value, number):
            term = jnp.dot(piece, spread, preferred_element_type=F32)
            total = term if total is None else total + term
        return total

    cum_last = cum[rows - 1 : rows, :]
    cum_end = jnp.sum(jnp.where(token == end_row, cum, 0.0), axis=0, keepdims=True)
    gate_row = jnp.where(last_id == prior_id, jnp.exp(cum_last), 0.0)
    end_gate = jnp.where(end_id == prior_id, jnp.exp(cum_end), 0.0)
    eight = lax.broadcasted_iota(jnp.int32, (8, narrow), 0)
    rows8 = jnp.where(
        eight == 0,
        gate_row,
        jnp.where(eight == 1, end_gate, jnp.where(eight == 2, over_lanes(skip_ref), 0.0)),
    )
    wide8 = expand(rows8, 3)
    gate_out[...] = wide8
    tail = jnp.where(ids == last_id, jnp.exp(jnp.minimum(cum_last - cum, 0.0)), 0.0) * step
    tail_wide = expand(tail, 2)
    end_ref[...] = expand(
        jnp.where(ids == end_id, jnp.exp(jnp.minimum(cum_end - cum, 0.0)), 0.0) * step, 2
    )
    carry_ref[...] = expand(jnp.where(ids == prior_id, jnp.exp(cum), 0.0), 2)

    forward(5)
    for c in part_v:
        c.wait_recv()
    pre = (own[...] + in_v[...].astype(F32)).astype(BF16)
    ext[8:, 0:width] = pre.astype(F32)
    halo_out[:, 0:width] = pre[rows - 16 :, :]
    for c in tiles_out:
        c.wait_recv()
    for half in range(2):
        first = tiles[2 * half].astype(F32)
        second = pltpu.roll(tiles[2 * half + 1].astype(F32), share, 1)
        both = jnp.where(lane < share, first, second)
        low = width + half * narrow
        ext[8:, low : low + narrow] = both
        halo_out[:, low : low + narrow] = both[rows - 16 :, :].astype(BF16)
    halo = rdma(
        halo_out, halo_in, halo_send.at[0], halo_recv.at[0], lax.rem(s + 1, 8), h
    )
    halo.start()

    part_g = [to_partner(3, out_g, in_g)]
    own[:, span_of(3)] = product(0, windows[3])

    halo.wait_recv()
    ext[0:8, :] = halo_in[8:16, :].astype(F32)
    inner = 4 * width
    same = [
        (segment(start + token - d) == ids).astype(F32) for d in range(3, 0, -1)
    ]
    chunks = (width + 2 * narrow) // narrow
    for j in range(chunks):
        low = j * narrow
        if low < width:
            from_lane = pl.ds(pl.multiple_of(h * width + low, 128), narrow)
        else:
            from_lane = pl.ds(inner + low - width, narrow)
        taps = channel_ref[:, from_lane]
        total = jnp.zeros((rows, narrow), F32) + taps[4:5, :]
        for tap in range(4):
            piece = ext[5 + tap : 5 + tap + rows, low : low + narrow] * taps[tap : tap + 1, :]
            total = total + (piece * same[tap] if tap < 3 else piece)
        conv[:, low : low + narrow] = jax.nn.silu(total).astype(BF16)

    values = conv[:, 0:width]
    write_turned = conv[:, width : width + narrow].astype(F32).T.astype(BF16)
    read_state = conv[:, width + narrow :]
    local = jnp.dot(
        write_turned,
        (values.astype(F32) * tail_wide).astype(BF16),
        preferred_element_type=F32,
    )
    local_f32[...] = local
    local_out[0] = local.astype(BF16)
    next_one = (
        rdma(
            local_out.at[0], local_in.at[0], state_send.at[0], state_recv.at[0], lax.rem(s + 1, 8), h
        ),
        rdma(gate_out, gate_in, state_send.at[1], state_recv.at[1], lax.rem(s + 1, 8), h),
    )
    next_two = rdma(
        local_out.at[1], local_in.at[1], state_send.at[2], state_recv.at[2], lax.rem(s + 2, 8), h
    )

    @pl.when(s < 7)
    def _():
        for c in next_one:
            c.start()

    part_g.append(to_partner(4, out_g, in_g))
    own[:, span_of(4)] = product(0, windows[4])
    inc[...] = jnp.zeros(inc.shape, F32)

    @pl.when(s > 0)
    def _():
        for c in next_one:
            c.wait_recv()
        inc[...] = local_in[0].astype(F32)

    @pl.when(s < 6)
    def _():
        local_out[1] = (local_f32[...] + wide8[0:1, :] * inc[...]).astype(BF16)
        next_two.start()

    met = jnp.where(
        lower & (segment(start + order) == segment(start + across)),
        jnp.dot(read_state, write_turned, preferred_element_type=F32),
        0.0,
    )
    pairs = width // narrow
    for j in range(pairs):
        pair = conv[:, j * narrow : (j + 1) * narrow]
        halves = []
        for a in range(2):
            at = share + 2 * j + a
            decay = cum_ref[:, at : at + 1] - cum_rows[at : at + 1, :]
            scores = met * jnp.exp(jnp.minimum(decay, 0.0)) * dt_rows[at : at + 1, :]
            halves.append(jnp.dot(scores.astype(BF16), pair, preferred_element_type=F32))
        y_ref[:, j * narrow : (j + 1) * narrow] = jnp.where(lane < share, halves[0], halves[1])
    end_local = jnp.dot(
        write_turned,
        (values.astype(F32) * end_ref[...]).astype(BF16),
        preferred_element_type=F32,
    )

    part_g.append(to_partner(5, out_g, in_g))
    own[:, span_of(5)] = product(0, windows[5])

    @pl.when(s > 1)
    def _():
        next_two.wait_recv()
        inc[...] += gate_in[0:1, :] * local_in[1].astype(F32)

    for c in part_g:
        c.wait_recv()
    for j in range(pairs):
        span = slice(j * narrow, (j + 1) * narrow)
        state = inc[:, span]
        final_ref[span, :] = (end_local[:, span] + wide8[1:2, span] * state).T
        before = jnp.dot(read_state, state.astype(BF16), preferred_element_type=F32)
        y = (
            y_ref[:, span]
            + before * carry_ref[:, span]
            + wide8[2:3, span] * conv[:, span].astype(F32)
        ).astype(BF16)
        gate = (own[:, span] + in_g[:, span].astype(F32)).astype(BF16).astype(F32)
        gated[:, span] = (y.astype(F32) * jax.nn.silu(gate)).astype(BF16)

    my_columns = pl.ds(pl.multiple_of(h * width, 128), width)
    turned = [
        rdma(
            gated.at[pl.ds(pl.multiple_of(heads[d] * rows_h, 64), rows_h)],
            whole.at[:, my_columns],
            turn_send.at[d],
            turn_recv.at[d],
            s,
            heads[d],
        )
        for d in range(3)
    ]
    for c in turned:
        c.start()
    keep = pltpu.make_async_copy(gated.at[my_tokens], whole.at[:, my_columns], local_sem.at[number + 2])
    keep.start()
    keep.wait()
    for c in turned:
        c.wait_recv()
    full = whole[...].astype(F32)
    mean = jnp.sum(full * full, axis=1, keepdims=True) / inner
    out_ref[...] = (full * lax.rsqrt(mean + epsilon) * channel_ref[5:6, 0:inner]).astype(BF16)

    for c in [*to_far, *to_beside, *passed, *hid_over, *hid_own, *hid_pass, *tiles_out, *turned]:
        c.wait_send()
    for c in [part_s, *part_v, *part_g, halo]:
        c.wait_send()

    @pl.when(s < 7)
    def _():
        for c in next_one:
            c.wait_send()

    @pl.when(s < 6)
    def _():
        next_two.wait_send()


def layer(
    hidden,
    w_values,
    w_gates,
    w_steps,
    w_states,
    conv_weight,
    conv_bias,
    step_bias,
    decay_rate,
    skip_gain,
    norm_gain,
    lengths,
):
    rows = hidden.shape[0] * 4
    width = w_values.shape[1]
    count = step_bias.shape[0]
    narrow = w_states.shape[1] // 2
    inner = norm_gain.shape[0]
    per_channel = jnp.concatenate(
        [
            conv_weight,
            conv_bias[None, :],
            jnp.pad(norm_gain, (0, conv_bias.shape[0] - inner))[None, :],
            jnp.zeros((2, conv_bias.shape[0]), F32),
        ],
        axis=0,
    )
    depth = 2 * w_values.shape[0]
    channels = width + 2 * narrow
    vmem = pl.BlockSpec(memory_space=pltpu.VMEM)
    smem = pl.BlockSpec(memory_space=pltpu.SMEM)
    anywhere = pl.BlockSpec(memory_space=pl.ANY)
    dma = pltpu.SemaphoreType.DMA
    gated_out, final = pl.pallas_call(
        layer_kernel,
        out_shape=(
            jax.ShapeDtypeStruct(hidden.shape, BF16),
            jax.ShapeDtypeStruct((width, narrow), F32),
        ),
        in_specs=[anywhere] * 3 + [vmem] * 3 + [smem] * 4,
        out_specs=[vmem] * 2,
        scratch_shapes=[
            pltpu.VMEM((2, 2, rows, depth), BF16),
            pltpu.VMEM((2, depth, 2 * width + narrow), BF16),
            pltpu.VMEM((rows, width), BF16),
            pltpu.VMEM((rows, narrow), BF16),
            pltpu.VMEM((rows, width), BF16),
            pltpu.VMEM((rows, width), BF16),
            pltpu.VMEM((rows, narrow), BF16),
            pltpu.VMEM((rows, width), BF16),
            pltpu.VMEM((rows, width), F32),
            pltpu.VMEM((rows, narrow), BF16),
            pltpu.VMEM((4, rows, narrow), BF16),
            dma((9,)),
            dma((7, 2)),
            dma((7, 2)),
            dma((3, 6)),
            dma((3, 6)),
            dma((6,)),
            dma((6,)),
            dma((3,)),
            dma((3,)),
            pltpu.VMEM((16, channels), BF16),
            pltpu.VMEM((16, channels), BF16),
            pltpu.VMEM((8 + rows, channels), F32),
            pltpu.VMEM((rows, channels), BF16),
            pltpu.VMEM((rows, narrow), F32),
            pltpu.VMEM((narrow, rows), F32),
            pltpu.VMEM((narrow, rows), F32),
            pltpu.VMEM((rows, width), F32),
            pltpu.VMEM((rows, width), F32),
            pltpu.VMEM((rows, width), F32),
            pltpu.VMEM((narrow, width), F32),
            pltpu.VMEM((2, narrow, width), BF16),
            pltpu.VMEM((8, width), F32),
            pltpu.VMEM((2, narrow, width), BF16),
            pltpu.VMEM((8, width), F32),
            pltpu.VMEM((rows, width), BF16),
            pltpu.VMEM(hidden.shape, BF16),
            dma((1,)),
            dma((1,)),
            dma((3,)),
            dma((3,)),
            dma((3,)),
            dma((3,)),
            pltpu.VMEM((w_values.shape[0], narrow), BF16),
            pltpu.VMEM((narrow, width), F32),
        ],
        compiler_params=pltpu.CompilerParams(
            collective_id=0, has_side_effects=True, vmem_limit_bytes=60 * 1024 * 1024
        ),
    )(
        hidden,
        w_values,
        w_gates,
        w_states,
        w_steps.T,
        per_channel,
        step_bias,
        decay_rate,
        skip_gain,
        lengths,
    )
    return gated_out, final.reshape(1, count, width // count, narrow)


def on_device(
    hidden,
    w_values,
    w_gates,
    w_steps,
    w_states,
    conv_weight,
    conv_bias,
    step_bias,
    decay_rate,
    skip_gain,
    norm_gain,
    lengths,
):
    groups = lax.axis_size("head")
    if lax.axis_size("seq") == 8 and groups == 4:
        return layer(
            hidden,
            w_values,
            w_gates,
            w_steps,
            w_states,
            conv_weight,
            conv_bias,
            step_bias,
            decay_rate,
            skip_gain,
            norm_gain,
            lengths,
        )
    group_index = lax.axis_index("head")
    block_index = lax.axis_index("seq")
    local_width = w_values.shape[1]
    inner_width = local_width * groups
    local_heads = decay_rate.shape[0]
    head_width = local_width // local_heads
    state_width = w_states.shape[1] // 2
    conv_taps = conv_weight.shape[0]
    prompt_ends = jnp.cumsum(lengths)
    block_hidden = lax.all_gather(hidden, "head", axis=0, tiled=True)
    block_rows = block_hidden.shape[0]
    sub_rows = block_rows // groups

    def contract(piece):
        return jnp.dot(block_hidden, piece, preferred_element_type=jnp.float32)

    pieces = (
        lax.all_gather(w_values, "seq", axis=0, tiled=True),
        lax.all_gather(w_states, "seq", axis=0, tiled=True),
        lax.all_gather(w_steps, "seq", axis=0, tiled=True),
        lax.all_gather(w_gates, "seq", axis=0, tiled=True),
    )
    values_sum, states_sum, steps_sum, gates_sum = tuple((contract(piece) for piece in pieces))
    pre_rows = jnp.concatenate(
        [values_sum.astype(jnp.bfloat16), states_sum.astype(jnp.bfloat16)], axis=1
    )
    local_taps = jnp.concatenate(
        [
            lax.dynamic_slice_in_dim(conv_weight, group_index * local_width, local_width, 1),
            conv_weight[:, inner_width:],
        ],
        axis=1,
    )
    local_bias = jnp.concatenate(
        [
            lax.dynamic_slice_in_dim(conv_bias, group_index * local_width, local_width, 0),
            conv_bias[inner_width:],
        ],
        axis=0,
    )
    block_start = block_index * block_rows
    rim_rows = pre_rows[block_rows - (conv_taps - 1) :]
    prior_rim = from_behind(rim_rows, "seq", 1)
    extended = jnp.concatenate([prior_rim, pre_rows], axis=0)
    ext_positions = (
        block_start - (conv_taps - 1) + jnp.arange(block_rows + conv_taps - 1, dtype=jnp.int32)
    )
    ext_ids = segments_at(ext_positions, prompt_ends)
    own_ids = ext_ids[conv_taps - 1 :]
    filtered = jnp.zeros(pre_rows.shape, jnp.float32) + local_bias[None, :]
    for offset in range(conv_taps):
        matches = (ext_ids[offset : offset + block_rows] == own_ids).astype(jnp.float32)
        filtered = (
            filtered
            + local_taps[offset][None, :]
            * extended[offset : offset + block_rows].astype(jnp.float32)
            * matches[:, None]
        )
    conv_out = jax.nn.silu(filtered).astype(jnp.bfloat16)
    head_values = conv_out[:, :local_width]
    both_states = conv_out[:, local_width:]
    stretch_rows = STRETCH
    stretches = block_rows // stretch_rows
    positions = block_start + jnp.arange(block_rows, dtype=jnp.int32)
    segment_ids = segments_at(positions, prompt_ends)
    next_ids = segments_at(positions + 1, prompt_ends)
    before_ids = segments_at(positions - 1, prompt_ends)
    stretch_ids = segment_ids.reshape(stretches, stretch_rows)
    prior_ids = before_ids.reshape(stretches, stretch_rows)[:, 0]
    ends_mask = (segment_ids != next_ids).reshape(stretches, stretch_rows)
    step_sizes = jax.nn.softplus(steps_sum + step_bias[None, :])
    decay_steps = step_sizes * decay_rate[None, :]
    log_decay = -jnp.cumsum(decay_steps.reshape(stretches, stretch_rows, local_heads), axis=1)
    decay_heads = jnp.swapaxes(log_decay, 1, 2)
    step_heads = jnp.swapaxes(step_sizes.reshape(stretches, stretch_rows, local_heads), 1, 2)
    values = head_values.reshape(stretches, stretch_rows, local_heads, head_width)
    write_state = both_states[:, :state_width].reshape(stretches, stretch_rows, state_width)
    read_state = both_states[:, state_width:].reshape(stretches, stretch_rows, state_width)
    intersection = jnp.einsum(
        "ctn,csn->cts", read_state, write_state, preferred_element_type=jnp.float32
    )
    token_order = jnp.arange(stretch_rows, dtype=jnp.int32)
    causal = token_order[:, None] >= token_order[None, :]
    allowed = causal[None] & (stretch_ids[:, :, None] == stretch_ids[:, None, :])
    spread = decay_heads[:, :, :, None] - decay_heads[:, :, None, :]
    weights = (
        jnp.where(allowed[:, None], jnp.exp(jnp.minimum(spread, 0.0)), 0.0)
        * step_heads[:, :, None, :]
    )
    scores = (intersection[:, None] * weights).astype(jnp.bfloat16)
    within_stretch = jnp.einsum(
        "chts,cshp->cthp", scores, values, preferred_element_type=jnp.float32
    )
    last_ids = stretch_ids[:, -1]
    tail_decay = decay_heads[:, :, -1:]
    keep_tail = (stretch_ids == last_ids[:, None])[:, None, :]
    tail_coef = (
        jnp.where(keep_tail, jnp.exp(jnp.minimum(tail_decay - decay_heads, 0.0)), 0.0) * step_heads
    )
    tail_rows = (values.astype(jnp.float32) * jnp.swapaxes(tail_coef, 1, 2)[:, :, :, None]).astype(
        jnp.bfloat16
    )
    stretch_states = jnp.einsum(
        "clhp,cln->chpn", tail_rows, write_state, preferred_element_type=jnp.float32
    )
    stretch_gates = (
        jnp.exp(decay_heads[:, :, -1]) * (last_ids == prior_ids).astype(jnp.float32)[:, None]
    )
    block_gate = jnp.ones((local_heads,), jnp.float32)
    block_state = jnp.zeros((local_heads, head_width, state_width), jnp.float32)
    block_state = stretch_gates[0][:, None, None] * block_state + stretch_states[0]
    block_gate = block_gate * stretch_gates[0]

    def compose(earlier, later):
        return (earlier[0] * later[0], later[0][:, None, None] * earlier[1] + later[1])

    identity_pair = (jnp.ones_like(block_gate), jnp.zeros_like(block_state))
    carried = prefix((block_gate, block_state), "seq", compose, identity_pair)
    incoming = carried[1]
    arriving = []
    arriving.append(incoming)
    arriving = jnp.stack(arriving)
    carry_mask = (stretch_ids == prior_ids[:, None]).astype(jnp.float32)
    carry_decay = jnp.exp(log_decay) * carry_mask[:, :, None]
    from_before = (
        jnp.einsum(
            "cln,chpn->clhp",
            read_state,
            arriving.astype(jnp.bfloat16),
            preferred_element_type=jnp.float32,
        )
        * carry_decay[:, :, :, None]
    )
    result = (
        within_stretch + from_before + skip_gain[None, None, :, None] * values.astype(jnp.float32)
    )
    ssm_rows = result.reshape(block_rows, local_width).astype(jnp.bfloat16)
    end_weight = ends_mask.astype(jnp.float32)
    has_end = jnp.sum(end_weight, axis=1)
    end_decay = jnp.sum(decay_heads * end_weight[:, None, :], axis=2)
    end_ids = jnp.sum(jnp.where(ends_mask, stretch_ids, 0), axis=1)
    keep_end = ((stretch_ids == end_ids[:, None]) & (has_end[:, None] > 0))[:, None, :]
    end_coef = (
        jnp.where(keep_end, jnp.exp(jnp.minimum(end_decay[:, :, None] - decay_heads, 0.0)), 0.0)
        * step_heads
    )
    end_rows = (values.astype(jnp.float32) * jnp.swapaxes(end_coef, 1, 2)[:, :, :, None]).astype(
        jnp.bfloat16
    )
    end_states = jnp.einsum(
        "clhp,cln->chpn", end_rows, write_state, preferred_element_type=jnp.float32
    )
    end_carry = (
        jnp.exp(end_decay) * ((end_ids == prior_ids) & (has_end > 0)).astype(jnp.float32)[:, None]
    )
    end_states = end_states + end_carry[:, :, None, None] * arriving
    final_block = jnp.sum(end_states, axis=0)[None]
    head_gates = gates_sum.astype(jnp.bfloat16)
    norm_slice = lax.dynamic_slice_in_dim(norm_gain, group_index * local_width, local_width)
    gated = ssm_rows.astype(jnp.float32) * jax.nn.silu(head_gates.astype(jnp.float32))
    squares = lax.psum(jnp.sum(gated * gated, axis=1), "head")
    scaled = gated * lax.rsqrt(squares / inner_width + epsilon)[:, None] * norm_slice[None, :]
    outgoing = scaled.astype(jnp.bfloat16)
    returned = lax.all_to_all(
        outgoing.reshape(groups, sub_rows, local_width),
        "head",
        split_axis=0,
        concat_axis=2,
        tiled=True,
    )
    gated_out = returned.reshape(sub_rows, inner_width)
    return (gated_out, final_block)


def solution(mesh):
    in_specs = (
        P(("seq", "head"), None),
        P("seq", "head"),
        P("seq", "head"),
        P("seq", "head"),
        P("seq", None),
        P(),
        P(),
        P("head"),
        P("head"),
        P("head"),
        P(),
        P(),
    )
    out_specs = (P(("seq", "head"), None), P("seq", "head", None, None))
    return jax.shard_map(
        on_device, mesh=mesh, in_specs=in_specs, out_specs=out_specs, check_vma=False
    )
```

```python
import jax
import jax.numpy as jnp
from jax import lax
from jax.experimental import pallas as pl
from jax.experimental.pallas import tpu as pltpu
from jax.sharding import PartitionSpec as P

STRETCH = 256


epsilon = 1e-05


def from_behind(block, axis, distance):
    devices = range(lax.axis_size(axis))
    route = [(i - distance, i) for i in devices if i - distance in devices]
    return lax.ppermute(block, axis, route)


def prefix(value, axis, join, neutral):
    place = lax.axis_index(axis)
    gathered = jax.tree.map(
        lambda a, kind: lax.all_gather(a.astype(kind), axis), value, (jnp.bfloat16, jnp.bfloat16)
    )
    state = jax.tree.map(lambda a, e: jnp.zeros_like(a) + jnp.asarray(e, a.dtype), value, neutral)

    def one(turn, state):
        return join(
            state,
            jax.tree.map(
                lambda a, own: lax.dynamic_index_in_dim(a, turn, 0, False).astype(own.dtype),
                gathered,
                value,
            ),
        )

    return lax.fori_loop(0, place, one, state)


def segments_at(positions, prompt_ends):
    counted = jnp.sum((prompt_ends[None, :] <= positions[:, None]).astype(jnp.int32), axis=1)
    return jnp.where(positions < 0, -1, counted)


MESH = pl.DeviceIdType.MESH
BF16 = jnp.bfloat16
F32 = jnp.float32


def rdma(src, dst, send_sem, recv_sem, seq, head):
    return pltpu.make_async_remote_copy(
        src_ref=src,
        dst_ref=dst,
        send_sem=send_sem,
        recv_sem=recv_sem,
        device_id=(seq, head),
        device_id_type=MESH,
    )


def layer_kernel(
    hidden_ref,
    values_ref,
    gates_ref,
    states_ref,
    steps_ref,
    taps_ref,
    offset_ref,
    norm_ref,
    bias_ref,
    decay_ref,
    skip_ref,
    lengths_ref,
    out_ref,
    final_ref,
    hid,
    wbuf,
    out_v,
    out_s,
    out_g,
    in_v,
    in_s,
    in_g,
    own,
    tile,
    tiles,
    local_sem,
    hid_send,
    hid_recv,
    w_send,
    w_recv,
    part_send,
    part_recv,
    tile_send,
    tile_recv,
    halo_out,
    halo_in,
    ext,
    conv,
    cum_ref,
    cum_rows,
    dt_rows,
    carry_ref,
    end_ref,
    y_ref,
    inc,
    local_out,
    gate_out,
    local_in,
    gate_in,
    gated,
    whole,
    halo_send,
    halo_recv,
    state_send,
    state_recv,
    turn_send,
    turn_recv,
    small_ref,
    local_f32,
):
    s = lax.axis_index("seq")
    h = lax.axis_index("head")
    z = lax.div(s, 2)
    x = lax.rem(s, 2)
    z_lo = lax.rem(z, 2)
    z_hi = lax.div(z, 2)
    beside = s + 1 - 2 * x
    partner = s + 2 - 4 * z_lo
    far = s + 4 - 8 * z_hi
    heads = [lax.rem(h + d, 4) for d in (1, 2, 3)]
    rows_w = values_ref.shape[0]
    rows_h = hidden_ref.shape[0]
    depth = 2 * rows_w
    width = values_ref.shape[1]
    narrow = small_ref.shape[1]
    count_heads = steps_ref.shape[0]

    share = narrow // 2
    barrier = pltpu.get_barrier_semaphore()
    for d in range(1, 8):
        pl.semaphore_signal(
            barrier, inc=1, device_id=(lax.rem(s + d, 8), h), device_id_type=MESH
        )
    for to in heads:
        pl.semaphore_signal(barrier, inc=1, device_id=(s, to), device_id_type=MESH)

    wide_states = states_ref[
        :, pl.ds(pl.multiple_of(lax.div(h, 2) * narrow, 128), narrow)
    ].astype(F32)
    turned_states = pltpu.roll(wide_states, share, 1)
    place = (
        lax.broadcasted_iota(jnp.int32, (count_heads, narrow), 1)
        == lax.broadcasted_iota(jnp.int32, (count_heads, narrow), 0) + share
    )
    step_columns = lax.dot_general(
        steps_ref[...],
        place.astype(F32).astype(BF16),
        (((0,), (0,)), ((), ())),
        preferred_element_type=F32,
    )
    small_ref[...] = jnp.where(
        lax.broadcasted_iota(jnp.int32, small_ref.shape, 1) < share,
        jnp.where(lax.rem(h, 2) == 1, turned_states, wide_states),
        step_columns,
    ).astype(BF16)

    my_rows = pl.ds(pl.multiple_of(x * rows_w, 64), rows_w)
    my_tokens = pl.ds(pl.multiple_of(h * rows_h, 64), rows_h)
    cuts = (0, 2 * narrow, width)
    gate_cuts = (0, 2 * narrow, 4 * narrow, width)
    pieces = [(small_ref, 0, width, narrow)]
    pieces += [(values_ref, a, a, b - a) for a, b in zip(cuts, cuts[1:])]
    pieces += [
        (gates_ref, a, width + narrow + a, b - a) for a, b in zip(gate_cuts, gate_cuts[1:])
    ]
    sources = [ref.at[:, pl.ds(a, size)] for ref, a, _, size in pieces]
    windows = [pl.ds(at, size) for _, _, at, size in pieces]
    number = len(pieces)

    def columns(low, zh):
        return pl.ds(pl.multiple_of((low + 2 * zh) * depth, 128), depth)

    local = []
    for p in range(number):
        local.append(
            pltpu.make_async_copy(
                sources[p], wbuf.at[z_hi, my_rows, windows[p]], local_sem.at[p]
            )
        )
    for zh in range(2):
        local.append(
            pltpu.make_async_copy(
                hidden_ref.at[:, columns(z_lo, zh)],
                hid.at[0, zh, my_tokens],
                local_sem.at[number + zh],
            )
        )
    for c in local:
        c.start()
    pl.semaphore_wait(barrier, 10)

    to_far = [
        rdma(sources[p], wbuf.at[z_hi, my_rows, windows[p]], w_send.at[0, p], w_recv.at[0, p], far, h)
        for p in range(number)
    ]
    to_beside = [
        rdma(sources[p], wbuf.at[z_hi, my_rows, windows[p]], w_send.at[1, p], w_recv.at[1, p], beside, h)
        for p in range(number)
    ]
    passed = [
        rdma(
            wbuf.at[1 - z_hi, my_rows, windows[p]],
            wbuf.at[1 - z_hi, my_rows, windows[p]],
            w_send.at[2, p],
            w_recv.at[2, p],
            beside,
            h,
        )
        for p in range(number)
    ]
    hid_over = [
        rdma(
            hidden_ref.at[:, columns(1 - z_lo, zh)],
            hid.at[1, zh, my_tokens],
            hid_send.at[0, zh],
            hid_recv.at[0, zh],
            partner,
            h,
        )
        for zh in range(2)
    ]
    hid_own = [
        rdma(
            hidden_ref.at[:, columns(z_lo, zh)],
            hid.at[0, zh, my_tokens],
            hid_send.at[1 + d, zh],
            hid_recv.at[1 + d, zh],
            s,
            heads[d],
        )
        for zh in range(2)
        for d in range(3)
    ]
    hid_pass = [
        rdma(
            hid.at[1, zh, my_tokens],
            hid.at[1, zh, my_tokens],
            hid_send.at[4 + d, zh],
            hid_recv.at[4 + d, zh],
            s,
            heads[d],
        )
        for zh in range(2)
        for d in range(3)
    ]
    for c in hid_over:
        c.start()
    for p in range(3):
        to_far[p].start()
        to_beside[p].start()
    for c in hid_own:
        c.start()
    for zh in range(2):
        hid_over[zh].wait_recv()
        for d in range(3):
            hid_pass[3 * zh + d].start()

    def forward(p):
        to_far[p].wait_recv()
        passed[p].start()
        if p + 3 < number:
            to_far[p + 3].start()
            to_beside[p + 3].start()

    def landed(p):
        to_beside[p].wait_recv()
        passed[p].wait_recv()

    def product(which, window):
        return jnp.dot(
            hid[which, 0], wbuf[0, :, window], preferred_element_type=F32
        ) + jnp.dot(hid[which, 1], wbuf[1, :, window], preferred_element_type=F32)

    def span_of(p):
        _, a, _, size = pieces[p]
        return slice(a, a + size)

    def to_partner(p, out, arriving):
        landed(p)
        span = span_of(p)
        out[:, span] = product(1, windows[p]).astype(out.dtype)
        part = rdma(
            out.at[:, span], arriving.at[:, span], part_send.at[p], part_recv.at[p], partner, h
        )
        part.start()
        return part

    forward(0)
    forward(1)
    for c in local:
        c.wait()
    for c in hid_own:
        c.wait_recv()
    for c in hid_pass:
        c.wait_recv()
    part_s = to_partner(0, out_s, in_s)
    small = product(0, windows[0])
    part_v = [to_partner(1, out_v, in_v)]
    part_s.wait_recv()
    small = small + in_s[...].astype(F32)
    tile[...] = small.astype(BF16)
    tiles_out = [
        rdma(tile, tiles.at[h], tile_send.at[d], tile_recv.at[d], s, heads[d]) for d in range(3)
    ]
    for c in tiles_out:
        c.start()
    tiles[h] = tile[...]
    own[:, span_of(1)] = product(0, windows[1])

    rows = own.shape[0]
    start = s * rows
    count = lengths_ref.shape[0]
    ends = []
    for i in range(count):
        ends.append(lengths_ref[i] + (ends[i - 1] if i else 0))

    def segment(position):
        found = jnp.where(position < 0, -1, 0)
        for end in ends:
            found = found + jnp.where(end <= position, 1, 0)
        return found

    last_id = segment(start + rows - 1)
    prior_id = segment(start - 1)
    end_id = jnp.int32(-2)
    end_row = jnp.int32(-1)
    for i, end in enumerate(ends):
        inside = (end - 1 >= start) & (end - 1 < start + rows)
        end_id = jnp.where(inside, i, end_id)
        end_row = jnp.where(inside, end - 1 - start, end_row)

    order = lax.broadcasted_iota(jnp.int32, (rows, rows), 0)
    across = lax.broadcasted_iota(jnp.int32, (rows, rows), 1)
    lower = order >= across
    lower_ones = lower.astype(F32).astype(BF16)
    lane = lax.broadcasted_iota(jnp.int32, (rows, narrow), 1)
    token = lax.broadcasted_iota(jnp.int32, (rows, narrow), 0)
    ids = segment(start + token)

    def parts(value, number):
        taken = []
        for _ in range(number):
            piece = value.astype(BF16)
            taken.append(piece)
            value = value - piece.astype(F32)
        return taken

    head_lane = lax.broadcasted_iota(jnp.int32, (8, narrow), 1) - share

    def over_lanes(ref):
        row = jnp.zeros((8, narrow), F32)
        for i in range(count_heads):
            row = jnp.where(head_lane == i, ref[i], row)
        return row

    step = jax.nn.softplus(small + over_lanes(bias_ref)[0:1, :])
    rate = step * over_lanes(decay_ref)[0:1, :]
    cum = jnp.zeros((rows, narrow), F32)
    for piece in parts(rate, 3):
        cum = cum - jnp.dot(lower_ones, piece, preferred_element_type=F32)
    cum_ref[...] = cum
    cum_rows[...] = cum.T
    dt_rows[...] = step.T
    head_row = lax.broadcasted_iota(jnp.int32, (narrow, width), 0) - share
    channel = lax.broadcasted_iota(jnp.int32, (narrow, width), 1)
    spread = (
        ((channel >= head_row * share) & (channel < head_row * share + share))
        .astype(F32)
        .astype(BF16)
    )

    def expand(value, number):
        total = None
        for piece in parts(value, number):
            term = jnp.dot(piece, spread, preferred_element_type=F32)
            total = term if total is None else total + term
        return total

    cum_last = cum[rows - 1 : rows, :]
    cum_end = jnp.sum(jnp.where(token == end_row, cum, 0.0), axis=0, keepdims=True)
    gate_row = jnp.where(last_id == prior_id, jnp.exp(cum_last), 0.0)
    end_gate = jnp.where(end_id == prior_id, jnp.exp(cum_end), 0.0)
    eight = lax.broadcasted_iota(jnp.int32, (8, narrow), 0)
    rows8 = jnp.where(
        eight == 0,
        gate_row,
        jnp.where(eight == 1, end_gate, jnp.where(eight == 2, over_lanes(skip_ref), 0.0)),
    )
    wide8 = expand(rows8, 3)
    gate_out[...] = wide8
    tail = jnp.where(ids == last_id, jnp.exp(jnp.minimum(cum_last - cum, 0.0)), 0.0) * step
    tail_wide = expand(tail, 2)
    end_ref[...] = expand(
        jnp.where(ids == end_id, jnp.exp(jnp.minimum(cum_end - cum, 0.0)), 0.0) * step, 2
    )
    carry_ref[...] = expand(jnp.where(ids == prior_id, jnp.exp(cum), 0.0), 2)

    for c in tiles_out:
        c.wait_recv()
    for half in range(2):
        first = tiles[2 * half].astype(F32)
        second = pltpu.roll(tiles[2 * half + 1].astype(F32), share, 1)
        both = jnp.where(lane < share, first, second)
        low = width + half * narrow
        ext[8:, low : low + narrow] = both
        halo_out[:, low : low + narrow] = both[rows - 16 :, :].astype(BF16)
    forward(2)
    part_v.append(to_partner(2, out_v, in_v))
    own[:, span_of(2)] = product(0, windows[2])
    for c in part_v:
        c.wait_recv()
    pre = (own[...] + in_v[...].astype(F32)).astype(BF16)
    ext[8:, 0:width] = pre.astype(F32)
    halo_out[:, 0:width] = pre[rows - 16 :, :]
    halo = rdma(
        halo_out, halo_in, halo_send.at[0], halo_recv.at[0], lax.rem(s + 1, 8), h
    )
    halo.start()

    halo.wait_recv()
    ext[0:8, :] = halo_in[8:16, :].astype(F32)
    inner = 4 * width
    same = [
        (segment(start + token - d) == ids).astype(F32) for d in range(3, 0, -1)
    ]
    chunks = (width + 2 * narrow) // narrow
    for j in range(chunks):
        low = j * narrow
        if low < width:
            from_lane = pl.ds(pl.multiple_of(h * width + low, 128), narrow)
            offset = offset_ref[pl.ds(h * (width // narrow) + j, 1), :]
        else:
            from_lane = pl.ds(inner + low - width, narrow)
            offset = offset_ref[pl.ds((inner + low - width) // narrow, 1), :]
        taps = taps_ref[:, from_lane]
        total = jnp.zeros((rows, narrow), F32) + offset
        for tap in range(4):
            piece = ext[5 + tap : 5 + tap + rows, low : low + narrow] * taps[tap : tap + 1, :]
            total = total + (piece * same[tap] if tap < 3 else piece)
        conv[:, low : low + narrow] = jax.nn.silu(total).astype(BF16)

    values = conv[:, 0:width]
    write_turned = conv[:, width : width + narrow].astype(F32).T.astype(BF16)
    read_state = conv[:, width + narrow :]
    local = jnp.dot(
        write_turned,
        (values.astype(F32) * tail_wide).astype(BF16),
        preferred_element_type=F32,
    )
    local_f32[...] = local
    local_out[0] = local.astype(BF16)
    next_one = (
        rdma(
            local_out.at[0], local_in.at[0], state_send.at[0], state_recv.at[0], lax.rem(s + 1, 8), h
        ),
        rdma(gate_out, gate_in, state_send.at[1], state_recv.at[1], lax.rem(s + 1, 8), h),
    )
    next_two = rdma(
        local_out.at[1], local_in.at[1], state_send.at[2], state_recv.at[2], lax.rem(s + 2, 8), h
    )

    @pl.when(s < 7)
    def _():
        for c in next_one:
            c.start()

    inc[...] = jnp.zeros(inc.shape, F32)

    @pl.when(s > 0)
    def _():
        for c in next_one:
            c.wait_recv()
        inc[...] = local_in[0].astype(F32)

    @pl.when(s < 6)
    def _():
        local_out[1] = (local_f32[...] + wide8[0:1, :] * inc[...]).astype(BF16)
        next_two.start()

    forward(3)
    met = jnp.where(
        lower & (segment(start + order) == segment(start + across)),
        jnp.dot(read_state, write_turned, preferred_element_type=F32),
        0.0,
    )
    pairs = width // narrow
    for j in range(pairs):
        pair = conv[:, j * narrow : (j + 1) * narrow]
        halves = []
        for a in range(2):
            at = share + 2 * j + a
            decay = cum_ref[:, at : at + 1] - cum_rows[at : at + 1, :]
            scores = met * jnp.exp(jnp.minimum(decay, 0.0)) * dt_rows[at : at + 1, :]
            halves.append(jnp.dot(scores.astype(BF16), pair, preferred_element_type=F32))
        y_ref[:, j * narrow : (j + 1) * narrow] = jnp.where(lane < share, halves[0], halves[1])
    end_local = jnp.dot(
        write_turned,
        (values.astype(F32) * end_ref[...]).astype(BF16),
        preferred_element_type=F32,
    )

    part_g = [to_partner(3, out_g, in_g)]
    own[:, span_of(3)] = product(0, windows[3])

    @pl.when(s > 1)
    def _():
        next_two.wait_recv()
        inc[...] += gate_in[0:1, :] * local_in[1].astype(F32)

    for j in range(pairs):
        span = slice(j * narrow, (j + 1) * narrow)
        state = inc[:, span]
        final_ref[span, :] = (end_local[:, span] + wide8[1:2, span] * state).T
        before = jnp.dot(read_state, state.astype(BF16), preferred_element_type=F32)
        y_ref[:, span] = (
            y_ref[:, span]
            + before * carry_ref[:, span]
            + wide8[2:3, span] * conv[:, span].astype(F32)
        )

    turned = []

    def gate_piece(p):
        span = span_of(p)
        part_g[p - 3].wait_recv()
        gate = (own[:, span] + in_g[:, span].astype(F32)).astype(BF16).astype(F32)
        y = y_ref[:, span].astype(BF16).astype(F32)
        gated[:, span] = (y * jax.nn.silu(gate)).astype(BF16)
        size = span.stop - span.start
        to_columns = pl.ds(pl.multiple_of(h * width + span.start, 128), size)
        for d in range(3):
            their_rows = pl.ds(pl.multiple_of(heads[d] * rows_h, 64), rows_h)
            copy = rdma(
                gated.at[their_rows, span],
                whole.at[:, to_columns],
                turn_send.at[p - 3, d],
                turn_recv.at[p - 3, d],
                s,
                heads[d],
            )
            copy.start()
            turned.append(copy)
        keep = pltpu.make_async_copy(
            gated.at[my_tokens, span], whole.at[:, to_columns], local_sem.at[number + p - 1]
        )
        keep.start()
        kept.append(keep)

    kept = []
    forward(4)
    part_g.append(to_partner(4, out_g, in_g))
    own[:, span_of(4)] = product(0, windows[4])
    gate_piece(3)
    forward(5)
    part_g.append(to_partner(5, out_g, in_g))
    own[:, span_of(5)] = product(0, windows[5])
    gate_piece(4)
    gate_piece(5)
    for c in kept:
        c.wait()
    for c in turned:
        c.wait_recv()
    full = whole[...].astype(F32)
    mean = jnp.sum(full * full, axis=1, keepdims=True) / inner
    scale = lax.rsqrt(mean + epsilon)
    for j in range(inner // narrow):
        span = slice(j * narrow, (j + 1) * narrow)
        out_ref[:, span] = (
            whole[:, span].astype(F32) * scale * norm_ref[j : j + 1, :]
        ).astype(BF16)

    for c in [*to_far, *to_beside, *passed, *hid_over, *hid_own, *hid_pass, *tiles_out, *turned]:
        c.wait_send()
    for c in [part_s, *part_v, *part_g, halo]:
        c.wait_send()

    @pl.when(s < 7)
    def _():
        for c in next_one:
            c.wait_send()

    @pl.when(s < 6)
    def _():
        next_two.wait_send()


def layer(
    hidden,
    w_values,
    w_gates,
    w_steps,
    w_states,
    conv_weight,
    conv_bias,
    step_bias,
    decay_rate,
    skip_gain,
    norm_gain,
    lengths,
):
    rows = hidden.shape[0] * 4
    width = w_values.shape[1]
    count = step_bias.shape[0]
    narrow = w_states.shape[1] // 2
    depth = 2 * w_values.shape[0]
    channels = width + 2 * narrow
    vmem = pl.BlockSpec(memory_space=pltpu.VMEM)
    smem = pl.BlockSpec(memory_space=pltpu.SMEM)
    far_memory = pl.BlockSpec(memory_space=pltpu.HBM)
    dma = pltpu.SemaphoreType.DMA
    gated_out, final = pl.pallas_call(
        layer_kernel,
        out_shape=(
            jax.ShapeDtypeStruct(hidden.shape, BF16),
            jax.ShapeDtypeStruct((width, narrow), F32),
        ),
        in_specs=[far_memory] * 3 + [vmem] * 5 + [smem] * 4,
        out_specs=[vmem] * 2,
        scratch_shapes=[
            pltpu.VMEM((2, 2, rows, depth), BF16),
            pltpu.VMEM((2, depth, 2 * width + narrow), BF16),
            pltpu.VMEM((rows, width), BF16),
            pltpu.VMEM((rows, narrow), BF16),
            pltpu.VMEM((rows, width), BF16),
            pltpu.VMEM((rows, width), BF16),
            pltpu.VMEM((rows, narrow), BF16),
            pltpu.VMEM((rows, width), BF16),
            pltpu.VMEM((rows, width), F32),
            pltpu.VMEM((rows, narrow), BF16),
            pltpu.VMEM((4, rows, narrow), BF16),
            dma((11,)),
            dma((7, 2)),
            dma((7, 2)),
            dma((3, 6)),
            dma((3, 6)),
            dma((6,)),
            dma((6,)),
            dma((3,)),
            dma((3,)),
            pltpu.VMEM((16, channels), BF16),
            pltpu.VMEM((16, channels), BF16),
            pltpu.VMEM((8 + rows, channels), F32),
            pltpu.VMEM((rows, channels), BF16),
            pltpu.VMEM((rows, narrow), F32),
            pltpu.VMEM((narrow, rows), F32),
            pltpu.VMEM((narrow, rows), F32),
            pltpu.VMEM((rows, width), F32),
            pltpu.VMEM((rows, width), F32),
            pltpu.VMEM((rows, width), F32),
            pltpu.VMEM((narrow, width), F32),
            pltpu.VMEM((2, narrow, width), BF16),
            pltpu.VMEM((8, width), F32),
            pltpu.VMEM((2, narrow, width), BF16),
            pltpu.VMEM((8, width), F32),
            pltpu.VMEM((rows, width), BF16),
            pltpu.VMEM(hidden.shape, BF16),
            dma((1,)),
            dma((1,)),
            dma((3,)),
            dma((3,)),
            dma((3, 3)),
            dma((3, 3)),
            pltpu.VMEM((w_values.shape[0], narrow), BF16),
            pltpu.VMEM((narrow, width), F32),
        ],
        compiler_params=pltpu.CompilerParams(
            collective_id=0, has_side_effects=True, vmem_limit_bytes=60 * 1024 * 1024
        ),
    )(
        hidden,
        w_values,
        w_gates,
        w_states,
        w_steps.T,
        conv_weight,
        conv_bias.reshape(-1, narrow),
        norm_gain.reshape(-1, narrow),
        step_bias,
        decay_rate,
        skip_gain,
        lengths,
    )
    return gated_out, final.reshape(1, count, width // count, narrow)


def on_device(
    hidden,
    w_values,
    w_gates,
    w_steps,
    w_states,
    conv_weight,
    conv_bias,
    step_bias,
    decay_rate,
    skip_gain,
    norm_gain,
    lengths,
):
    groups = lax.axis_size("head")
    if lax.axis_size("seq") == 8 and groups == 4:
        return layer(
            hidden,
            w_values,
            w_gates,
            w_steps,
            w_states,
            conv_weight,
            conv_bias,
            step_bias,
            decay_rate,
            skip_gain,
            norm_gain,
            lengths,
        )
    group_index = lax.axis_index("head")
    block_index = lax.axis_index("seq")
    local_width = w_values.shape[1]
    inner_width = local_width * groups
    local_heads = decay_rate.shape[0]
    head_width = local_width // local_heads
    state_width = w_states.shape[1] // 2
    conv_taps = conv_weight.shape[0]
    prompt_ends = jnp.cumsum(lengths)
    block_hidden = lax.all_gather(hidden, "head", axis=0, tiled=True)
    block_rows = block_hidden.shape[0]
    sub_rows = block_rows // groups

    def contract(piece):
        return jnp.dot(block_hidden, piece, preferred_element_type=jnp.float32)

    pieces = (
        lax.all_gather(w_values, "seq", axis=0, tiled=True),
        lax.all_gather(w_states, "seq", axis=0, tiled=True),
        lax.all_gather(w_steps, "seq", axis=0, tiled=True),
        lax.all_gather(w_gates, "seq", axis=0, tiled=True),
    )
    values_sum, states_sum, steps_sum, gates_sum = tuple((contract(piece) for piece in pieces))
    pre_rows = jnp.concatenate(
        [values_sum.astype(jnp.bfloat16), states_sum.astype(jnp.bfloat16)], axis=1
    )
    local_taps = jnp.concatenate(
        [
            lax.dynamic_slice_in_dim(conv_weight, group_index * local_width, local_width, 1),
            conv_weight[:, inner_width:],
        ],
        axis=1,
    )
    local_bias = jnp.concatenate(
        [
            lax.dynamic_slice_in_dim(conv_bias, group_index * local_width, local_width, 0),
            conv_bias[inner_width:],
        ],
        axis=0,
    )
    block_start = block_index * block_rows
    rim_rows = pre_rows[block_rows - (conv_taps - 1) :]
    prior_rim = from_behind(rim_rows, "seq", 1)
    extended = jnp.concatenate([prior_rim, pre_rows], axis=0)
    ext_positions = (
        block_start - (conv_taps - 1) + jnp.arange(block_rows + conv_taps - 1, dtype=jnp.int32)
    )
    ext_ids = segments_at(ext_positions, prompt_ends)
    own_ids = ext_ids[conv_taps - 1 :]
    filtered = jnp.zeros(pre_rows.shape, jnp.float32) + local_bias[None, :]
    for offset in range(conv_taps):
        matches = (ext_ids[offset : offset + block_rows] == own_ids).astype(jnp.float32)
        filtered = (
            filtered
            + local_taps[offset][None, :]
            * extended[offset : offset + block_rows].astype(jnp.float32)
            * matches[:, None]
        )
    conv_out = jax.nn.silu(filtered).astype(jnp.bfloat16)
    head_values = conv_out[:, :local_width]
    both_states = conv_out[:, local_width:]
    stretch_rows = STRETCH
    stretches = block_rows // stretch_rows
    positions = block_start + jnp.arange(block_rows, dtype=jnp.int32)
    segment_ids = segments_at(positions, prompt_ends)
    next_ids = segments_at(positions + 1, prompt_ends)
    before_ids = segments_at(positions - 1, prompt_ends)
    stretch_ids = segment_ids.reshape(stretches, stretch_rows)
    prior_ids = before_ids.reshape(stretches, stretch_rows)[:, 0]
    ends_mask = (segment_ids != next_ids).reshape(stretches, stretch_rows)
    step_sizes = jax.nn.softplus(steps_sum + step_bias[None, :])
    decay_steps = step_sizes * decay_rate[None, :]
    log_decay = -jnp.cumsum(decay_steps.reshape(stretches, stretch_rows, local_heads), axis=1)
    decay_heads = jnp.swapaxes(log_decay, 1, 2)
    step_heads = jnp.swapaxes(step_sizes.reshape(stretches, stretch_rows, local_heads), 1, 2)
    values = head_values.reshape(stretches, stretch_rows, local_heads, head_width)
    write_state = both_states[:, :state_width].reshape(stretches, stretch_rows, state_width)
    read_state = both_states[:, state_width:].reshape(stretches, stretch_rows, state_width)
    intersection = jnp.einsum(
        "ctn,csn->cts", read_state, write_state, preferred_element_type=jnp.float32
    )
    token_order = jnp.arange(stretch_rows, dtype=jnp.int32)
    causal = token_order[:, None] >= token_order[None, :]
    allowed = causal[None] & (stretch_ids[:, :, None] == stretch_ids[:, None, :])
    spread = decay_heads[:, :, :, None] - decay_heads[:, :, None, :]
    weights = (
        jnp.where(allowed[:, None], jnp.exp(jnp.minimum(spread, 0.0)), 0.0)
        * step_heads[:, :, None, :]
    )
    scores = (intersection[:, None] * weights).astype(jnp.bfloat16)
    within_stretch = jnp.einsum(
        "chts,cshp->cthp", scores, values, preferred_element_type=jnp.float32
    )
    last_ids = stretch_ids[:, -1]
    tail_decay = decay_heads[:, :, -1:]
    keep_tail = (stretch_ids == last_ids[:, None])[:, None, :]
    tail_coef = (
        jnp.where(keep_tail, jnp.exp(jnp.minimum(tail_decay - decay_heads, 0.0)), 0.0) * step_heads
    )
    tail_rows = (values.astype(jnp.float32) * jnp.swapaxes(tail_coef, 1, 2)[:, :, :, None]).astype(
        jnp.bfloat16
    )
    stretch_states = jnp.einsum(
        "clhp,cln->chpn", tail_rows, write_state, preferred_element_type=jnp.float32
    )
    stretch_gates = (
        jnp.exp(decay_heads[:, :, -1]) * (last_ids == prior_ids).astype(jnp.float32)[:, None]
    )
    block_gate = jnp.ones((local_heads,), jnp.float32)
    block_state = jnp.zeros((local_heads, head_width, state_width), jnp.float32)
    block_state = stretch_gates[0][:, None, None] * block_state + stretch_states[0]
    block_gate = block_gate * stretch_gates[0]

    def compose(earlier, later):
        return (earlier[0] * later[0], later[0][:, None, None] * earlier[1] + later[1])

    identity_pair = (jnp.ones_like(block_gate), jnp.zeros_like(block_state))
    carried = prefix((block_gate, block_state), "seq", compose, identity_pair)
    incoming = carried[1]
    arriving = []
    arriving.append(incoming)
    arriving = jnp.stack(arriving)
    carry_mask = (stretch_ids == prior_ids[:, None]).astype(jnp.float32)
    carry_decay = jnp.exp(log_decay) * carry_mask[:, :, None]
    from_before = (
        jnp.einsum(
            "cln,chpn->clhp",
            read_state,
            arriving.astype(jnp.bfloat16),
            preferred_element_type=jnp.float32,
        )
        * carry_decay[:, :, :, None]
    )
    result = (
        within_stretch + from_before + skip_gain[None, None, :, None] * values.astype(jnp.float32)
    )
    ssm_rows = result.reshape(block_rows, local_width).astype(jnp.bfloat16)
    end_weight = ends_mask.astype(jnp.float32)
    has_end = jnp.sum(end_weight, axis=1)
    end_decay = jnp.sum(decay_heads * end_weight[:, None, :], axis=2)
    end_ids = jnp.sum(jnp.where(ends_mask, stretch_ids, 0), axis=1)
    keep_end = ((stretch_ids == end_ids[:, None]) & (has_end[:, None] > 0))[:, None, :]
    end_coef = (
        jnp.where(keep_end, jnp.exp(jnp.minimum(end_decay[:, :, None] - decay_heads, 0.0)), 0.0)
        * step_heads
    )
    end_rows = (values.astype(jnp.float32) * jnp.swapaxes(end_coef, 1, 2)[:, :, :, None]).astype(
        jnp.bfloat16
    )
    end_states = jnp.einsum(
        "clhp,cln->chpn", end_rows, write_state, preferred_element_type=jnp.float32
    )
    end_carry = (
        jnp.exp(end_decay) * ((end_ids == prior_ids) & (has_end > 0)).astype(jnp.float32)[:, None]
    )
    end_states = end_states + end_carry[:, :, None, None] * arriving
    final_block = jnp.sum(end_states, axis=0)[None]
    head_gates = gates_sum.astype(jnp.bfloat16)
    norm_slice = lax.dynamic_slice_in_dim(norm_gain, group_index * local_width, local_width)
    gated = ssm_rows.astype(jnp.float32) * jax.nn.silu(head_gates.astype(jnp.float32))
    squares = lax.psum(jnp.sum(gated * gated, axis=1), "head")
    scaled = gated * lax.rsqrt(squares / inner_width + epsilon)[:, None] * norm_slice[None, :]
    outgoing = scaled.astype(jnp.bfloat16)
    returned = lax.all_to_all(
        outgoing.reshape(groups, sub_rows, local_width),
        "head",
        split_axis=0,
        concat_axis=2,
        tiled=True,
    )
    gated_out = returned.reshape(sub_rows, inner_width)
    return (gated_out, final_block)


def solution(mesh):
    in_specs = (
        P(("seq", "head"), None),
        P("seq", "head"),
        P("seq", "head"),
        P("seq", "head"),
        P("seq", None),
        P(),
        P(),
        P("head"),
        P("head"),
        P("head"),
        P(),
        P(),
    )
    out_specs = (P(("seq", "head"), None), P("seq", "head", None, None))
    return jax.shard_map(
        on_device, mesh=mesh, in_specs=in_specs, out_specs=out_specs, check_vma=False
    )
```

```python
import jax
import jax.numpy as jnp
from jax import lax
from jax.experimental import pallas as pl
from jax.experimental.pallas import tpu as pltpu
from jax.sharding import PartitionSpec as P

STRETCH = 256


epsilon = 1e-05


def from_behind(block, axis, distance):
    devices = range(lax.axis_size(axis))
    route = [(i - distance, i) for i in devices if i - distance in devices]
    return lax.ppermute(block, axis, route)


def prefix(value, axis, join, neutral):
    place = lax.axis_index(axis)
    gathered = jax.tree.map(
        lambda a, kind: lax.all_gather(a.astype(kind), axis), value, (jnp.bfloat16, jnp.bfloat16)
    )
    state = jax.tree.map(lambda a, e: jnp.zeros_like(a) + jnp.asarray(e, a.dtype), value, neutral)

    def one(turn, state):
        return join(
            state,
            jax.tree.map(
                lambda a, own: lax.dynamic_index_in_dim(a, turn, 0, False).astype(own.dtype),
                gathered,
                value,
            ),
        )

    return lax.fori_loop(0, place, one, state)


def segments_at(positions, prompt_ends):
    counted = jnp.sum((prompt_ends[None, :] <= positions[:, None]).astype(jnp.int32), axis=1)
    return jnp.where(positions < 0, -1, counted)


MESH = pl.DeviceIdType.MESH
BF16 = jnp.bfloat16
F32 = jnp.float32


def rdma(src, dst, send_sem, recv_sem, seq, head):
    return pltpu.make_async_remote_copy(
        src_ref=src,
        dst_ref=dst,
        send_sem=send_sem,
        recv_sem=recv_sem,
        device_id=(seq, head),
        device_id_type=MESH,
    )


def layer_kernel(
    hidden_ref,
    values_ref,
    gates_ref,
    states_ref,
    steps_ref,
    taps_ref,
    offset_ref,
    norm_ref,
    bias_ref,
    decay_ref,
    skip_ref,
    lengths_ref,
    out_ref,
    final_ref,
    hid,
    wbuf,
    out_v,
    out_s,
    out_g,
    in_v,
    in_s,
    in_g,
    own,
    tile,
    tiles,
    local_sem,
    hid_send,
    hid_recv,
    w_send,
    w_recv,
    part_send,
    part_recv,
    tile_send,
    tile_recv,
    halo_out,
    halo_in,
    ext,
    conv,
    cum_ref,
    cum_rows,
    dt_rows,
    carry_ref,
    end_ref,
    y_ref,
    inc,
    local_out,
    gate_out,
    local_in,
    gate_in,
    gated,
    whole,
    halo_send,
    halo_recv,
    state_send,
    state_recv,
    turn_send,
    turn_recv,
    small_ref,
    local_f32,
):
    s = lax.axis_index("seq")
    h = lax.axis_index("head")
    z = lax.div(s, 2)
    x = lax.rem(s, 2)
    z_lo = lax.rem(z, 2)
    z_hi = lax.div(z, 2)
    beside = s + 1 - 2 * x
    partner = s + 2 - 4 * z_lo
    far = s + 4 - 8 * z_hi
    heads = [lax.rem(h + d, 4) for d in (1, 2, 3)]
    rows_w = values_ref.shape[0]
    rows_h = hidden_ref.shape[0]
    depth = 2 * rows_w
    width = values_ref.shape[1]
    narrow = small_ref.shape[1]
    count_heads = steps_ref.shape[0]

    share = narrow // 2
    barrier = pltpu.get_barrier_semaphore()
    for d in range(1, 8):
        pl.semaphore_signal(
            barrier, inc=1, device_id=(lax.rem(s + d, 8), h), device_id_type=MESH
        )
    for to in heads:
        pl.semaphore_signal(barrier, inc=1, device_id=(s, to), device_id_type=MESH)

    wide_states = states_ref[
        :, pl.ds(pl.multiple_of(lax.div(h, 2) * narrow, 128), narrow)
    ].astype(F32)
    turned_states = pltpu.roll(wide_states, share, 1)
    place = (
        lax.broadcasted_iota(jnp.int32, (count_heads, narrow), 1)
        == lax.broadcasted_iota(jnp.int32, (count_heads, narrow), 0) + share
    )
    step_columns = lax.dot_general(
        steps_ref[...],
        place.astype(F32).astype(BF16),
        (((0,), (0,)), ((), ())),
        preferred_element_type=F32,
    )
    small_ref[...] = jnp.where(
        lax.broadcasted_iota(jnp.int32, small_ref.shape, 1) < share,
        jnp.where(lax.rem(h, 2) == 1, turned_states, wide_states),
        step_columns,
    ).astype(BF16)

    my_rows = pl.ds(pl.multiple_of(x * rows_w, 64), rows_w)
    my_tokens = pl.ds(pl.multiple_of(h * rows_h, 64), rows_h)
    cuts = (0, 2 * narrow, width)
    gate_cuts = (0, 2 * narrow, 4 * narrow, width)
    pieces = [(small_ref, 0, width, narrow)]
    pieces += [(values_ref, a, a, b - a) for a, b in zip(cuts, cuts[1:])]
    pieces += [
        (gates_ref, a, width + narrow + a, b - a) for a, b in zip(gate_cuts, gate_cuts[1:])
    ]
    sources = [ref.at[:, pl.ds(a, size)] for ref, a, _, size in pieces]
    windows = [pl.ds(at, size) for _, _, at, size in pieces]
    number = len(pieces)

    def columns(low, zh):
        return pl.ds(pl.multiple_of((low + 2 * zh) * depth, 128), depth)

    local = []
    for p in range(number):
        local.append(
            pltpu.make_async_copy(
                sources[p], wbuf.at[z_hi, my_rows, windows[p]], local_sem.at[p]
            )
        )
    for zh in range(2):
        local.append(
            pltpu.make_async_copy(
                hidden_ref.at[:, columns(z_lo, zh)],
                hid.at[0, zh, my_tokens],
                local_sem.at[number + zh],
            )
        )
    for c in local:
        c.start()
    pl.semaphore_wait(barrier, 10)

    to_far = [
        rdma(sources[p], wbuf.at[z_hi, my_rows, windows[p]], w_send.at[0, p], w_recv.at[0, p], far, h)
        for p in range(number)
    ]
    to_beside = [
        rdma(sources[p], wbuf.at[z_hi, my_rows, windows[p]], w_send.at[1, p], w_recv.at[1, p], beside, h)
        for p in range(number)
    ]
    passed = [
        rdma(
            wbuf.at[1 - z_hi, my_rows, windows[p]],
            wbuf.at[1 - z_hi, my_rows, windows[p]],
            w_send.at[2, p],
            w_recv.at[2, p],
            beside,
            h,
        )
        for p in range(number)
    ]
    hid_over = [
        rdma(
            hidden_ref.at[:, columns(1 - z_lo, zh)],
            hid.at[1, zh, my_tokens],
            hid_send.at[0, zh],
            hid_recv.at[0, zh],
            partner,
            h,
        )
        for zh in range(2)
    ]
    hid_own = [
        rdma(
            hidden_ref.at[:, columns(z_lo, zh)],
            hid.at[0, zh, my_tokens],
            hid_send.at[1 + d, zh],
            hid_recv.at[1 + d, zh],
            s,
            heads[d],
        )
        for zh in range(2)
        for d in range(3)
    ]
    hid_pass = [
        rdma(
            hid.at[1, zh, my_tokens],
            hid.at[1, zh, my_tokens],
            hid_send.at[4 + d, zh],
            hid_recv.at[4 + d, zh],
            s,
            heads[d],
        )
        for zh in range(2)
        for d in range(3)
    ]
    for c in hid_over:
        c.start()
    for p in range(3):
        to_far[p].start()
        to_beside[p].start()
    for c in hid_own:
        c.start()
    for zh in range(2):
        hid_over[zh].wait_recv()
        for d in range(3):
            hid_pass[3 * zh + d].start()

    def forward(p):
        to_far[p].wait_recv()
        passed[p].start()
        if p + 3 < number:
            to_far[p + 3].start()
            to_beside[p + 3].start()

    def landed(p):
        to_beside[p].wait_recv()
        passed[p].wait_recv()

    def product(which, window):
        return jnp.dot(
            hid[which, 0], wbuf[0, :, window], preferred_element_type=F32
        ) + jnp.dot(hid[which, 1], wbuf[1, :, window], preferred_element_type=F32)

    def span_of(p):
        _, a, _, size = pieces[p]
        return slice(a, a + size)

    def to_partner(p, out, arriving):
        landed(p)
        span = span_of(p)
        out[:, span] = product(1, windows[p]).astype(out.dtype)
        part = rdma(
            out.at[:, span], arriving.at[:, span], part_send.at[p], part_recv.at[p], partner, h
        )
        part.start()
        return part

    for p in range(3):
        forward(p)
    for c in local:
        c.wait()
    for c in hid_own:
        c.wait_recv()
    for c in hid_pass:
        c.wait_recv()
    part_s = to_partner(0, out_s, in_s)
    part_v = [to_partner(1, out_v, in_v)]
    forward(3)
    part_v.append(to_partner(2, out_v, in_v))
    small = product(0, windows[0])
    part_s.wait_recv()
    small = small + in_s[...].astype(F32)
    tile[...] = small.astype(BF16)
    tiles_out = [
        rdma(tile, tiles.at[h], tile_send.at[d], tile_recv.at[d], s, heads[d]) for d in range(3)
    ]
    for c in tiles_out:
        c.start()
    tiles[h] = tile[...]
    for p in (1, 2):
        own[:, span_of(p)] = product(0, windows[p])

    rows = own.shape[0]
    start = s * rows
    count = lengths_ref.shape[0]
    ends = []
    for i in range(count):
        ends.append(lengths_ref[i] + (ends[i - 1] if i else 0))

    def segment(position):
        found = jnp.where(position < 0, -1, 0)
        for end in ends:
            found = found + jnp.where(end <= position, 1, 0)
        return found

    last_id = segment(start + rows - 1)
    prior_id = segment(start - 1)
    end_id = jnp.int32(-2)
    end_row = jnp.int32(-1)
    for i, end in enumerate(ends):
        inside = (end - 1 >= start) & (end - 1 < start + rows)
        end_id = jnp.where(inside, i, end_id)
        end_row = jnp.where(inside, end - 1 - start, end_row)

    order = lax.broadcasted_iota(jnp.int32, (rows, rows), 0)
    across = lax.broadcasted_iota(jnp.int32, (rows, rows), 1)
    lower = order >= across
    lower_ones = lower.astype(F32).astype(BF16)
    lane = lax.broadcasted_iota(jnp.int32, (rows, narrow), 1)
    token = lax.broadcasted_iota(jnp.int32, (rows, narrow), 0)
    ids = segment(start + token)

    def parts(value, number):
        taken = []
        for _ in range(number):
            piece = value.astype(BF16)
            taken.append(piece)
            value = value - piece.astype(F32)
        return taken

    head_lane = lax.broadcasted_iota(jnp.int32, (8, narrow), 1) - share

    def over_lanes(ref):
        row = jnp.zeros((8, narrow), F32)
        for i in range(count_heads):
            row = jnp.where(head_lane == i, ref[i], row)
        return row

    step = jax.nn.softplus(small + over_lanes(bias_ref)[0:1, :])
    rate = step * over_lanes(decay_ref)[0:1, :]
    cum = jnp.zeros((rows, narrow), F32)
    for piece in parts(rate, 3):
        cum = cum - jnp.dot(lower_ones, piece, preferred_element_type=F32)
    cum_ref[...] = cum
    cum_rows[...] = cum.T
    dt_rows[...] = step.T
    head_row = lax.broadcasted_iota(jnp.int32, (narrow, width), 0) - share
    channel = lax.broadcasted_iota(jnp.int32, (narrow, width), 1)
    spread = (
        ((channel >= head_row * share) & (channel < head_row * share + share))
        .astype(F32)
        .astype(BF16)
    )

    def expand(value, number):
        total = None
        for piece in parts(value, number):
            term = jnp.dot(piece, spread, preferred_element_type=F32)
            total = term if total is None else total + term
        return total

    cum_last = cum[rows - 1 : rows, :]
    cum_end = jnp.sum(jnp.where(token == end_row, cum, 0.0), axis=0, keepdims=True)
    gate_row = jnp.where(last_id == prior_id, jnp.exp(cum_last), 0.0)
    end_gate = jnp.where(end_id == prior_id, jnp.exp(cum_end), 0.0)
    eight = lax.broadcasted_iota(jnp.int32, (8, narrow), 0)
    rows8 = jnp.where(
        eight == 0,
        gate_row,
        jnp.where(eight == 1, end_gate, jnp.where(eight == 2, over_lanes(skip_ref), 0.0)),
    )
    wide8 = expand(rows8, 3)
    gate_out[...] = wide8
    tail = jnp.where(ids == last_id, jnp.exp(jnp.minimum(cum_last - cum, 0.0)), 0.0) * step
    tail_wide = expand(tail, 2)
    end_ref[...] = expand(
        jnp.where(ids == end_id, jnp.exp(jnp.minimum(cum_end - cum, 0.0)), 0.0) * step, 2
    )
    carry_ref[...] = expand(jnp.where(ids == prior_id, jnp.exp(cum), 0.0), 2)

    for c in tiles_out:
        c.wait_recv()
    for half in range(2):
        first = tiles[2 * half].astype(F32)
        second = pltpu.roll(tiles[2 * half + 1].astype(F32), share, 1)
        both = jnp.where(lane < share, first, second)
        low = width + half * narrow
        ext[8:, low : low + narrow] = both
        halo_out[:, low : low + narrow] = both[rows - 16 :, :].astype(BF16)
    for c in part_v:
        c.wait_recv()
    pre = (own[...] + in_v[...].astype(F32)).astype(BF16)
    ext[8:, 0:width] = pre.astype(F32)
    halo_out[:, 0:width] = pre[rows - 16 :, :]
    halo = rdma(
        halo_out, halo_in, halo_send.at[0], halo_recv.at[0], lax.rem(s + 1, 8), h
    )
    halo.start()

    forward(4)
    halo.wait_recv()
    ext[0:8, :] = halo_in[8:16, :].astype(F32)
    inner = 4 * width
    same = [
        (segment(start + token - d) == ids).astype(F32) for d in range(3, 0, -1)
    ]
    chunks = (width + 2 * narrow) // narrow
    for j in range(chunks):
        low = j * narrow
        if low < width:
            from_lane = pl.ds(pl.multiple_of(h * width + low, 128), narrow)
            offset = offset_ref[pl.ds(h * (width // narrow) + j, 1), :]
        else:
            from_lane = pl.ds(inner + low - width, narrow)
            offset = offset_ref[pl.ds((inner + low - width) // narrow, 1), :]
        taps = taps_ref[:, from_lane]
        total = jnp.zeros((rows, narrow), F32) + offset
        for tap in range(4):
            piece = ext[5 + tap : 5 + tap + rows, low : low + narrow] * taps[tap : tap + 1, :]
            total = total + (piece * same[tap] if tap < 3 else piece)
        conv[:, low : low + narrow] = jax.nn.silu(total).astype(BF16)

    values = conv[:, 0:width]
    write_turned = conv[:, width : width + narrow].astype(F32).T.astype(BF16)
    read_state = conv[:, width + narrow :]
    local = jnp.dot(
        write_turned,
        (values.astype(F32) * tail_wide).astype(BF16),
        preferred_element_type=F32,
    )
    local_f32[...] = local
    local_out[0] = local.astype(BF16)
    next_one = (
        rdma(
            local_out.at[0], local_in.at[0], state_send.at[0], state_recv.at[0], lax.rem(s + 1, 8), h
        ),
        rdma(gate_out, gate_in, state_send.at[1], state_recv.at[1], lax.rem(s + 1, 8), h),
    )
    next_two = rdma(
        local_out.at[1], local_in.at[1], state_send.at[2], state_recv.at[2], lax.rem(s + 2, 8), h
    )

    @pl.when(s < 7)
    def _():
        for c in next_one:
            c.start()

    forward(5)
    inc[...] = jnp.zeros(inc.shape, F32)

    @pl.when(s > 0)
    def _():
        for c in next_one:
            c.wait_recv()
        inc[...] = local_in[0].astype(F32)

    @pl.when(s < 6)
    def _():
        local_out[1] = (local_f32[...] + wide8[0:1, :] * inc[...]).astype(BF16)
        next_two.start()

    met = jnp.where(
        lower & (segment(start + order) == segment(start + across)),
        jnp.dot(read_state, write_turned, preferred_element_type=F32),
        0.0,
    )
    pairs = width // narrow
    for j in range(pairs):
        pair = conv[:, j * narrow : (j + 1) * narrow]
        halves = []
        for a in range(2):
            at = share + 2 * j + a
            decay = cum_ref[:, at : at + 1] - cum_rows[at : at + 1, :]
            scores = met * jnp.exp(jnp.minimum(decay, 0.0)) * dt_rows[at : at + 1, :]
            halves.append(jnp.dot(scores.astype(BF16), pair, preferred_element_type=F32))
        y_ref[:, j * narrow : (j + 1) * narrow] = jnp.where(lane < share, halves[0], halves[1])
    end_local = jnp.dot(
        write_turned,
        (values.astype(F32) * end_ref[...]).astype(BF16),
        preferred_element_type=F32,
    )

    part_g = []
    for p in (3, 4):
        part_g.append(to_partner(p, out_g, in_g))
        own[:, span_of(p)] = product(0, windows[p])

    @pl.when(s > 1)
    def _():
        next_two.wait_recv()
        inc[...] += gate_in[0:1, :] * local_in[1].astype(F32)

    for j in range(pairs):
        span = slice(j * narrow, (j + 1) * narrow)
        state = inc[:, span]
        final_ref[span, :] = (end_local[:, span] + wide8[1:2, span] * state).T
        before = jnp.dot(read_state, state.astype(BF16), preferred_element_type=F32)
        y_ref[:, span] = (
            y_ref[:, span]
            + before * carry_ref[:, span]
            + wide8[2:3, span] * conv[:, span].astype(F32)
        )

    turned = []

    def gate_piece(p):
        span = span_of(p)
        part_g[p - 3].wait_recv()
        gate = (own[:, span] + in_g[:, span].astype(F32)).astype(BF16).astype(F32)
        y = y_ref[:, span].astype(BF16).astype(F32)
        gated[:, span] = (y * jax.nn.silu(gate)).astype(BF16)
        size = span.stop - span.start
        to_columns = pl.ds(pl.multiple_of(h * width + span.start, 128), size)
        for d in range(3):
            their_rows = pl.ds(pl.multiple_of(heads[d] * rows_h, 64), rows_h)
            copy = rdma(
                gated.at[their_rows, span],
                whole.at[:, to_columns],
                turn_send.at[p - 3, d],
                turn_recv.at[p - 3, d],
                s,
                heads[d],
            )
            copy.start()
            turned.append(copy)
        keep = pltpu.make_async_copy(
            gated.at[my_tokens, span], whole.at[:, to_columns], local_sem.at[number + p - 1]
        )
        keep.start()
        kept.append(keep)

    kept = []
    gate_piece(3)
    part_g.append(to_partner(5, out_g, in_g))
    own[:, span_of(5)] = product(0, windows[5])
    gate_piece(4)
    gate_piece(5)
    for c in kept:
        c.wait()
    for c in turned:
        c.wait_recv()
    full = whole[...].astype(F32)
    mean = jnp.sum(full * full, axis=1, keepdims=True) / inner
    scale = lax.rsqrt(mean + epsilon)
    for j in range(inner // narrow):
        span = slice(j * narrow, (j + 1) * narrow)
        out_ref[:, span] = (
            whole[:, span].astype(F32) * scale * norm_ref[j : j + 1, :]
        ).astype(BF16)

    for c in [*to_far, *to_beside, *passed, *hid_over, *hid_own, *hid_pass, *tiles_out, *turned]:
        c.wait_send()
    for c in [part_s, *part_v, *part_g, halo]:
        c.wait_send()

    @pl.when(s < 7)
    def _():
        for c in next_one:
            c.wait_send()

    @pl.when(s < 6)
    def _():
        next_two.wait_send()


def layer(
    hidden,
    w_values,
    w_gates,
    w_steps,
    w_states,
    conv_weight,
    conv_bias,
    step_bias,
    decay_rate,
    skip_gain,
    norm_gain,
    lengths,
):
    rows = hidden.shape[0] * 4
    width = w_values.shape[1]
    count = step_bias.shape[0]
    narrow = w_states.shape[1] // 2
    depth = 2 * w_values.shape[0]
    channels = width + 2 * narrow
    vmem = pl.BlockSpec(memory_space=pltpu.VMEM)
    smem = pl.BlockSpec(memory_space=pltpu.SMEM)
    far_memory = pl.BlockSpec(memory_space=pltpu.HBM)
    dma = pltpu.SemaphoreType.DMA
    gated_out, final = pl.pallas_call(
        layer_kernel,
        out_shape=(
            jax.ShapeDtypeStruct(hidden.shape, BF16),
            jax.ShapeDtypeStruct((width, narrow), F32),
        ),
        in_specs=[far_memory] * 3 + [vmem] * 5 + [smem] * 4,
        out_specs=[vmem] * 2,
        scratch_shapes=[
            pltpu.VMEM((2, 2, rows, depth), BF16),
            pltpu.VMEM((2, depth, 2 * width + narrow), BF16),
            pltpu.VMEM((rows, width), BF16),
            pltpu.VMEM((rows, narrow), BF16),
            pltpu.VMEM((rows, width), BF16),
            pltpu.VMEM((rows, width), BF16),
            pltpu.VMEM((rows, narrow), BF16),
            pltpu.VMEM((rows, width), BF16),
            pltpu.VMEM((rows, width), F32),
            pltpu.VMEM((rows, narrow), BF16),
            pltpu.VMEM((4, rows, narrow), BF16),
            dma((11,)),
            dma((7, 2)),
            dma((7, 2)),
            dma((3, 6)),
            dma((3, 6)),
            dma((6,)),
            dma((6,)),
            dma((3,)),
            dma((3,)),
            pltpu.VMEM((16, channels), BF16),
            pltpu.VMEM((16, channels), BF16),
            pltpu.VMEM((8 + rows, channels), F32),
            pltpu.VMEM((rows, channels), BF16),
            pltpu.VMEM((rows, narrow), F32),
            pltpu.VMEM((narrow, rows), F32),
            pltpu.VMEM((narrow, rows), F32),
            pltpu.VMEM((rows, width), F32),
            pltpu.VMEM((rows, width), F32),
            pltpu.VMEM((rows, width), F32),
            pltpu.VMEM((narrow, width), F32),
            pltpu.VMEM((2, narrow, width), BF16),
            pltpu.VMEM((8, width), F32),
            pltpu.VMEM((2, narrow, width), BF16),
            pltpu.VMEM((8, width), F32),
            pltpu.VMEM((rows, width), BF16),
            pltpu.VMEM(hidden.shape, BF16),
            dma((1,)),
            dma((1,)),
            dma((3,)),
            dma((3,)),
            dma((3, 3)),
            dma((3, 3)),
            pltpu.VMEM((w_values.shape[0], narrow), BF16),
            pltpu.VMEM((narrow, width), F32),
        ],
        compiler_params=pltpu.CompilerParams(
            collective_id=0, has_side_effects=True, vmem_limit_bytes=60 * 1024 * 1024
        ),
    )(
        hidden,
        w_values,
        w_gates,
        w_states,
        w_steps.T,
        conv_weight,
        conv_bias.reshape(-1, narrow),
        norm_gain.reshape(-1, narrow),
        step_bias,
        decay_rate,
        skip_gain,
        lengths,
    )
    return gated_out, final.reshape(1, count, width // count, narrow)


def on_device(
    hidden,
    w_values,
    w_gates,
    w_steps,
    w_states,
    conv_weight,
    conv_bias,
    step_bias,
    decay_rate,
    skip_gain,
    norm_gain,
    lengths,
):
    groups = lax.axis_size("head")
    if lax.axis_size("seq") == 8 and groups == 4:
        return layer(
            hidden,
            w_values,
            w_gates,
            w_steps,
            w_states,
            conv_weight,
            conv_bias,
            step_bias,
            decay_rate,
            skip_gain,
            norm_gain,
            lengths,
        )
    group_index = lax.axis_index("head")
    block_index = lax.axis_index("seq")
    local_width = w_values.shape[1]
    inner_width = local_width * groups
    local_heads = decay_rate.shape[0]
    head_width = local_width // local_heads
    state_width = w_states.shape[1] // 2
    conv_taps = conv_weight.shape[0]
    prompt_ends = jnp.cumsum(lengths)
    block_hidden = lax.all_gather(hidden, "head", axis=0, tiled=True)
    block_rows = block_hidden.shape[0]
    sub_rows = block_rows // groups

    def contract(piece):
        return jnp.dot(block_hidden, piece, preferred_element_type=jnp.float32)

    pieces = (
        lax.all_gather(w_values, "seq", axis=0, tiled=True),
        lax.all_gather(w_states, "seq", axis=0, tiled=True),
        lax.all_gather(w_steps, "seq", axis=0, tiled=True),
        lax.all_gather(w_gates, "seq", axis=0, tiled=True),
    )
    values_sum, states_sum, steps_sum, gates_sum = tuple((contract(piece) for piece in pieces))
    pre_rows = jnp.concatenate(
        [values_sum.astype(jnp.bfloat16), states_sum.astype(jnp.bfloat16)], axis=1
    )
    local_taps = jnp.concatenate(
        [
            lax.dynamic_slice_in_dim(conv_weight, group_index * local_width, local_width, 1),
            conv_weight[:, inner_width:],
        ],
        axis=1,
    )
    local_bias = jnp.concatenate(
        [
            lax.dynamic_slice_in_dim(conv_bias, group_index * local_width, local_width, 0),
            conv_bias[inner_width:],
        ],
        axis=0,
    )
    block_start = block_index * block_rows
    rim_rows = pre_rows[block_rows - (conv_taps - 1) :]
    prior_rim = from_behind(rim_rows, "seq", 1)
    extended = jnp.concatenate([prior_rim, pre_rows], axis=0)
    ext_positions = (
        block_start - (conv_taps - 1) + jnp.arange(block_rows + conv_taps - 1, dtype=jnp.int32)
    )
    ext_ids = segments_at(ext_positions, prompt_ends)
    own_ids = ext_ids[conv_taps - 1 :]
    filtered = jnp.zeros(pre_rows.shape, jnp.float32) + local_bias[None, :]
    for offset in range(conv_taps):
        matches = (ext_ids[offset : offset + block_rows] == own_ids).astype(jnp.float32)
        filtered = (
            filtered
            + local_taps[offset][None, :]
            * extended[offset : offset + block_rows].astype(jnp.float32)
            * matches[:, None]
        )
    conv_out = jax.nn.silu(filtered).astype(jnp.bfloat16)
    head_values = conv_out[:, :local_width]
    both_states = conv_out[:, local_width:]
    stretch_rows = STRETCH
    stretches = block_rows // stretch_rows
    positions = block_start + jnp.arange(block_rows, dtype=jnp.int32)
    segment_ids = segments_at(positions, prompt_ends)
    next_ids = segments_at(positions + 1, prompt_ends)
    before_ids = segments_at(positions - 1, prompt_ends)
    stretch_ids = segment_ids.reshape(stretches, stretch_rows)
    prior_ids = before_ids.reshape(stretches, stretch_rows)[:, 0]
    ends_mask = (segment_ids != next_ids).reshape(stretches, stretch_rows)
    step_sizes = jax.nn.softplus(steps_sum + step_bias[None, :])
    decay_steps = step_sizes * decay_rate[None, :]
    log_decay = -jnp.cumsum(decay_steps.reshape(stretches, stretch_rows, local_heads), axis=1)
    decay_heads = jnp.swapaxes(log_decay, 1, 2)
    step_heads = jnp.swapaxes(step_sizes.reshape(stretches, stretch_rows, local_heads), 1, 2)
    values = head_values.reshape(stretches, stretch_rows, local_heads, head_width)
    write_state = both_states[:, :state_width].reshape(stretches, stretch_rows, state_width)
    read_state = both_states[:, state_width:].reshape(stretches, stretch_rows, state_width)
    intersection = jnp.einsum(
        "ctn,csn->cts", read_state, write_state, preferred_element_type=jnp.float32
    )
    token_order = jnp.arange(stretch_rows, dtype=jnp.int32)
    causal = token_order[:, None] >= token_order[None, :]
    allowed = causal[None] & (stretch_ids[:, :, None] == stretch_ids[:, None, :])
    spread = decay_heads[:, :, :, None] - decay_heads[:, :, None, :]
    weights = (
        jnp.where(allowed[:, None], jnp.exp(jnp.minimum(spread, 0.0)), 0.0)
        * step_heads[:, :, None, :]
    )
    scores = (intersection[:, None] * weights).astype(jnp.bfloat16)
    within_stretch = jnp.einsum(
        "chts,cshp->cthp", scores, values, preferred_element_type=jnp.float32
    )
    last_ids = stretch_ids[:, -1]
    tail_decay = decay_heads[:, :, -1:]
    keep_tail = (stretch_ids == last_ids[:, None])[:, None, :]
    tail_coef = (
        jnp.where(keep_tail, jnp.exp(jnp.minimum(tail_decay - decay_heads, 0.0)), 0.0) * step_heads
    )
    tail_rows = (values.astype(jnp.float32) * jnp.swapaxes(tail_coef, 1, 2)[:, :, :, None]).astype(
        jnp.bfloat16
    )
    stretch_states = jnp.einsum(
        "clhp,cln->chpn", tail_rows, write_state, preferred_element_type=jnp.float32
    )
    stretch_gates = (
        jnp.exp(decay_heads[:, :, -1]) * (last_ids == prior_ids).astype(jnp.float32)[:, None]
    )
    block_gate = jnp.ones((local_heads,), jnp.float32)
    block_state = jnp.zeros((local_heads, head_width, state_width), jnp.float32)
    block_state = stretch_gates[0][:, None, None] * block_state + stretch_states[0]
    block_gate = block_gate * stretch_gates[0]

    def compose(earlier, later):
        return (earlier[0] * later[0], later[0][:, None, None] * earlier[1] + later[1])

    identity_pair = (jnp.ones_like(block_gate), jnp.zeros_like(block_state))
    carried = prefix((block_gate, block_state), "seq", compose, identity_pair)
    incoming = carried[1]
    arriving = []
    arriving.append(incoming)
    arriving = jnp.stack(arriving)
    carry_mask = (stretch_ids == prior_ids[:, None]).astype(jnp.float32)
    carry_decay = jnp.exp(log_decay) * carry_mask[:, :, None]
    from_before = (
        jnp.einsum(
            "cln,chpn->clhp",
            read_state,
            arriving.astype(jnp.bfloat16),
            preferred_element_type=jnp.float32,
        )
        * carry_decay[:, :, :, None]
    )
    result = (
        within_stretch + from_before + skip_gain[None, None, :, None] * values.astype(jnp.float32)
    )
    ssm_rows = result.reshape(block_rows, local_width).astype(jnp.bfloat16)
    end_weight = ends_mask.astype(jnp.float32)
    has_end = jnp.sum(end_weight, axis=1)
    end_decay = jnp.sum(decay_heads * end_weight[:, None, :], axis=2)
    end_ids = jnp.sum(jnp.where(ends_mask, stretch_ids, 0), axis=1)
    keep_end = ((stretch_ids == end_ids[:, None]) & (has_end[:, None] > 0))[:, None, :]
    end_coef = (
        jnp.where(keep_end, jnp.exp(jnp.minimum(end_decay[:, :, None] - decay_heads, 0.0)), 0.0)
        * step_heads
    )
    end_rows = (values.astype(jnp.float32) * jnp.swapaxes(end_coef, 1, 2)[:, :, :, None]).astype(
        jnp.bfloat16
    )
    end_states = jnp.einsum(
        "clhp,cln->chpn", end_rows, write_state, preferred_element_type=jnp.float32
    )
    end_carry = (
        jnp.exp(end_decay) * ((end_ids == prior_ids) & (has_end > 0)).astype(jnp.float32)[:, None]
    )
    end_states = end_states + end_carry[:, :, None, None] * arriving
    final_block = jnp.sum(end_states, axis=0)[None]
    head_gates = gates_sum.astype(jnp.bfloat16)
    norm_slice = lax.dynamic_slice_in_dim(norm_gain, group_index * local_width, local_width)
    gated = ssm_rows.astype(jnp.float32) * jax.nn.silu(head_gates.astype(jnp.float32))
    squares = lax.psum(jnp.sum(gated * gated, axis=1), "head")
    scaled = gated * lax.rsqrt(squares / inner_width + epsilon)[:, None] * norm_slice[None, :]
    outgoing = scaled.astype(jnp.bfloat16)
    returned = lax.all_to_all(
        outgoing.reshape(groups, sub_rows, local_width),
        "head",
        split_axis=0,
        concat_axis=2,
        tiled=True,
    )
    gated_out = returned.reshape(sub_rows, inner_width)
    return (gated_out, final_block)


def solution(mesh):
    in_specs = (
        P(("seq", "head"), None),
        P("seq", "head"),
        P("seq", "head"),
        P("seq", "head"),
        P("seq", None),
        P(),
        P(),
        P("head"),
        P("head"),
        P("head"),
        P(),
        P(),
    )
    out_specs = (P(("seq", "head"), None), P("seq", "head", None, None))
    return jax.shard_map(
        on_device, mesh=mesh, in_specs=in_specs, out_specs=out_specs, check_vma=False
    )
```

```python
import jax
import jax.numpy as jnp
from jax import lax
from jax.experimental import pallas as pl
from jax.experimental.pallas import tpu as pltpu
from jax.sharding import PartitionSpec as P

STRETCH = 256


epsilon = 1e-05


def from_behind(block, axis, distance):
    devices = range(lax.axis_size(axis))
    route = [(i - distance, i) for i in devices if i - distance in devices]
    return lax.ppermute(block, axis, route)


def prefix(value, axis, join, neutral):
    place = lax.axis_index(axis)
    gathered = jax.tree.map(
        lambda a, kind: lax.all_gather(a.astype(kind), axis), value, (jnp.bfloat16, jnp.bfloat16)
    )
    state = jax.tree.map(lambda a, e: jnp.zeros_like(a) + jnp.asarray(e, a.dtype), value, neutral)

    def one(turn, state):
        return join(
            state,
            jax.tree.map(
                lambda a, own: lax.dynamic_index_in_dim(a, turn, 0, False).astype(own.dtype),
                gathered,
                value,
            ),
        )

    return lax.fori_loop(0, place, one, state)


def segments_at(positions, prompt_ends):
    counted = jnp.sum((prompt_ends[None, :] <= positions[:, None]).astype(jnp.int32), axis=1)
    return jnp.where(positions < 0, -1, counted)


MESH = pl.DeviceIdType.MESH
BF16 = jnp.bfloat16
F32 = jnp.float32


def rdma(src, dst, send_sem, recv_sem, seq, head):
    return pltpu.make_async_remote_copy(
        src_ref=src,
        dst_ref=dst,
        send_sem=send_sem,
        recv_sem=recv_sem,
        device_id=(seq, head),
        device_id_type=MESH,
    )


def layer_kernel(
    hidden_ref,
    values_ref,
    gates_ref,
    states_ref,
    steps_ref,
    taps_ref,
    offset_ref,
    norm_ref,
    bias_ref,
    decay_ref,
    skip_ref,
    lengths_ref,
    out_ref,
    final_ref,
    hid,
    wbuf,
    out_v,
    out_s,
    out_g,
    in_v,
    in_s,
    in_g,
    own,
    tile,
    tiles,
    local_sem,
    hid_send,
    hid_recv,
    w_send,
    w_recv,
    part_send,
    part_recv,
    tile_send,
    tile_recv,
    halo_out,
    halo_in,
    ext,
    conv,
    cum_ref,
    cum_rows,
    dt_rows,
    carry_ref,
    end_ref,
    y_ref,
    inc,
    local_out,
    gate_out,
    local_in,
    gate_in,
    gated,
    whole,
    halo_send,
    halo_recv,
    state_send,
    state_recv,
    turn_send,
    turn_recv,
    small_ref,
    local_f32,
):
    s = lax.axis_index("seq")
    h = lax.axis_index("head")
    z = lax.div(s, 2)
    x = lax.rem(s, 2)
    z_lo = lax.rem(z, 2)
    z_hi = lax.div(z, 2)
    beside = s + 1 - 2 * x
    partner = s + 2 - 4 * z_lo
    far = s + 4 - 8 * z_hi
    heads = [lax.rem(h + d, 4) for d in (1, 2, 3)]
    rows_w = values_ref.shape[0]
    rows_h = hidden_ref.shape[0]
    depth = 2 * rows_w
    width = values_ref.shape[1]
    narrow = small_ref.shape[1]
    count_heads = steps_ref.shape[0]

    share = narrow // 2
    barrier = pltpu.get_barrier_semaphore()
    for d in range(1, 8):
        pl.semaphore_signal(
            barrier, inc=1, device_id=(lax.rem(s + d, 8), h), device_id_type=MESH
        )
    for to in heads:
        pl.semaphore_signal(barrier, inc=1, device_id=(s, to), device_id_type=MESH)

    wide_states = states_ref[
        :, pl.ds(pl.multiple_of(lax.div(h, 2) * narrow, 128), narrow)
    ].astype(F32)
    turned_states = pltpu.roll(wide_states, share, 1)
    place = (
        lax.broadcasted_iota(jnp.int32, (count_heads, narrow), 1)
        == lax.broadcasted_iota(jnp.int32, (count_heads, narrow), 0) + share
    )
    step_columns = lax.dot_general(
        steps_ref[...],
        place.astype(F32).astype(BF16),
        (((0,), (0,)), ((), ())),
        preferred_element_type=F32,
    )
    small_ref[...] = jnp.where(
        lax.broadcasted_iota(jnp.int32, small_ref.shape, 1) < share,
        jnp.where(lax.rem(h, 2) == 1, turned_states, wide_states),
        step_columns,
    ).astype(BF16)

    my_rows = pl.ds(pl.multiple_of(x * rows_w, 64), rows_w)
    my_tokens = pl.ds(pl.multiple_of(h * rows_h, 64), rows_h)
    cuts = (0, 2 * narrow, width)
    gate_cuts = (0, 2 * narrow, 4 * narrow, width)
    pieces = [(small_ref, 0, width, narrow)]
    pieces += [(values_ref, a, a, b - a) for a, b in zip(cuts, cuts[1:])]
    pieces += [
        (gates_ref, a, width + narrow + a, b - a) for a, b in zip(gate_cuts, gate_cuts[1:])
    ]
    sources = [ref.at[:, pl.ds(a, size)] for ref, a, _, size in pieces]
    windows = [pl.ds(at, size) for _, _, at, size in pieces]
    number = len(pieces)

    def columns(low, zh):
        return pl.ds(pl.multiple_of((low + 2 * zh) * depth, 128), depth)

    local = []
    for p in range(number):
        local.append(
            pltpu.make_async_copy(
                sources[p], wbuf.at[z_hi, my_rows, windows[p]], local_sem.at[p]
            )
        )
    for zh in range(2):
        local.append(
            pltpu.make_async_copy(
                hidden_ref.at[:, columns(z_lo, zh)],
                hid.at[0, zh, my_tokens],
                local_sem.at[number + zh],
            )
        )
    for c in local:
        c.start()
    pl.semaphore_wait(barrier, 10)

    to_far = [
        rdma(sources[p], wbuf.at[z_hi, my_rows, windows[p]], w_send.at[0, p], w_recv.at[0, p], far, h)
        for p in range(number)
    ]
    to_beside = [
        rdma(sources[p], wbuf.at[z_hi, my_rows, windows[p]], w_send.at[1, p], w_recv.at[1, p], beside, h)
        for p in range(number)
    ]
    passed = [
        rdma(
            wbuf.at[1 - z_hi, my_rows, windows[p]],
            wbuf.at[1 - z_hi, my_rows, windows[p]],
            w_send.at[2, p],
            w_recv.at[2, p],
            beside,
            h,
        )
        for p in range(number)
    ]
    hid_over = [
        rdma(
            hidden_ref.at[:, columns(1 - z_lo, zh)],
            hid.at[1, zh, my_tokens],
            hid_send.at[0, zh],
            hid_recv.at[0, zh],
            partner,
            h,
        )
        for zh in range(2)
    ]
    hid_own = [
        rdma(
            hidden_ref.at[:, columns(z_lo, zh)],
            hid.at[0, zh, my_tokens],
            hid_send.at[1 + d, zh],
            hid_recv.at[1 + d, zh],
            s,
            heads[d],
        )
        for zh in range(2)
        for d in range(3)
    ]
    hid_pass = [
        rdma(
            hid.at[1, zh, my_tokens],
            hid.at[1, zh, my_tokens],
            hid_send.at[4 + d, zh],
            hid_recv.at[4 + d, zh],
            s,
            heads[d],
        )
        for zh in range(2)
        for d in range(3)
    ]
    for c in hid_over:
        c.start()
    for p in range(3):
        to_far[p].start()
        to_beside[p].start()
    for c in hid_own:
        c.start()
    for zh in range(2):
        hid_over[zh].wait_recv()
        for d in range(3):
            hid_pass[3 * zh + d].start()

    def forward(p):
        to_far[p].wait_recv()
        passed[p].start()
        if p + 3 < number:
            to_far[p + 3].start()
            to_beside[p + 3].start()

    def landed(p):
        to_beside[p].wait_recv()
        passed[p].wait_recv()

    def product(which, window):
        return jnp.dot(
            hid[which, 0], wbuf[0, :, window], preferred_element_type=F32
        ) + jnp.dot(hid[which, 1], wbuf[1, :, window], preferred_element_type=F32)

    def span_of(p):
        _, a, _, size = pieces[p]
        return slice(a, a + size)

    def to_partner(p, out, arriving):
        landed(p)
        span = span_of(p)
        out[:, span] = product(1, windows[p]).astype(out.dtype)
        part = rdma(
            out.at[:, span], arriving.at[:, span], part_send.at[p], part_recv.at[p], partner, h
        )
        part.start()
        return part

    for p in range(3):
        forward(p)
    for c in local:
        c.wait()
    for c in hid_own:
        c.wait_recv()
    for c in hid_pass:
        c.wait_recv()
    part_s = to_partner(0, out_s, in_s)
    part_v = [to_partner(1, out_v, in_v)]
    forward(3)
    part_v.append(to_partner(2, out_v, in_v))
    small = product(0, windows[0])
    part_s.wait_recv()
    small = small + in_s[...].astype(F32)
    tile[...] = small.astype(BF16)
    tiles_out = [
        rdma(tile, tiles.at[h], tile_send.at[d], tile_recv.at[d], s, heads[d]) for d in range(3)
    ]
    for c in tiles_out:
        c.start()
    tiles[h] = tile[...]
    for p in (1, 2):
        own[:, span_of(p)] = product(0, windows[p])
    forward(4)

    rows = own.shape[0]
    start = s * rows
    count = lengths_ref.shape[0]
    ends = []
    for i in range(count):
        ends.append(lengths_ref[i] + (ends[i - 1] if i else 0))

    def segment(position):
        found = jnp.where(position < 0, -1, 0)
        for end in ends:
            found = found + jnp.where(end <= position, 1, 0)
        return found

    last_id = segment(start + rows - 1)
    prior_id = segment(start - 1)
    end_id = jnp.int32(-2)
    end_row = jnp.int32(-1)
    for i, end in enumerate(ends):
        inside = (end - 1 >= start) & (end - 1 < start + rows)
        end_id = jnp.where(inside, i, end_id)
        end_row = jnp.where(inside, end - 1 - start, end_row)

    order = lax.broadcasted_iota(jnp.int32, (rows, rows), 0)
    across = lax.broadcasted_iota(jnp.int32, (rows, rows), 1)
    lower = order >= across
    lower_ones = lower.astype(F32).astype(BF16)
    lane = lax.broadcasted_iota(jnp.int32, (rows, narrow), 1)
    token = lax.broadcasted_iota(jnp.int32, (rows, narrow), 0)
    ids = segment(start + token)

    def parts(value, number):
        taken = []
        for _ in range(number):
            piece = value.astype(BF16)
            taken.append(piece)
            value = value - piece.astype(F32)
        return taken

    head_lane = lax.broadcasted_iota(jnp.int32, (8, narrow), 1) - share

    def over_lanes(ref):
        row = jnp.zeros((8, narrow), F32)
        for i in range(count_heads):
            row = jnp.where(head_lane == i, ref[i], row)
        return row

    step = jax.nn.softplus(small + over_lanes(bias_ref)[0:1, :])
    rate = step * over_lanes(decay_ref)[0:1, :]
    cum = jnp.zeros((rows, narrow), F32)
    for piece in parts(rate, 3):
        cum = cum - jnp.dot(lower_ones, piece, preferred_element_type=F32)
    cum_ref[...] = cum
    cum_rows[...] = cum.T
    dt_rows[...] = step.T
    head_row = lax.broadcasted_iota(jnp.int32, (narrow, width), 0) - share
    channel = lax.broadcasted_iota(jnp.int32, (narrow, width), 1)
    spread = (
        ((channel >= head_row * share) & (channel < head_row * share + share))
        .astype(F32)
        .astype(BF16)
    )

    def expand(value, number):
        total = None
        for piece in parts(value, number):
            term = jnp.dot(piece, spread, preferred_element_type=F32)
            total = term if total is None else total + term
        return total

    cum_last = cum[rows - 1 : rows, :]
    cum_end = jnp.sum(jnp.where(token == end_row, cum, 0.0), axis=0, keepdims=True)
    gate_row = jnp.where(last_id == prior_id, jnp.exp(cum_last), 0.0)
    end_gate = jnp.where(end_id == prior_id, jnp.exp(cum_end), 0.0)
    eight = lax.broadcasted_iota(jnp.int32, (8, narrow), 0)
    rows8 = jnp.where(
        eight == 0,
        gate_row,
        jnp.where(eight == 1, end_gate, jnp.where(eight == 2, over_lanes(skip_ref), 0.0)),
    )
    wide8 = expand(rows8, 3)
    gate_out[...] = wide8
    tail = jnp.where(ids == last_id, jnp.exp(jnp.minimum(cum_last - cum, 0.0)), 0.0) * step
    tail_wide = expand(tail, 2)
    end_ref[...] = expand(
        jnp.where(ids == end_id, jnp.exp(jnp.minimum(cum_end - cum, 0.0)), 0.0) * step, 2
    )
    carry_ref[...] = expand(jnp.where(ids == prior_id, jnp.exp(cum), 0.0), 2)

    forward(5)
    for c in part_v:
        c.wait_recv()
    pre = (own[...] + in_v[...].astype(F32)).astype(BF16)
    ext[8:, 0:width] = pre.astype(F32)
    halo_out[:, 0:width] = pre[rows - 16 :, :]
    for c in tiles_out:
        c.wait_recv()
    for half in range(2):
        first = tiles[2 * half].astype(F32)
        second = pltpu.roll(tiles[2 * half + 1].astype(F32), share, 1)
        both = jnp.where(lane < share, first, second)
        low = width + half * narrow
        ext[8:, low : low + narrow] = both
        halo_out[:, low : low + narrow] = both[rows - 16 :, :].astype(BF16)
    halo = rdma(
        halo_out, halo_in, halo_send.at[0], halo_recv.at[0], lax.rem(s + 1, 8), h
    )
    halo.start()

    part_g = [to_partner(3, out_g, in_g)]
    own[:, span_of(3)] = product(0, windows[3])

    halo.wait_recv()
    ext[0:8, :] = halo_in[8:16, :].astype(F32)
    inner = 4 * width
    same = [
        (segment(start + token - d) == ids).astype(F32) for d in range(3, 0, -1)
    ]
    chunks = (width + 2 * narrow) // narrow
    for j in range(chunks):
        low = j * narrow
        if low < width:
            from_lane = pl.ds(pl.multiple_of(h * width + low, 128), narrow)
            offset = offset_ref[pl.ds(h * (width // narrow) + j, 1), :]
        else:
            from_lane = pl.ds(inner + low - width, narrow)
            offset = offset_ref[pl.ds((inner + low - width) // narrow, 1), :]
        taps = taps_ref[:, from_lane]
        total = jnp.zeros((rows, narrow), F32) + offset
        for tap in range(4):
            piece = ext[5 + tap : 5 + tap + rows, low : low + narrow] * taps[tap : tap + 1, :]
            total = total + (piece * same[tap] if tap < 3 else piece)
        conv[:, low : low + narrow] = jax.nn.silu(total).astype(BF16)

    values = conv[:, 0:width]
    write_turned = conv[:, width : width + narrow].astype(F32).T.astype(BF16)
    read_state = conv[:, width + narrow :]
    local = jnp.dot(
        write_turned,
        (values.astype(F32) * tail_wide).astype(BF16),
        preferred_element_type=F32,
    )
    local_f32[...] = local
    local_out[0] = local.astype(BF16)
    next_one = (
        rdma(
            local_out.at[0], local_in.at[0], state_send.at[0], state_recv.at[0], lax.rem(s + 1, 8), h
        ),
        rdma(gate_out, gate_in, state_send.at[1], state_recv.at[1], lax.rem(s + 1, 8), h),
    )
    next_two = rdma(
        local_out.at[1], local_in.at[1], state_send.at[2], state_recv.at[2], lax.rem(s + 2, 8), h
    )

    @pl.when(s < 7)
    def _():
        for c in next_one:
            c.start()

    part_g.append(to_partner(4, out_g, in_g))
    own[:, span_of(4)] = product(0, windows[4])
    inc[...] = jnp.zeros(inc.shape, F32)

    @pl.when(s > 0)
    def _():
        for c in next_one:
            c.wait_recv()
        inc[...] = local_in[0].astype(F32)

    @pl.when(s < 6)
    def _():
        local_out[1] = (local_f32[...] + wide8[0:1, :] * inc[...]).astype(BF16)
        next_two.start()

    met = jnp.where(
        lower & (segment(start + order) == segment(start + across)),
        jnp.dot(read_state, write_turned, preferred_element_type=F32),
        0.0,
    )
    pairs = width // narrow
    for j in range(pairs):
        pair = conv[:, j * narrow : (j + 1) * narrow]
        halves = []
        for a in range(2):
            at = share + 2 * j + a
            decay = cum_ref[:, at : at + 1] - cum_rows[at : at + 1, :]
            scores = met * jnp.exp(jnp.minimum(decay, 0.0)) * dt_rows[at : at + 1, :]
            halves.append(jnp.dot(scores.astype(BF16), pair, preferred_element_type=F32))
        y_ref[:, j * narrow : (j + 1) * narrow] = jnp.where(lane < share, halves[0], halves[1])
    end_local = jnp.dot(
        write_turned,
        (values.astype(F32) * end_ref[...]).astype(BF16),
        preferred_element_type=F32,
    )

    part_g.append(to_partner(5, out_g, in_g))
    own[:, span_of(5)] = product(0, windows[5])

    @pl.when(s > 1)
    def _():
        next_two.wait_recv()
        inc[...] += gate_in[0:1, :] * local_in[1].astype(F32)

    for c in part_g:
        c.wait_recv()
    for j in range(pairs):
        span = slice(j * narrow, (j + 1) * narrow)
        state = inc[:, span]
        final_ref[span, :] = (end_local[:, span] + wide8[1:2, span] * state).T
        before = jnp.dot(read_state, state.astype(BF16), preferred_element_type=F32)
        y = (
            y_ref[:, span]
            + before * carry_ref[:, span]
            + wide8[2:3, span] * conv[:, span].astype(F32)
        ).astype(BF16)
        gate = (own[:, span] + in_g[:, span].astype(F32)).astype(BF16).astype(F32)
        gated[:, span] = (y.astype(F32) * jax.nn.silu(gate)).astype(BF16)

    my_columns = pl.ds(pl.multiple_of(h * width, 128), width)
    turned = [
        rdma(
            gated.at[pl.ds(pl.multiple_of(heads[d] * rows_h, 64), rows_h)],
            whole.at[:, my_columns],
            turn_send.at[d],
            turn_recv.at[d],
            s,
            heads[d],
        )
        for d in range(3)
    ]
    for c in turned:
        c.start()
    keep = pltpu.make_async_copy(gated.at[my_tokens], whole.at[:, my_columns], local_sem.at[number + 2])
    keep.start()
    keep.wait()
    for c in turned:
        c.wait_recv()
    full = whole[...].astype(F32)
    mean = jnp.sum(full * full, axis=1, keepdims=True) / inner
    scale = lax.rsqrt(mean + epsilon)
    for j in range(inner // narrow):
        span = slice(j * narrow, (j + 1) * narrow)
        out_ref[:, span] = (
            whole[:, span].astype(F32) * scale * norm_ref[j : j + 1, :]
        ).astype(BF16)

    for c in [*to_far, *to_beside, *passed, *hid_over, *hid_own, *hid_pass, *tiles_out, *turned]:
        c.wait_send()
    for c in [part_s, *part_v, *part_g, halo]:
        c.wait_send()

    @pl.when(s < 7)
    def _():
        for c in next_one:
            c.wait_send()

    @pl.when(s < 6)
    def _():
        next_two.wait_send()


def layer(
    hidden,
    w_values,
    w_gates,
    w_steps,
    w_states,
    conv_weight,
    conv_bias,
    step_bias,
    decay_rate,
    skip_gain,
    norm_gain,
    lengths,
):
    rows = hidden.shape[0] * 4
    width = w_values.shape[1]
    count = step_bias.shape[0]
    narrow = w_states.shape[1] // 2
    inner = norm_gain.shape[0]
    depth = 2 * w_values.shape[0]
    channels = width + 2 * narrow
    vmem = pl.BlockSpec(memory_space=pltpu.VMEM)
    smem = pl.BlockSpec(memory_space=pltpu.SMEM)
    anywhere = pl.BlockSpec(memory_space=pl.ANY)
    dma = pltpu.SemaphoreType.DMA
    gated_out, final = pl.pallas_call(
        layer_kernel,
        out_shape=(
            jax.ShapeDtypeStruct(hidden.shape, BF16),
            jax.ShapeDtypeStruct((width, narrow), F32),
        ),
        in_specs=[anywhere] * 3 + [vmem] * 5 + [smem] * 4,
        out_specs=[vmem] * 2,
        scratch_shapes=[
            pltpu.VMEM((2, 2, rows, depth), BF16),
            pltpu.VMEM((2, depth, 2 * width + narrow), BF16),
            pltpu.VMEM((rows, width), BF16),
            pltpu.VMEM((rows, narrow), BF16),
            pltpu.VMEM((rows, width), BF16),
            pltpu.VMEM((rows, width), BF16),
            pltpu.VMEM((rows, narrow), BF16),
            pltpu.VMEM((rows, width), BF16),
            pltpu.VMEM((rows, width), F32),
            pltpu.VMEM((rows, narrow), BF16),
            pltpu.VMEM((4, rows, narrow), BF16),
            dma((9,)),
            dma((7, 2)),
            dma((7, 2)),
            dma((3, 6)),
            dma((3, 6)),
            dma((6,)),
            dma((6,)),
            dma((3,)),
            dma((3,)),
            pltpu.VMEM((16, channels), BF16),
            pltpu.VMEM((16, channels), BF16),
            pltpu.VMEM((8 + rows, channels), F32),
            pltpu.VMEM((rows, channels), BF16),
            pltpu.VMEM((rows, narrow), F32),
            pltpu.VMEM((narrow, rows), F32),
            pltpu.VMEM((narrow, rows), F32),
            pltpu.VMEM((rows, width), F32),
            pltpu.VMEM((rows, width), F32),
            pltpu.VMEM((rows, width), F32),
            pltpu.VMEM((narrow, width), F32),
            pltpu.VMEM((2, narrow, width), BF16),
            pltpu.VMEM((8, width), F32),
            pltpu.VMEM((2, narrow, width), BF16),
            pltpu.VMEM((8, width), F32),
            pltpu.VMEM((rows, width), BF16),
            pltpu.VMEM(hidden.shape, BF16),
            dma((1,)),
            dma((1,)),
            dma((3,)),
            dma((3,)),
            dma((3,)),
            dma((3,)),
            pltpu.VMEM((w_values.shape[0], narrow), BF16),
            pltpu.VMEM((narrow, width), F32),
        ],
        compiler_params=pltpu.CompilerParams(
            collective_id=0, has_side_effects=True, vmem_limit_bytes=60 * 1024 * 1024
        ),
    )(
        hidden,
        w_values,
        w_gates,
        w_states,
        w_steps.T,
        conv_weight,
        conv_bias.reshape(-1, narrow),
        norm_gain.reshape(-1, narrow),
        step_bias,
        decay_rate,
        skip_gain,
        lengths,
    )
    return gated_out, final.reshape(1, count, width // count, narrow)


def on_device(
    hidden,
    w_values,
    w_gates,
    w_steps,
    w_states,
    conv_weight,
    conv_bias,
    step_bias,
    decay_rate,
    skip_gain,
    norm_gain,
    lengths,
):
    groups = lax.axis_size("head")
    if lax.axis_size("seq") == 8 and groups == 4:
        return layer(
            hidden,
            w_values,
            w_gates,
            w_steps,
            w_states,
            conv_weight,
            conv_bias,
            step_bias,
            decay_rate,
            skip_gain,
            norm_gain,
            lengths,
        )
    group_index = lax.axis_index("head")
    block_index = lax.axis_index("seq")
    local_width = w_values.shape[1]
    inner_width = local_width * groups
    local_heads = decay_rate.shape[0]
    head_width = local_width // local_heads
    state_width = w_states.shape[1] // 2
    conv_taps = conv_weight.shape[0]
    prompt_ends = jnp.cumsum(lengths)
    block_hidden = lax.all_gather(hidden, "head", axis=0, tiled=True)
    block_rows = block_hidden.shape[0]
    sub_rows = block_rows // groups

    def contract(piece):
        return jnp.dot(block_hidden, piece, preferred_element_type=jnp.float32)

    pieces = (
        lax.all_gather(w_values, "seq", axis=0, tiled=True),
        lax.all_gather(w_states, "seq", axis=0, tiled=True),
        lax.all_gather(w_steps, "seq", axis=0, tiled=True),
        lax.all_gather(w_gates, "seq", axis=0, tiled=True),
    )
    values_sum, states_sum, steps_sum, gates_sum = tuple((contract(piece) for piece in pieces))
    pre_rows = jnp.concatenate(
        [values_sum.astype(jnp.bfloat16), states_sum.astype(jnp.bfloat16)], axis=1
    )
    local_taps = jnp.concatenate(
        [
            lax.dynamic_slice_in_dim(conv_weight, group_index * local_width, local_width, 1),
            conv_weight[:, inner_width:],
        ],
        axis=1,
    )
    local_bias = jnp.concatenate(
        [
            lax.dynamic_slice_in_dim(conv_bias, group_index * local_width, local_width, 0),
            conv_bias[inner_width:],
        ],
        axis=0,
    )
    block_start = block_index * block_rows
    rim_rows = pre_rows[block_rows - (conv_taps - 1) :]
    prior_rim = from_behind(rim_rows, "seq", 1)
    extended = jnp.concatenate([prior_rim, pre_rows], axis=0)
    ext_positions = (
        block_start - (conv_taps - 1) + jnp.arange(block_rows + conv_taps - 1, dtype=jnp.int32)
    )
    ext_ids = segments_at(ext_positions, prompt_ends)
    own_ids = ext_ids[conv_taps - 1 :]
    filtered = jnp.zeros(pre_rows.shape, jnp.float32) + local_bias[None, :]
    for offset in range(conv_taps):
        matches = (ext_ids[offset : offset + block_rows] == own_ids).astype(jnp.float32)
        filtered = (
            filtered
            + local_taps[offset][None, :]
            * extended[offset : offset + block_rows].astype(jnp.float32)
            * matches[:, None]
        )
    conv_out = jax.nn.silu(filtered).astype(jnp.bfloat16)
    head_values = conv_out[:, :local_width]
    both_states = conv_out[:, local_width:]
    stretch_rows = STRETCH
    stretches = block_rows // stretch_rows
    positions = block_start + jnp.arange(block_rows, dtype=jnp.int32)
    segment_ids = segments_at(positions, prompt_ends)
    next_ids = segments_at(positions + 1, prompt_ends)
    before_ids = segments_at(positions - 1, prompt_ends)
    stretch_ids = segment_ids.reshape(stretches, stretch_rows)
    prior_ids = before_ids.reshape(stretches, stretch_rows)[:, 0]
    ends_mask = (segment_ids != next_ids).reshape(stretches, stretch_rows)
    step_sizes = jax.nn.softplus(steps_sum + step_bias[None, :])
    decay_steps = step_sizes * decay_rate[None, :]
    log_decay = -jnp.cumsum(decay_steps.reshape(stretches, stretch_rows, local_heads), axis=1)
    decay_heads = jnp.swapaxes(log_decay, 1, 2)
    step_heads = jnp.swapaxes(step_sizes.reshape(stretches, stretch_rows, local_heads), 1, 2)
    values = head_values.reshape(stretches, stretch_rows, local_heads, head_width)
    write_state = both_states[:, :state_width].reshape(stretches, stretch_rows, state_width)
    read_state = both_states[:, state_width:].reshape(stretches, stretch_rows, state_width)
    intersection = jnp.einsum(
        "ctn,csn->cts", read_state, write_state, preferred_element_type=jnp.float32
    )
    token_order = jnp.arange(stretch_rows, dtype=jnp.int32)
    causal = token_order[:, None] >= token_order[None, :]
    allowed = causal[None] & (stretch_ids[:, :, None] == stretch_ids[:, None, :])
    spread = decay_heads[:, :, :, None] - decay_heads[:, :, None, :]
    weights = (
        jnp.where(allowed[:, None], jnp.exp(jnp.minimum(spread, 0.0)), 0.0)
        * step_heads[:, :, None, :]
    )
    scores = (intersection[:, None] * weights).astype(jnp.bfloat16)
    within_stretch = jnp.einsum(
        "chts,cshp->cthp", scores, values, preferred_element_type=jnp.float32
    )
    last_ids = stretch_ids[:, -1]
    tail_decay = decay_heads[:, :, -1:]
    keep_tail = (stretch_ids == last_ids[:, None])[:, None, :]
    tail_coef = (
        jnp.where(keep_tail, jnp.exp(jnp.minimum(tail_decay - decay_heads, 0.0)), 0.0) * step_heads
    )
    tail_rows = (values.astype(jnp.float32) * jnp.swapaxes(tail_coef, 1, 2)[:, :, :, None]).astype(
        jnp.bfloat16
    )
    stretch_states = jnp.einsum(
        "clhp,cln->chpn", tail_rows, write_state, preferred_element_type=jnp.float32
    )
    stretch_gates = (
        jnp.exp(decay_heads[:, :, -1]) * (last_ids == prior_ids).astype(jnp.float32)[:, None]
    )
    block_gate = jnp.ones((local_heads,), jnp.float32)
    block_state = jnp.zeros((local_heads, head_width, state_width), jnp.float32)
    block_state = stretch_gates[0][:, None, None] * block_state + stretch_states[0]
    block_gate = block_gate * stretch_gates[0]

    def compose(earlier, later):
        return (earlier[0] * later[0], later[0][:, None, None] * earlier[1] + later[1])

    identity_pair = (jnp.ones_like(block_gate), jnp.zeros_like(block_state))
    carried = prefix((block_gate, block_state), "seq", compose, identity_pair)
    incoming = carried[1]
    arriving = []
    arriving.append(incoming)
    arriving = jnp.stack(arriving)
    carry_mask = (stretch_ids == prior_ids[:, None]).astype(jnp.float32)
    carry_decay = jnp.exp(log_decay) * carry_mask[:, :, None]
    from_before = (
        jnp.einsum(
            "cln,chpn->clhp",
            read_state,
            arriving.astype(jnp.bfloat16),
            preferred_element_type=jnp.float32,
        )
        * carry_decay[:, :, :, None]
    )
    result = (
        within_stretch + from_before + skip_gain[None, None, :, None] * values.astype(jnp.float32)
    )
    ssm_rows = result.reshape(block_rows, local_width).astype(jnp.bfloat16)
    end_weight = ends_mask.astype(jnp.float32)
    has_end = jnp.sum(end_weight, axis=1)
    end_decay = jnp.sum(decay_heads * end_weight[:, None, :], axis=2)
    end_ids = jnp.sum(jnp.where(ends_mask, stretch_ids, 0), axis=1)
    keep_end = ((stretch_ids == end_ids[:, None]) & (has_end[:, None] > 0))[:, None, :]
    end_coef = (
        jnp.where(keep_end, jnp.exp(jnp.minimum(end_decay[:, :, None] - decay_heads, 0.0)), 0.0)
        * step_heads
    )
    end_rows = (values.astype(jnp.float32) * jnp.swapaxes(end_coef, 1, 2)[:, :, :, None]).astype(
        jnp.bfloat16
    )
    end_states = jnp.einsum(
        "clhp,cln->chpn", end_rows, write_state, preferred_element_type=jnp.float32
    )
    end_carry = (
        jnp.exp(end_decay) * ((end_ids == prior_ids) & (has_end > 0)).astype(jnp.float32)[:, None]
    )
    end_states = end_states + end_carry[:, :, None, None] * arriving
    final_block = jnp.sum(end_states, axis=0)[None]
    head_gates = gates_sum.astype(jnp.bfloat16)
    norm_slice = lax.dynamic_slice_in_dim(norm_gain, group_index * local_width, local_width)
    gated = ssm_rows.astype(jnp.float32) * jax.nn.silu(head_gates.astype(jnp.float32))
    squares = lax.psum(jnp.sum(gated * gated, axis=1), "head")
    scaled = gated * lax.rsqrt(squares / inner_width + epsilon)[:, None] * norm_slice[None, :]
    outgoing = scaled.astype(jnp.bfloat16)
    returned = lax.all_to_all(
        outgoing.reshape(groups, sub_rows, local_width),
        "head",
        split_axis=0,
        concat_axis=2,
        tiled=True,
    )
    gated_out = returned.reshape(sub_rows, inner_width)
    return (gated_out, final_block)


def solution(mesh):
    in_specs = (
        P(("seq", "head"), None),
        P("seq", "head"),
        P("seq", "head"),
        P("seq", "head"),
        P("seq", None),
        P(),
        P(),
        P("head"),
        P("head"),
        P("head"),
        P(),
        P(),
    )
    out_specs = (P(("seq", "head"), None), P("seq", "head", None, None))
    return jax.shard_map(
        on_device, mesh=mesh, in_specs=in_specs, out_specs=out_specs, check_vma=False
    )
```
